32 devices in a mesh: dp: 8 (over z, y), cand: 4 (over x, core).
Axes of the slice: x: 2, y: 2, z: 4, core: 2. Of those that a mesh axis runs over, the one named last changes fastest.
Arguments:
- tokens: bfloat16 [32768, 768], P(('dp', 'cand')), may hold values from -6 to 6
- score_vec: float32 [768], replicated, may hold values from -0.4375 to 0.4375
- pair_lengths: int32 [64, 4], P(('dp', 'cand')), may hold values from 1 to 320, 512 in all within a row
- query_ids: int32 [256], P(('dp', 'cand')), may hold values from 0 to 1
- labels: int32 [256], P(('dp', 'cand')), may hold values from 0 to 3
- attention_weight: float32 [4, 768, 768], P(None, ('dp', 'cand')), may hold values from -1.299038 to 1.299038
- expand_weight: float32 [768, 3072], P(('dp', 'cand')), may hold values from -0.649519 to 0.649519
- shrink_weight: float32 [3072, 768], P(('dp', 'cand')), may hold values from -0.23454855 to 0.23454855
- vector_weight: float32 [12, 768], P(None, ('dp', 'cand')), may hold values from -1.8 to 1.8
- attention_first: float32 [4, 768, 768], P(None, ('dp', 'cand')), may hold values from -0.75 to 0.75
- expand_first: float32 [768, 3072], P(('dp', 'cand')), may hold values from -0.75 to 0.75
- shrink_first: float32 [3072, 768], P(('dp', 'cand')), may hold values from -1.25 to 1.25
- vector_first: float32 [12, 768], P(None, ('dp', 'cand')), may hold values from -2.0922725 to 2.0922725
- attention_second: float32 [4, 768, 768], P(None, ('dp', 'cand')), may hold values from 6.510417e-05 to 0.00109375
- expand_second: float32 [768, 3072], P(('dp', 'cand')), may hold values from 6.510417e-05 to 0.00109375
- shrink_second: float32 [3072, 768], P(('dp', 'cand')), may hold values from 0.0002109375 to 0.003515625
- vector_second: float32 [12, 768], P(None, ('dp', 'cand')), may hold values from 7.291667e-06 to 0.050260417
Outputs:
- grad_tokens: float32 [32768, 768], P(('dp', 'cand'))
- scores: float32 [256], P(('dp', 'cand'))
- score_grads: float32 [256], P(('dp', 'cand'))
- trust_ratios: float32 [7], replicated
- group_norms: float32 [2, 7], replicated
- attention_new: float32 [4, 768, 768], P(None, ('dp', 'cand'))
- expand_new: float32 [768, 3072], P(('dp', 'cand'))
- shrink_new: float32 [3072, 768], P(('dp', 'cand'))
- vector_new: float32 [12, 768], P(None, ('dp', 'cand'))
- attention_moment: float32 [4, 768, 768], P(None, ('dp', 'cand'))
- expand_moment: float32 [768, 3072], P(('dp', 'cand'))
- shrink_moment: float32 [3072, 768], P(('dp', 'cand'))
- vector_moment: float32 [12, 768], P(None, ('dp', 'cand'))
- attention_square: float32 [4, 768, 768], P(None, ('dp', 'cand'))
- expand_square: float32 [768, 3072], P(('dp', 'cand'))
- shrink_square: float32 [3072, 768], P(('dp', 'cand'))
- vector_square: float32 [12, 768], P(None, ('dp', 'cand'))
The draws below stay inside these ranges and needn't reach their ends.
Inputs may be any that keep to these rules, and one draw needn't show every extreme that they name: `pair_lengths`: each pack's 4 pairs fill its 512 rows; in each pack the longest pair has exactly 320 rows.
All inputs are finite; a program needn't handle non-finite values.
Results may differ from the reference program's by a relative error of at most 0.012.
The reference program's roundings to bfloat16 on the way count: a program that leaves them out, or rounds other values in their place, can miss the bound.
Values may be sent and summed in bfloat16 or wider, within the bound.
No kernel may reach another device: no remote copies, remote signals or barrier semaphores. Data moves between devices by JAX's collectives and lax.ppermute only.
A program may use at most 192 MiB of HBM per device.

```python
import math
import jax
import jax.numpy as jnp
import numpy as np
from jax import lax

D = 768
HEADS = 12
HEAD_DIM = 64
FF = 3072
PACK = 512
PAIRS_PACK = 4
STEP = 10
QUERIES_DEV = 2
MOST_LEN = 320
PAIRS_DEV = 8
PACKS = 64
TOKENS = 32768
PAIRS = 256
N_CAND = 4


def ramped_normal(key, shape, ramp_dim, ramp_len, base):
    noise = jnp.clip(jax.random.normal(key, shape, jnp.float32), -6.0, 6.0)
    ramp = 1.0 + 2.0 * jnp.arange(ramp_len, dtype=jnp.float32) / (ramp_len - 1)
    view = [1] * len(shape)
    view[ramp_dim] = ramp_len
    return noise * ramp.reshape(view) * base


def vector_levels():
    table = jnp.array([0.05, 0.15, 0.05, 1.0, 0.05, 0.05, 1.0, 0.05, 0.05, 0.05, 0.05, 0.05], jnp.float32)
    ratio = PAIRS * PAIRS_PACK / (PACK * D)
    return table * (62.0 * ratio ** 0.5)


def draw_attention_weight(key, part):
    key = jax.random.fold_in(key, 11)
    scales = jnp.array([0.6, 0.6, 1.0, 2.0], jnp.float32) * D ** (-0.5)
    return ramped_normal(key, (4, D, D), 1, D, 1.0) * scales[:, None, None]


def draw_expand_weight(key, part):
    key = jax.random.fold_in(key, 12)
    return ramped_normal(key, (D, FF), 0, D, D ** (-0.5))


def draw_shrink_weight(key, part):
    key = jax.random.fold_in(key, 13)
    return ramped_normal(key, (FF, D), 0, FF, 0.7 * FF ** (-0.5))


def draw_vector_weight(key, part):
    key = jax.random.fold_in(key, 14)
    noise = jnp.clip(jax.random.normal(key, (12, D), jnp.float32), -6.0, 6.0)
    places = jnp.arange(12)
    gain_rows = (places == 3) | (places == 6)
    return jnp.where(gain_rows[:, None], 1.0 + 0.3 * jnp.tanh(noise), 0.3 * noise)


def draw_vector_first(key, part):
    key = jax.random.fold_in(key, 15)
    noise = jnp.clip(jax.random.normal(key, (12, D), jnp.float32), -6.0, 6.0)
    return noise * (0.11 * vector_levels())[:, None]


def draw_vector_second(key, part):
    key = jax.random.fold_in(key, 16)
    spread = jax.random.uniform(key, (12, D), jnp.float32, math.log(0.3), math.log(5.0))
    levels = vector_levels()
    return jnp.exp(spread) * (0.001 * levels * levels)[:, None]


def place_ends(entries, own_key, low, high):
    longest = entries.shape.index(max(entries.shape))
    spots = []
    for shift in (0, 1):
        where = [jax.random.randint(jax.random.fold_in(own_key, axis), (), 0, length) for axis, length in enumerate(entries.shape)]
        where[longest] = (where[longest] + shift) % entries.shape[longest]
        spots.append(tuple(where))
    return entries.at[spots[0]].set(low).at[spots[1]].set(high)


def level_of(own_key, dims, cuts, smallest, high):
    level = 1.0
    for position, parts in cuts:
        steps = jax.random.uniform(jax.random.fold_in(jax.random.fold_in(own_key, 6), position), (parts,), jnp.float32, smallest / len(cuts), high / len(cuts))
        level = level * jnp.repeat(jnp.exp(steps), dims[position] // parts).reshape((-1,) + (1,) * (len(dims) - 1 - position))
    return level


def length_profile(count, total, limit, slope):
    weights = [(1 << 20) // math.isqrt(standing ** slope) + 1 for standing in range(2, count + 1)]
    surplus, holding = total - limit - (count - 1), [1] * (count - 1)
    while surplus > 0:
        free = [i for i in range(count - 1) if holding[i] < limit]
        mass, budget = sum([weights[i] for i in free]), surplus
        for i in free:
            extra = min(limit - holding[i], max(1, budget * weights[i] // mass), surplus)
            holding[i] = holding[i] + extra
            surplus = surplus - extra
    return np.array([limit] + holding)


def uneven(stream_key, count, total, most, skew):
    if count == 2:
        one = jax.random.randint(stream_key, (), max(1, total - most), min(most, total - 1) + 1)
        return jnp.stack([one, total - one])
    lengths = jnp.asarray(length_profile(count, total, most, skew), jnp.int32)
    twos = (count - 1) // 2
    donor, receiver = lengths[1:1 + 2 * twos:2], lengths[2:2 + 2 * twos:2]
    room = jnp.minimum(donor - 1, most - receiver)
    passed = jax.random.randint(jax.random.fold_in(stream_key, 1), (twos,), 0, 1 << 20) % (room + 1)
    lengths = lengths.at[1:1 + 2 * twos:2].set(donor - passed).at[2:2 + 2 * twos:2].set(receiver + passed)
    return lengths[jax.random.permutation(jax.random.fold_in(stream_key, 2), count)]


def centred(key, shape, scale, most, pieces=(), kind=jnp.bfloat16):
    values = scale * jax.random.normal(key, shape, jnp.float32)
    if pieces:
        values = values * level_of(key, shape, pieces, -0.22, 0.18)
    return jnp.clip(values, -most, most).astype(kind)


def setup_inputs(seed: int = 0) -> dict:
    keys = jax.random.split(jax.random.key(seed), 18)
    tokens = centred(keys[0], (TOKENS, D), 1.0, 6.0, ((0, 32),))
    score_vec = centred(keys[1], (D,), (D // 4) ** -0.5, 0.4375, (), jnp.float32)
    pair_lengths = jax.vmap(lambda own: uneven(own, PAIRS_PACK, PACK, MOST_LEN, 2))(jax.random.split(keys[2], PACKS)).reshape((PACKS, PAIRS_PACK)).astype(jnp.int32)
    query_ids = place_ends(jax.random.randint(keys[3], (PAIRS,), 0, QUERIES_DEV), jax.random.fold_in(keys[3], 1), 0, QUERIES_DEV - 1).astype(jnp.int32)
    labels = place_ends(jax.random.randint(keys[4], (PAIRS,), 0, 4), jax.random.fold_in(keys[4], 1), 0, 3).astype(jnp.int32)
    attention_weight = draw_attention_weight(jax.random.fold_in(keys[17], 71), 0)
    expand_weight = draw_expand_weight(jax.random.fold_in(keys[17], 71), 0)
    shrink_weight = draw_shrink_weight(jax.random.fold_in(keys[17], 71), 0)
    vector_weight = draw_vector_weight(jax.random.fold_in(keys[17], 71), 0)
    attention_first = centred(keys[9], (4, D, D), (1.0 * (PAIRS * PAIRS_PACK * (PACK * D) ** -1) ** 0.5), 0.75, ((1, 32),), jnp.float32)
    expand_first = centred(keys[10], (D, FF), (1.0 * (PAIRS * PAIRS_PACK * (PACK * D) ** -1) ** 0.5), 0.75, ((0, 32),), jnp.float32)
    shrink_first = centred(keys[11], (FF, D), (1.8 * (PAIRS * PAIRS_PACK * (PACK * D) ** -1) ** 0.5), 1.25, ((0, 32),), jnp.float32)
    vector_first = draw_vector_first(jax.random.fold_in(keys[17], 71), 0)
    attention_second = jnp.clip(jnp.exp(math.log(0.00109375) - 2.821379 * jax.random.uniform(keys[13], (4, D, D), jnp.float32) ** level_of(keys[13], (4, D, D), ((1, 32),), -0.2, 0.2)), 6.510417006211355e-05, 0.00109375)
    expand_second = jnp.clip(jnp.exp(math.log(0.00109375) - 2.821379 * jax.random.uniform(keys[14], (D, FF), jnp.float32) ** level_of(keys[14], (D, FF), ((0, 32),), -0.2, 0.2)), 6.510417006211355e-05, 0.00109375)
    shrink_second = jnp.clip(jnp.exp(math.log(0.003515625) - 2.8134107 * jax.random.uniform(keys[15], (FF, D), jnp.float32) ** level_of(keys[15], (FF, D), ((0, 32),), -0.2, 0.2)), 0.0002109375, 0.003515625)
    vector_second = draw_vector_second(jax.random.fold_in(keys[17], 71), 0)
    return dict(tokens=tokens, score_vec=score_vec, pair_lengths=pair_lengths, query_ids=query_ids, labels=labels, attention_weight=attention_weight, expand_weight=expand_weight, shrink_weight=shrink_weight, vector_weight=vector_weight, attention_first=attention_first, expand_first=expand_first, shrink_first=shrink_first, vector_first=vector_first, attention_second=attention_second, expand_second=expand_second, shrink_second=shrink_second, vector_second=vector_second)


norm_eps = 1e-05
beta_first = 0.9
beta_second = 0.999
learn_rate = 1.0
weight_decay = 0.01
step_eps = 1e-06
masked_fill = -1e+30

@jax.custom_vjp
def low(v):
    return lax.optimization_barrier(v.astype(jnp.bfloat16)).astype(jnp.float32)

@jax.custom_vjp
def low_back(v):
    return v

def low_keep(v):
    return (low(v), None)

def low_pass(kept, grad):
    return (grad,)

def back_keep(v):
    return (v, None)

def back_low(kept, grad):
    return (low(grad),)
low.defvjp(low_keep, low_pass)
low_back.defvjp(back_keep, back_low)

def product(left, right):
    return jnp.dot(left, right, precision=lax.Precision.HIGHEST, preferred_element_type=jnp.float32)

def layer_norm(hidden, gain, shift):
    center = hidden - lax.optimization_barrier(jnp.mean(hidden, axis=-1, keepdims=True))
    spread = lax.optimization_barrier(jnp.mean(center * center, axis=-1, keepdims=True))
    return center * lax.rsqrt(spread + norm_eps) * gain + shift

def pack_layout(pair_lengths):
    ends = jnp.cumsum(pair_lengths, axis=-1, dtype=jnp.int32)
    places = jnp.arange(PACK, dtype=jnp.int32)
    segment = lax.optimization_barrier(jnp.sum((places[None, :, None] >= ends[:, None, :]).astype(jnp.int32), axis=-1, dtype=jnp.int32))
    return segment

def attend(bundle):
    query, key_rows, value, segment = bundle
    query_heads = query.reshape(PACK, HEADS, HEAD_DIM)
    key_heads = key_rows.reshape(PACK, HEADS, HEAD_DIM)
    value_heads = value.reshape(PACK, HEADS, HEAD_DIM)
    logits = jnp.einsum('qhd,khd->hqk', query_heads, key_heads, precision=lax.Precision.HIGHEST) * HEAD_DIM ** (-0.5)
    logits = low_back(logits)
    same_pair = segment[:, None] == segment[None, :]
    logits = jnp.where(same_pair[None], logits, masked_fill)
    row_peak = lax.optimization_barrier(jnp.max(logits, axis=-1, keepdims=True))
    expos = jnp.exp(logits - row_peak)
    probs = low(expos / lax.optimization_barrier(jnp.sum(expos, axis=-1, keepdims=True)))
    context = jnp.einsum('hqk,khd->qhd', probs, value_heads, precision=lax.Precision.HIGHEST)
    return context.reshape(PACK, D)

def forward(attention_weight, expand_weight, shrink_weight, vector_weight, tokens_f, score_vec, segment, member, lengths_f):
    matrices = low(attention_weight)
    expand = low(expand_weight)
    shrink = low(shrink_weight)
    vector = low(vector_weight)
    query = low(low_back(product(tokens_f, matrices[0]) + vector[0]))
    key_rows = low(low_back(product(tokens_f, matrices[1])))
    value = low(low_back(product(tokens_f, matrices[2]) + vector[1]))
    context = lax.map(jax.checkpoint(attend), (query.reshape(PACKS, PACK, D), key_rows.reshape(PACKS, PACK, D), value.reshape(PACKS, PACK, D), segment))
    context = low(low_back(context.reshape(TOKENS, D)))
    attended = low_back(product(context, matrices[3]) + vector[2])
    first_out = layer_norm(tokens_f + attended, vector[3], vector[4])
    inner = low_back(product(low(first_out), expand) + vector[8:12].reshape(FF))
    active = low(jax.nn.gelu(inner, approximate=False))
    outer = low_back(product(active, shrink) + vector[5])
    final = layer_norm(first_out + outer, vector[6], vector[7])
    row_score = lax.optimization_barrier(jnp.sum(final * score_vec, axis=1)).reshape(PACKS, PACK, 1)
    pooled = lax.optimization_barrier(jnp.sum(row_score * member, axis=1)) / lengths_f
    return pooled.reshape(PAIRS)

def listwise(scores, groups, labels_f):
    same_group = groups[:, None] == groups[None, :]
    peak = lax.optimization_barrier(jnp.max(jnp.where(same_group, scores[None, :], masked_fill), axis=1))
    total = lax.optimization_barrier(jnp.sum(jnp.exp(jnp.where(same_group, scores[None, :] - peak[:, None], masked_fill)), axis=1))
    return jnp.sum(labels_f * (peak + jnp.log(total) - scores))

def adam_step(weight, grad, first, second, decay):
    first_new = beta_first * first + (1.0 - beta_first) * grad
    second_new = beta_second * second + (1.0 - beta_second) * grad * grad
    update = first_new / (1.0 - beta_first ** STEP) / (jnp.sqrt(second_new / (1.0 - beta_second ** STEP)) + step_eps) + decay * weight
    return (first_new, second_new, update)

def group_squares(attention, expand, shrink, vector):
    return jnp.concatenate([lax.optimization_barrier(jnp.sum(attention * attention, axis=(1, 2))), jnp.sum(expand * expand)[None], jnp.sum(shrink * shrink)[None], jnp.sum(vector * vector)[None]])

def reference(tokens, score_vec, pair_lengths, query_ids, labels, attention_weight, expand_weight, shrink_weight, vector_weight, attention_first, expand_first, shrink_first, vector_first, attention_second, expand_second, shrink_second, vector_second):
    segment = pack_layout(pair_lengths)
    member = (segment[:, :, None] == jnp.arange(PAIRS_PACK, dtype=jnp.int32)[None, None, :]).astype(jnp.float32)
    lengths_f = pair_lengths.astype(jnp.float32)
    groups = jnp.arange(PAIRS, dtype=jnp.int32) // (PAIRS_DEV * N_CAND) * QUERIES_DEV + query_ids
    tokens_f = tokens.astype(jnp.float32)

    def scored(attention, expand, shrink, vector, rows):
        return forward(attention, expand, shrink, vector, rows, score_vec, segment, member, lengths_f)
    scores, pull_back = jax.vjp(scored, attention_weight, expand_weight, shrink_weight, vector_weight, tokens_f)
    score_grads = jax.grad(listwise)(scores, groups, labels.astype(jnp.float32))
    grad_attention, grad_expand, grad_shrink, grad_vector, grad_tokens = pull_back(score_grads)
    attention_moment, attention_square, attention_step = adam_step(attention_weight, grad_attention, attention_first, attention_second, weight_decay)
    expand_moment, expand_square, expand_step = adam_step(expand_weight, grad_expand, expand_first, expand_second, weight_decay)
    shrink_moment, shrink_square, shrink_step = adam_step(shrink_weight, grad_shrink, shrink_first, shrink_second, weight_decay)
    vector_moment, vector_square, vector_step = adam_step(vector_weight, grad_vector, vector_first, vector_second, 0.0)
    master_sq = group_squares(attention_weight, expand_weight, shrink_weight, vector_weight)
    step_sq = group_squares(attention_step, expand_step, shrink_step, vector_step)
    trust_ratios = jnp.sqrt(master_sq) * lax.rsqrt(step_sq + 1e-12)
    group_norms = jnp.stack([jnp.sqrt(master_sq), jnp.sqrt(step_sq)])
    attention_new = attention_weight - learn_rate * trust_ratios[0:4][:, None, None] * attention_step
    expand_new = expand_weight - learn_rate * trust_ratios[4] * expand_step
    shrink_new = shrink_weight - learn_rate * trust_ratios[5] * shrink_step
    vector_new = vector_weight - learn_rate * trust_ratios[6] * vector_step
    return (grad_tokens, scores, score_grads, trust_ratios, group_norms, attention_new, expand_new, shrink_new, vector_new, attention_moment, expand_moment, shrink_moment, vector_moment, attention_square, expand_square, shrink_square, vector_square)
```

```python
import functools

import jax
import jax.numpy as jnp
from jax import lax
from jax.experimental import pallas as pl
from jax.experimental.pallas import tpu as pltpu
from jax.sharding import PartitionSpec as P

D = 768
HEADS = 12
HEAD_DIM = 64
FF = 3072
PACK = 512
PAIRS_PACK = 4
STEP = 10
QUERIES_DEV = 2

norm_eps = 1e-05
beta_first = 0.9
beta_second = 0.999
learn_rate = 1.0
weight_decay = 0.01
step_eps = 1e-06
masked_fill = -1e30

BOTH = ("dp", "cand")
LANES = 128
CHIPS = 16
ROWS_A = D // CHIPS
ROWS_B = FF // CHIPS // 2
HALF = D // 2
INNER_A = D + HALF
WIDE_A = INNER_A + LANES
WIDE_B = FF // 2 + HALF
TILE = 256
MIB = 1 << 20
ROOM = {
    "project": 12,
    "attend": 16,
    "expand_rows": 26,
    "shrink_rows": 20,
    "shrink_back": 28,
    "rows_back": 32,
    "expand_grads": 14,
    "attend_back": 16,
    "project_grads": 16,
    "token_grads": 16,
    "pick": 12,
    "add_blocks": 12,
    "step_wide": 12,
    "step_narrow": 12,
    "apply_step": 12,
}
bf16 = jnp.bfloat16
f32 = jnp.float32
B_Q, B_V, B_O, G_1, S_1, B_2, G_2, S_2, B_FF = range(9)
VECTORS = 12
OWN, OTHER, CORE, OWN_CHIP, OTHER_CHIP = 0, CHIPS, 2 * CHIPS, 2 * CHIPS + 1, 3 * CHIPS + 1
TABLE = 4 * CHIPS + 1
ENDS = 2 * TABLE


def mm(a, b):
    return lax.dot_general(a, b, (((1,), (0,)), ((), ())), preferred_element_type=f32)


def mm_nt(a, b):
    return lax.dot_general(a, b, (((1,), (1,)), ((), ())), preferred_element_type=f32)


def mm_tn(a, b):
    return lax.dot_general(a, b, (((0,), (0,)), ((), ())), preferred_element_type=f32)


def row_mean(v):
    return jnp.sum(v, axis=1, keepdims=True) * (1.0 / D)


def norm_parts(hidden):
    center = hidden - row_mean(hidden)
    inverse = lax.rsqrt(row_mean(center * center) + norm_eps)
    return center * inverse, inverse


def segments(table, pack, first_row, rows):
    row = lax.broadcasted_iota(jnp.int32, (rows, LANES), 0) + first_row
    return sum(
        jnp.where(row >= table[ENDS + pack * PAIRS_PACK + i], 1, 0) for i in range(PAIRS_PACK)
    )


def whole(array):
    zeros = (0,) * array.ndim
    return array, pl.BlockSpec(array.shape, lambda *_: zeros, pipeline_mode=pl.Buffered(1))


def rows_of(array, tile=TILE):
    return array, pl.BlockSpec((tile, array.shape[1]), lambda i, *_: (i, 0))


def out_rows(tokens, width, dtype, tile=TILE):
    return jax.ShapeDtypeStruct((tokens, width), dtype), pl.BlockSpec((tile, width), lambda i, *_: (i, 0))


def in_hbm(out):
    shape, spec = out
    return pltpu.HBM(shape.shape, shape.dtype), spec


def from_hbm(operand):
    array, spec = operand
    return pltpu.with_memory_space_constraint(array, pltpu.HBM), spec


def out_whole(shape, dtype):
    zeros = (0,) * len(shape)
    return jax.ShapeDtypeStruct(shape, dtype), pl.BlockSpec(shape, lambda *_: zeros)


def launch(name, body, grid, table, operands, outs, scratch=(), weights=(), after=(), into=()):
    operands = list(operands)
    count = len(operands)
    outs = list(outs)
    idle = pl.BlockSpec(memory_space=pl.ANY)
    arrays = [a for a, _ in operands]
    specs = [spec for _, spec in operands]
    rooms = []
    for weight in weights:
        arrays += [pltpu.with_memory_space_constraint(a, pltpu.HBM) for a in weight.pieces]
        specs += [idle] * len(weight.pieces)
        rooms += [pltpu.VMEM(weight.shape, bf16), pltpu.SemaphoreType.DMA((2, CHIPS))]
    aliases = {1 + len(arrays) + i: i for i in range(len(into))}
    arrays += list(into) + list(after)
    specs += [idle] * (len(into) + len(after))

    def kernel(table_ref, *refs):
        ins = refs[:count]
        rest = refs[len(arrays) :]
        held = rest[len(outs) + len(scratch) :]
        if weights:

            @pl.when(pl.program_id(0) == 0)
            def _():
                copies, at = [], count
                for i, weight in enumerate(weights):
                    pieces = refs[at : at + len(weight.pieces)]
                    at += len(pieces)
                    copies += weight.copies(table_ref, pieces, held[2 * i], held[2 * i + 1])
                for copy in copies:
                    copy.start()
                for copy in copies:
                    copy.wait()

        body(table_ref, *ins, *held[::2], *rest[: len(outs) + len(scratch)])

    results = pl.pallas_call(
        kernel,
        out_shape=[shape for shape, _ in outs],
        grid_spec=pltpu.PrefetchScalarGridSpec(
            num_scalar_prefetch=1,
            grid=grid,
            in_specs=specs,
            out_specs=[spec for _, spec in outs],
            scratch_shapes=list(scratch) + rooms,
        ),
        input_output_aliases=aliases,
        compiler_params=pltpu.CompilerParams(vmem_limit_bytes=ROOM[name] * MIB),
        name=name,
    )(table, *arrays)
    return results


def pick(table, parts, rows, low, high, after=()):
    width = parts[0][0].shape[1]
    moves, used, at = [], [], 0
    for array, count in parts:
        start, stop = max(low, at), min(high, at + count)
        if start < stop:
            moves.append(((start - at) * rows, (start - low) * rows, (stop - start) * rows))
            used.append(array)
        at += count

    def body(table, *refs):
        for ref, (source, target, size) in zip(refs[:-1], moves):
            refs[-1][target : target + size, :] = ref[source : source + size, :]

    return launch(
        "pick", body, (1,), table, [whole(a) for a in used],
        [out_whole(((high - low) * rows, width), bf16)], after=after,
    )[0]


def add_blocks(table, terms, low, high, after=()):
    operands = []
    for term in terms:
        array, first = next(
            (a, at) for a, at in term if at <= low and high <= at + a.shape[0]
        )
        _, rows, width = array.shape
        spec = pl.BlockSpec((1, rows, width), lambda i, *_, skip=low - first: (i + skip, 0, 0))
        operands.append((array, spec))

    def body(table, *refs):
        refs[-1][...] = sum(ref[...].astype(f32) for ref in refs[:-1]).astype(bf16)

    return launch(
        "add_blocks", body, (high - low,), table, operands,
        [
            (
                jax.ShapeDtypeStruct((high - low, rows, width), bf16),
                pl.BlockSpec((1, rows, width), lambda i, *_: (i, 0, 0)),
            )
        ],
        after=after,
    )[0]


class Blocks:
    def __init__(self, own, others, rows, base):
        self.counts = [count for _, count in own]
        self.pieces = [a for a, _ in own] + list(others)
        self.rows = rows
        self.base = base
        width = self.pieces[0].shape[1]
        self.shape = (2 * CHIPS * rows, width) if rows == ROWS_B else (2, CHIPS * rows, width)

    def copies(self, table, refs, whole_ref, sems):
        core = table[CORE]
        out = []
        places = [(piece, at) for piece, count in enumerate(self.counts) for at in range(count)]
        for position, (piece, at) in enumerate(places):
            for which in range(2):
                chip = table[self.base + (OWN_CHIP, OTHER_CHIP)[which] + position]
                half = core if which == 0 else 1 - core
                if self.rows == ROWS_B:
                    at_row = pl.multiple_of((2 * chip + half) * self.rows, self.rows)
                    there = whole_ref.at[pl.ds(at_row, self.rows)]
                else:
                    at_row = pl.multiple_of(chip * self.rows, self.rows)
                    there = whole_ref.at[half, pl.ds(at_row, self.rows)]
                here = refs[which * len(self.counts) + piece].at[pl.ds(at * self.rows, self.rows)]
                out.append(pltpu.make_async_copy(here, there, sems.at[which, position]))
        return out


def project(table, x, w_a, after=()):
    tokens = x.shape[0]

    def body(table, x_ref, w_ref, q_ref, k_ref, v_ref, vec_ref):
        @pl.when(pl.program_id(0) == 0)
        def _():
            for half in range(2):
                turned = jnp.transpose(w_ref[half, :, INNER_A:].astype(f32))
                vec_ref[6 * half : 6 * half + 6, :] = turned[:6]

        x = x_ref[...]
        low = mm(x, w_ref[0, :, :INNER_A])
        q_ref[...] = (low[:, :D] + vec_ref[B_Q : B_Q + 1, :]).astype(bf16)
        k_ref[:, :HALF] = low[:, D:].astype(bf16)
        high = mm(x, w_ref[1, :, :INNER_A])
        k_ref[:, HALF:] = high[:, :HALF].astype(bf16)
        v_ref[...] = (high[:, HALF:] + vec_ref[B_V : B_V + 1, :]).astype(bf16)

    return launch(
        "project", body, (tokens // TILE,), table,
        [rows_of(x)], [out_rows(tokens, D, bf16)] * 3 + [out_whole((16, D), f32)],
        weights=[w_a], after=after,
    )


def attend(table, pack, q, k, v, into=(), after=()):
    tokens, width = q.shape
    pair_block = pl.BlockSpec((PACK, LANES), lambda h, *_: (pack, h))

    def body(table, q_ref, k_ref, v_ref, ctx_ref, e_ref, inv_ref, end_ref):
        end_ref[...] = jnp.zeros((8, LANES), f32)
        lane = lax.broadcasted_iota(jnp.int32, (PACK, LANES), 1)
        segment = segments(table, pack, 0, PACK)
        apart = jnp.where((lane < PAIRS_PACK) & (lane != segment), masked_fill, 0.0).astype(bf16)
        belongs = jnp.where(lane == segment, 1.0, 0.0).astype(bf16)
        keys = jnp.concatenate([k_ref[...], belongs], axis=1)
        values = jnp.concatenate([v_ref[...], jnp.ones((PACK, LANES), bf16)], axis=1)
        queries = q_ref[...].astype(f32) * HEAD_DIM ** (-0.5)
        first = lane < HEAD_DIM
        outs = []
        for head in range(2):
            mine = jnp.where(first if head == 0 else ~first, queries, 0.0).astype(bf16)
            logits = mm_nt(jnp.concatenate([mine, apart], axis=1), keys)
            peak = jnp.max(logits, axis=1, keepdims=True)
            expos = jnp.exp(logits - peak).astype(bf16)
            e_ref[head] = expos
            outs.append(mm(expos, values))
        total = jnp.where(first, outs[0][:, LANES:], outs[1][:, LANES:])
        inverse = 1.0 / total
        inv_ref[...] = inverse
        ctx_ref[...] = (jnp.where(first, outs[0][:, :LANES], outs[1][:, :LANES]) * inverse).astype(bf16)

    heads = width // HEAD_DIM
    return launch(
        "attend", body, (heads // 2,), table,
        [(a, pair_block) for a in (q, k, v)],
        [
            (jax.ShapeDtypeStruct((tokens, width), bf16), pair_block),
            in_hbm(
                (
                    jax.ShapeDtypeStruct((heads, tokens, PACK), bf16),
                    pl.BlockSpec((2, PACK, PACK), lambda h, *_: (h, pack, 0)),
                )
            ),
            (jax.ShapeDtypeStruct((tokens, width), f32), pair_block),
            out_whole((8, LANES), f32),
        ],
        into=into, after=after,
    )


def gelu_parts(v):
    phi = 0.5 + 0.5 * lax.erf(v * 0.7071067811865476)
    return v * phi, phi + v * (jnp.exp(v * v * -0.5) * 0.3989422804014327)


def expand_rows(table, x, ctx, w_b, vec, after=()):
    tokens = x.shape[0]
    step = HALF

    def body(table, x_ref, ctx_ref, vec_ref, w_ref, n1_ref, r1_ref, fb_ref, act_ref, slope_ref):
        ctx = ctx_ref[...]
        attended = jnp.concatenate([mm(ctx, w_ref[half, :, FF // 2 :]) for half in range(2)], axis=1)
        hidden = x_ref[...].astype(f32) + attended + vec_ref[B_O : B_O + 1, :]
        normed, inverse = norm_parts(hidden)
        n1_ref[...] = normed
        r1_ref[...] = jnp.broadcast_to(inverse, (TILE, LANES))
        first_b = (normed * vec_ref[G_1 : G_1 + 1, :] + vec_ref[S_1 : S_1 + 1, :]).astype(bf16)
        fb_ref[...] = first_b
        for j in range(FF // step):
            half, at = divmod(j * step, FF // 2)
            row, column = divmod(j * step, D)
            bias = vec_ref[B_FF + row : B_FF + row + 1, column : column + step]
            active, slope = gelu_parts(mm(first_b, w_ref[half, :, at : at + step]) + bias)
            act_ref[:, j * step : (j + 1) * step] = active.astype(bf16)
            slope_ref[:, j * step : (j + 1) * step] = slope.astype(bf16)

    return launch(
        "expand_rows", body, (tokens // TILE,), table,
        [rows_of(x), rows_of(ctx), whole(vec)],
        [
            in_hbm(out_rows(tokens, D, f32)),
            in_hbm(out_rows(tokens, LANES, f32)),
            in_hbm(out_rows(tokens, D, bf16)),
            in_hbm(out_rows(tokens, FF, bf16)),
            in_hbm(out_rows(tokens, FF, bf16)),
        ],
        weights=[w_b], after=after,
    )


def shrink_rows(table, active, w_2, n1, vec, score_vec, facts, after=()):
    tokens = active.shape[0]

    def body(table, act_ref, n1_ref, vec_ref, sv_ref, facts_ref, w_ref, n2_ref, r2_ref, stats_ref):
        step = pl.program_id(0)
        outer = mm(act_ref[...], w_ref[...])
        first_out = n1_ref[...] * vec_ref[G_1 : G_1 + 1, :] + vec_ref[S_1 : S_1 + 1, :]
        normed, inverse = norm_parts(first_out + outer + vec_ref[B_2 : B_2 + 1, :])
        n2_ref[...] = normed
        r2_ref[...] = jnp.broadcast_to(inverse, (TILE, LANES))
        score_vec = sv_ref[...]
        final = normed * vec_ref[G_2 : G_2 + 1, :] + vec_ref[S_2 : S_2 + 1, :]
        row_score = jnp.sum(final * score_vec, axis=1, keepdims=True)
        lane = lax.broadcasted_iota(jnp.int32, (TILE, LANES), 1)
        pack = step // (PACK // TILE)
        segment = segments(table, pack, step % (PACK // TILE) * TILE, TILE)
        here = lane == segment + pack * PAIRS_PACK
        shares = jnp.sum(jnp.where(here, row_score, 0.0), axis=0, keepdims=True)

        @pl.when(step == 0)
        def _():
            stats_ref[...] = facts_ref[...]

        stats_ref[0:1, :] += shares

        @pl.when(step == pl.num_programs(0) - 1)
        def _():
            stats_ref[0:1, :] = stats_ref[0:1, :] / facts_ref[3:4, :]

    return launch(
        "shrink_rows", body, (tokens // TILE,), table,
        [rows_of(active), from_hbm(rows_of(n1)), whole(vec), whole(score_vec), whole(facts)],
        [out_rows(tokens, D, f32), out_rows(tokens, LANES, f32), out_whole((8, LANES), f32)],
        weights=[w_2], after=after,
    )


def loss_parts(blocks):
    own = blocks[0]
    own_ids = own[1:2]
    grads = -own[2:3]
    for query in range(QUERIES_DEV):
        inside = [b[1:2] == float(query) for b in blocks]
        peak = functools.reduce(
            jnp.maximum,
            [jnp.where(i, b[0:1], masked_fill) for i, b in zip(inside, blocks)],
        )
        peak = jnp.max(peak, axis=1, keepdims=True)
        total = sum(jnp.where(i, jnp.exp(jnp.where(i, b[0:1] - peak, 0.0)), 0.0) for i, b in zip(inside, blocks))
        total = jnp.sum(total, axis=1, keepdims=True)
        labels = sum(jnp.where(i, b[2:3], 0.0) for i, b in zip(inside, blocks))
        labels = jnp.sum(labels, axis=1, keepdims=True)
        share = jnp.exp(jnp.where(inside[0], own[0:1] - peak, 0.0)) / total * labels
        grads = grads + jnp.where(own_ids == float(query), share, 0.0)
    return jnp.where(own_ids >= 0.0, grads, 0.0)


def shrink_back(table, blocks, n2, r2, vec, score_vec, active, after=()):
    tokens = n2.shape[0]
    count = len(blocks)

    def body(table, *refs):
        block_refs = refs[:count]
        n2_ref, r2_ref, vec_ref, sv_ref, act_ref = refs[count : count + 5]
        outer_ref, dh_ref, keep_ref, send_ref, sums_ref, grads_ref = refs[count + 5 :]
        step = pl.program_id(0)
        core = table[CORE]

        @pl.when(step == 0)
        def _():
            parts = [b[...] for b in block_refs]
            grads = loss_parts(parts)
            grads_ref[...] = jnp.broadcast_to(grads, (8, LANES))
            per_row = grads / parts[0][3:4]
            score_vec = sv_ref[...]
            weighted = score_vec * vec_ref[G_2 : G_2 + 1, :]
            middle = jnp.mean(weighted, axis=1, keepdims=True)
            lane = lax.broadcasted_iota(jnp.int32, (TILE, LANES), 1)
            bias = jnp.zeros((1, D), f32)
            gain = jnp.zeros((1, D), f32)
            shift = jnp.zeros((1, 1), f32)
            for i in range(tokens // TILE):
                here = pl.ds(i * TILE, TILE)
                pack, first_row = divmod(i * TILE, PACK)
                pair = segments(table, pack, first_row, TILE) + pack * PAIRS_PACK
                scale = jnp.sum(jnp.where(lane == pair, per_row, 0.0), axis=1, keepdims=True)
                normed = n2_ref[here, :]
                along = row_mean(normed * weighted)
                back = (scale * r2_ref[here, :1]) * (weighted - middle - normed * along)
                dh_ref[here, :] = back
                rounded = back.astype(bf16)
                outer_ref[here, :] = rounded
                bias = bias + jnp.sum(rounded.astype(f32), axis=0, keepdims=True)
                gain = gain + jnp.sum(normed * scale, axis=0, keepdims=True)
                shift = shift + jnp.sum(scale, axis=0, keepdims=True)
            sums_ref[...] = jnp.concatenate(
                [bias, gain * score_vec, shift * score_vec, jnp.zeros((5, D), f32)], axis=0
            )

        grad = mm_tn(act_ref[...], outer_ref[...])
        for pair in range(2):
            chip = 2 * step + pair
            at = pair * 2 * ROWS_B
            low = grad[at : at + ROWS_B].astype(bf16)
            high = grad[at + ROWS_B : at + 2 * ROWS_B].astype(bf16)
            keep_ref[table[TABLE + OWN + chip]] = jnp.where(core == 0, low, high)
            send_ref[table[TABLE + OTHER + chip]] = jnp.where(core == 0, high, low)

    return launch(
        "shrink_back", body, (CHIPS // 2,), table,
        [whole(b) for b in blocks]
        + [whole(a) for a in (n2, r2, vec, score_vec)]
        + [(active, pl.BlockSpec((tokens, 4 * ROWS_B), lambda i, *_: (0, i)))],
        [
            out_whole((tokens, D), bf16),
            in_hbm(out_whole((tokens, D), f32)),
            out_whole((CHIPS, ROWS_B, D), bf16),
            out_whole((CHIPS, ROWS_B, D), bf16),
            out_whole((8, D), f32),
            out_whole((8, LANES), f32),
        ],
        after=after,
    )


def rows_back(table, outer, dh2, slope, n1, r1, w_2, w_b, vec, after=()):
    tokens = outer.shape[0]

    def body(
        table, outer_ref, dh_ref, slope_ref, n1_ref, r1_ref, vec_ref, w2_ref, wb_ref,
        inner_ref, dh1_ref, attn_ref, dctx_ref, sums_ref, ff_ref,
    ):
        @pl.when(pl.program_id(0) == 0)
        def _():
            sums_ref[...] = jnp.zeros_like(sums_ref)
            ff_ref[...] = jnp.zeros_like(ff_ref)

        outer = outer_ref[...]
        first = dh_ref[...]
        step = D
        for j in range(FF // step):
            half, at = divmod(j * step, FF // 2)
            here = slice(j * step, (j + 1) * step)
            active = mm_nt(outer, w2_ref[here, :])
            inner = (active * slope_ref[:, here].astype(f32)).astype(bf16)
            inner_ref[:, here] = inner
            ff_ref[j : j + 1, :] += jnp.sum(inner.astype(f32), axis=0, keepdims=True)
            first = first + mm_nt(inner, wb_ref[half, :, at : at + step])
        normed = n1_ref[...]
        dn = first * vec_ref[G_1 : G_1 + 1, :]
        back = r1_ref[:, :1] * (dn - row_mean(dn) - normed * row_mean(dn * normed))
        dh1_ref[...] = back
        rounded = back.astype(bf16)
        attn_ref[...] = rounded
        sums_ref[0:1, :] += jnp.sum(rounded.astype(f32), axis=0, keepdims=True)
        sums_ref[1:2, :] += jnp.sum(first * normed, axis=0, keepdims=True)
        sums_ref[2:3, :] += jnp.sum(first, axis=0, keepdims=True)
        dctx = mm_nt(rounded[:, :HALF], wb_ref[0, :, FF // 2 :]) + mm_nt(
            rounded[:, HALF:], wb_ref[1, :, FF // 2 :]
        )
        dctx_ref[...] = dctx.astype(bf16)

    return launch(
        "rows_back", body, (tokens // TILE,), table,
        [rows_of(outer), from_hbm(rows_of(dh2)), from_hbm(rows_of(slope)), from_hbm(rows_of(n1)), from_hbm(rows_of(r1)), whole(vec)],
        [
            in_hbm(out_rows(tokens, FF, bf16)),
            in_hbm(out_rows(tokens, D, f32)),
            out_rows(tokens, D, bf16),
            out_rows(tokens, D, bf16),
            out_whole((8, D), f32),
            out_whole((8, D), f32),
        ],
        weights=[w_2, w_b], after=after,
    )


def expand_grads(table, send, first_b, ctx, inner, attn, after=()):
    tokens = first_b.shape[0]
    tiles = WIDE_B // HALF

    def half_of(t):
        return 1 - t[CORE] if send else t[CORE]

    def body(table, fb_ref, ctx_ref, inner_ref, attn_ref, out_ref):
        step = pl.program_id(0)
        offset = OTHER if send else OWN

        def put(grad):
            for chip in range(CHIPS):
                out_ref[table[offset + chip]] = grad[chip * ROWS_A : (chip + 1) * ROWS_A].astype(bf16)

        @pl.when(step < tiles - 1)
        def _():
            put(mm_tn(fb_ref[...], inner_ref[...]))

        @pl.when(step == tiles - 1)
        def _():
            put(mm_tn(ctx_ref[...], attn_ref[...]))

    return launch(
        "expand_grads", body, (tiles,), table,
        [whole(first_b), whole(ctx)]
        + [
            (
                inner,
                pl.BlockSpec(
                    (tokens, HALF),
                    lambda i, t: (0, half_of(t) * (tiles - 1) + jnp.minimum(i, tiles - 2)),
                ),
            ),
            (attn, pl.BlockSpec((tokens, HALF), lambda i, t: (0, half_of(t)))),
        ],
        [
            (
                jax.ShapeDtypeStruct((CHIPS, ROWS_A, WIDE_B), bf16),
                pl.BlockSpec((CHIPS, ROWS_A, HALF), lambda i, t: (0, 0, i)),
            )
        ],
        after=after,
    )[0]


def attend_back(table, pack, q, k, v, expos, inverse, ctx, dctx, into=(), after=()):
    tokens, width = q.shape
    packs = tokens // PACK
    pairs = width // LANES
    block = pl.BlockSpec((PACK, LANES), lambda h, *_: (pack, h))

    def body(table, q_ref, k_ref, v_ref, e_ref, inv_ref, ctx_ref, dctx_ref, out_ref, sums_ref, end_ref):
        end_ref[...] = jnp.zeros((8, LANES), f32)
        lane = lax.broadcasted_iota(jnp.int32, (PACK, LANES), 1)
        first = lane < HEAD_DIM
        scaled = (dctx_ref[...].astype(f32) * inv_ref[...]).astype(bf16)
        scaled_f = scaled.astype(f32)
        product = scaled_f * ctx_ref[...].astype(f32)
        queries = q_ref[...]
        keys = k_ref[...]
        values = jnp.concatenate([v_ref[...], jnp.where(lane < 3, 1.0, 0.0).astype(bf16)], axis=1)
        parts = []
        for head in range(2):
            mine = first if head == 0 else ~first
            delta = -jnp.sum(jnp.where(mine, product, 0.0), axis=1, keepdims=True)
            delta_1 = delta.astype(bf16).astype(f32)
            delta_2 = (delta - delta_1).astype(bf16).astype(f32)
            delta_3 = delta - delta_1 - delta_2
            minus = jnp.where(
                lane == 0, delta_1, jnp.where(lane == 1, delta_2, jnp.where(lane == 2, delta_3, 0.0))
            )
            left = jnp.concatenate(
                [jnp.where(mine, scaled_f, 0.0).astype(bf16), minus.astype(bf16)], axis=1
            )
            expos = e_ref[head]
            grad_logits = (expos.astype(f32) * mm_nt(left, values)).astype(bf16)
            parts.append((mm(grad_logits, keys), mm_tn(grad_logits, queries), mm_tn(expos, scaled)))
        scale = HEAD_DIM ** (-0.5)
        grad_q, grad_k, grad_v = (jnp.where(first, a, b) for a, b in zip(*parts))
        grad_q = (grad_q * scale).astype(bf16)
        grad_v = grad_v.astype(bf16)
        out_ref[0] = grad_q
        out_ref[1] = (grad_k * scale).astype(bf16)
        out_ref[2] = grad_v
        sums_ref[...] = jnp.concatenate(
            [
                jnp.sum(grad_q.astype(f32), axis=0, keepdims=True),
                jnp.sum(grad_v.astype(f32), axis=0, keepdims=True),
                jnp.zeros((6, LANES), f32),
            ],
            axis=0,
        )

    return launch(
        "attend_back", body, (pairs,), table,
        [(a, block) for a in (q, k, v)]
        + [from_hbm((expos, pl.BlockSpec((2, PACK, PACK), lambda h, *_: (h, pack, 0))))]
        + [(a, block) for a in (inverse, ctx, dctx)],
        [
            (
                jax.ShapeDtypeStruct((3, tokens, width), bf16),
                pl.BlockSpec((3, PACK, LANES), lambda h, *_: (0, pack, h)),
            ),
            (
                jax.ShapeDtypeStruct((8 * packs, width), f32),
                pl.BlockSpec((8, LANES), lambda h, *_: (pack, h)),
            ),
            out_whole((8, LANES), f32),
        ],
        into=into, after=after,
    )


def project_grads(table, send, x, grads, sums, after=()):
    tokens = x.shape[0]
    packs = tokens // PACK
    tiles = INNER_A // HALF
    offset = OTHER if send else OWN

    def half_of(t):
        return 1 - t[CORE] if send else t[CORE]

    def tile_of(i, t):
        tile = half_of(t) * tiles + i
        return (tile // 2, 0, tile % 2)

    def body(table, x_ref, d_ref, sa_ref, s2_ref, s1_ref, ff_ref, out_ref):
        step = pl.program_id(0)
        grad = mm_tn(x_ref[...], d_ref[0])
        here = pl.ds(pl.multiple_of(step * HALF, HALF), HALF)
        for chip in range(CHIPS):
            out_ref[table[offset + chip], :, here] = grad[chip * ROWS_A : (chip + 1) * ROWS_A].astype(bf16)

        @pl.when(step == 0)
        def _():
            attended = sum(sa_ref[8 * p : 8 * (p + 1), :] for p in range(packs))
            low = jnp.concatenate([attended[0:2], s1_ref[0:3, :], s2_ref[0:1, :]], axis=0)
            high = jnp.concatenate([s2_ref[1:3, :], ff_ref[0:4, :]], axis=0)
            rows = jnp.where(half_of(table) == 0, low, high)
            rows = jnp.concatenate([rows, jnp.zeros((LANES - 6, D), f32)], axis=0)
            turned = jnp.transpose(rows).astype(bf16)
            for chip in range(CHIPS):
                out_ref[table[offset + chip], :, INNER_A:] = turned[chip * ROWS_A : (chip + 1) * ROWS_A]

    return launch(
        "project_grads", body, (tiles,), table,
        [whole(x), (grads, pl.BlockSpec((1, tokens, HALF), tile_of))] + [whole(a) for a in sums],
        [out_whole((CHIPS, ROWS_A, WIDE_A), bf16)],
        after=after,
    )[0]


def token_grads(table, base, grads, w_a, after=()):
    tokens = base.shape[0]

    def body(table, base_ref, d_ref, w_ref, out_ref):
        grad_k = d_ref[1]
        low = jnp.concatenate([d_ref[0], grad_k[:, :HALF]], axis=1)
        high = jnp.concatenate([grad_k[:, HALF:], d_ref[2]], axis=1)
        out_ref[...] = base_ref[...] + mm_nt(low, w_ref[0, :, :INNER_A]) + mm_nt(high, w_ref[1, :, :INNER_A])

    return launch(
        "token_grads", body, (tokens // TILE,), table,
        [from_hbm(rows_of(base)), (grads, pl.BlockSpec((3, TILE, D), lambda i, *_: (0, i, 0)))],
        [out_rows(tokens, D, f32)],
        weights=[w_a], after=after,
    )[0]


def lamb(weight, grad, first, second, decay=weight_decay):
    first_new = beta_first * first + (1.0 - beta_first) * grad
    second_new = beta_second * second + (1.0 - beta_second) * grad * grad
    update = (first_new * (1.0 / (1.0 - beta_first**STEP))) / (
        jnp.sqrt(second_new * (1.0 / (1.0 - beta_second**STEP))) + step_eps
    )
    if decay:
        update = update + decay * weight
    return first_new, second_new, update


def square_rows(entries):
    lane = lax.broadcasted_iota(jnp.int32, (1, LANES), 1)
    rows = [jnp.zeros((1, LANES), f32), jnp.zeros((1, LANES), f32)]
    for group, arrays in entries:
        for i, a in enumerate(arrays):
            total = jnp.sum(jnp.sum(a * a, axis=1, keepdims=True), axis=0, keepdims=True)
            rows[i] = rows[i] + jnp.where(lane == group, total, 0.0)
    return jnp.concatenate(rows + [jnp.zeros((6, LANES), f32)], axis=0)


def like(array):
    return out_whole(array.shape, f32)


def step_wide(table, expand, shrink, parts_b, terms_2):
    rows = expand[0].shape[0]

    def body(table, ew, em, ev, sw, sm, sv, mine_ref, came_ref, *refs):
        term_refs = refs[: len(terms_2)]
        em_out, ev_out, eu_out, sm_out, sv_out, su_out, sums_ref = refs[len(terms_2) :]
        mine, came = mine_ref[...], came_ref[...].astype(f32)
        core = table[CORE]
        grad = jnp.concatenate(
            [
                jnp.where(core == 0, mine, came)[:, : FF // 2],
                jnp.where(core == 0, came, mine)[:, : FF // 2],
            ],
            axis=1,
        )
        em_out[...], ev_out[...], step_e = lamb(ew[...], grad, em[...], ev[...])
        eu_out[...] = step_e
        grad = sum(ref[...].astype(f32) for ref in term_refs)
        sm_out[...], sv_out[...], step_s = lamb(sw[...], grad, sm[...], sv[...])
        su_out[...] = step_s
        sums_ref[...] = square_rows([(4, (ew[...], step_e)), (5, (sw[...], step_s))])

    return launch(
        "step_wide", body, (1,), table,
        [whole(a) for a in (*expand, *shrink, *parts_b, *terms_2)],
        [like(expand[0])] * 3 + [like(shrink[0])] * 3 + [out_whole((8, LANES), f32)],

    )


def step_narrow(table, attention, vector, parts_a, parts_b, sums):
    rows = attention[0].shape[1]
    def body(table, aw, am, av, vw, vm, vv, mine_a, came_a, mine_b, came_b, sums_ref, *outs):
        am_out, av_out, au_out, vm_out, vv_out, vu_out, sums_out = outs
        core = table[CORE]

        def halves(mine_ref, came_ref):
            mine, came = mine_ref[...], came_ref[...].astype(f32)
            return jnp.where(core == 0, mine, came), jnp.where(core == 0, came, mine)

        low_a, high_a = halves(mine_a, came_a)
        low_b, high_b = halves(mine_b, came_b)
        grads = [
            low_a[:, :D],
            jnp.concatenate([low_a[:, D:INNER_A], high_a[:, :HALF]], axis=1),
            high_a[:, HALF:INNER_A],
            jnp.concatenate([low_b[:, FF // 2 :], high_b[:, FF // 2 :]], axis=1),
        ]
        entries = []
        for i, grad in enumerate(grads):
            am_out[i], av_out[i], step = lamb(aw[i], grad, am[i], av[i])
            au_out[i] = step
            entries.append((i, (aw[i], step)))
        rest = jnp.zeros((LANES - rows, LANES), f32)
        grad = jnp.concatenate(
            [
                jnp.transpose(jnp.concatenate([part[:, INNER_A:], rest], axis=0))[:6, :rows]
                for part in (low_a, high_a)
            ],
            axis=0,
        )
        vm_out[...], vv_out[...], step = lamb(vw[...], grad, vm[...], vv[...], 0.0)
        vu_out[...] = step
        entries.append((6, (vw[...], step)))
        sums_out[...] = sums_ref[...] + square_rows(entries)

    return launch(
        "step_narrow", body, (1,), table,
        [whole(a) for a in (*attention, *vector, *parts_a, *parts_b, sums)],
        [like(attention[0])] * 3 + [like(vector[0])] * 3 + [out_whole((8, LANES), f32)],

    )


def apply_step(table, sums, masters, steps):
    def body(table, sums_ref, aw, ew, sw, vw, au, eu, su, vu, a_out, e_out, s_out, v_out, norms_ref):
        master, step = sums_ref[0:1, :], sums_ref[1:2, :]
        ratio = jnp.sqrt(master) * lax.rsqrt(step + 1e-12)
        norms_ref[...] = jnp.concatenate(
            [ratio, jnp.sqrt(master), jnp.sqrt(step), jnp.zeros((5, LANES), f32)], axis=0
        )
        lane = lax.broadcasted_iota(jnp.int32, (1, LANES), 1)

        def of(group):
            return jnp.sum(jnp.where(lane == group, ratio, 0.0), axis=1, keepdims=True) * learn_rate

        for i in range(4):
            a_out[i] = aw[i] - of(i) * au[i]
        e_out[...] = ew[...] - of(4) * eu[...]
        s_out[...] = sw[...] - of(5) * su[...]
        v_out[...] = vw[...] - of(6) * vu[...]

    return launch(
        "apply_step", body, (1,), table,
        [whole(a) for a in (sums, *masters, *steps)],
        [like(a) for a in masters] + [out_whole((8, LANES), f32)],
    )


ACROSS_LAST = ((8, 4, 1, 2), (4, 8, 2, 1))
ALONG_LAST = ((1, 2, 8, 4), (2, 1, 4, 8))


def device_count():
    return lax.axis_size("dp") * lax.axis_size("cand")


def staged():
    return device_count() == 2 * CHIPS


def exchange(a, orders, stage):
    pairs = [(i, i ^ (2 * orders[i % 2][stage])) for i in range(device_count())]
    return lax.ppermute(a, BOTH, pairs)


def swap_core(a):
    return lax.ppermute(a, BOTH, [(i, i ^ 1) for i in range(device_count())])


def layout_table(index, orders):
    plain = jnp.arange(CHIPS, dtype=jnp.int32)
    if not staged():
        return jnp.concatenate([plain, plain, jnp.zeros((1,), jnp.int32), plain, plain])
    core = index % 2
    chip = index // 2

    def by_order(bits):
        position = jnp.zeros((CHIPS,), jnp.int32)
        holder = jnp.zeros((CHIPS,), jnp.int32)
        for stage, bit in enumerate(bits):
            position = position + jnp.where(((plain ^ chip) & bit) != 0, 1 << stage, 0)
            holder = holder + jnp.where((plain & (1 << stage)) != 0, bit, 0)
        return position, holder ^ chip

    parts = [by_order(bits) for bits in orders]
    own = [jnp.where(core == 0, a, b) for a, b in zip(*parts)]
    other = [jnp.where(core == 0, b, a) for a, b in zip(*parts)]
    return jnp.concatenate([own[0], other[0], core[None], own[1], other[1]]).astype(jnp.int32)


def behind(a, *others):
    return lax.optimization_barrier((a, *others))[0] if others else a


class Gathered:
    def __init__(self, table, block, rows, orders, base):
        self.table = table
        self.rows, self.orders, self.base = rows, orders, base
        self.parts = [(block, 1)]
        self.sent, self.came = [], []
        self.stage = 0
        self.others = []

    def send(self, low, high, *after):
        if self.stage == 0:
            block = behind(self.parts[0][0], *after)
        else:
            block = pick(self.table, self.parts, self.rows, low, high, after)
        came = exchange(block, self.orders, self.stage)
        self.sent.append((block, high - low))
        self.came.append((came, high - low))
        if high == 1 << self.stage:
            self.parts = (self.parts if self.stage < 3 else self.sent) + self.came
            self.sent, self.came = [], []
            self.stage += 1
        return came

    def step(self, *after):
        return self.send(0, 1 << self.stage, *after)

    def swap(self, *after):
        part = self.parts[len(self.others)][0]
        self.others.append(swap_core(behind(part, *after)))
        return self.others[-1]

    def blocks(self):
        return Blocks(self.parts, self.others, self.rows, self.base)


class Whole:
    def __init__(self, pieces, rows, base):
        halves = [(a, CHIPS // 2) for a in pieces[:2]]
        self.own = Blocks(halves, pieces[2:], rows, base)

    def send(self, low, high, *after):
        return self.own.pieces[0]

    step = swap = lambda self, *after: self.own.pieces[0]

    def blocks(self):
        return self.own


class Scattered:
    def __init__(self, table, keep, send, orders):
        self.table = table
        self.terms = [[(keep, 0)], [(swap_core(send), 0)]]
        self.orders = orders
        self.stage = 3
        self.came = []
        self.left = 1 << 3

    def send(self, low, high, *after):
        first = 1 << self.stage
        total = self.going = add_blocks(self.table, self.terms, first + low, first + high, after)
        came = exchange(total, self.orders, self.stage)
        self.came.append((came, low))
        self.left -= high - low
        if self.left == 0:
            self.next_stage()
        return came

    def next_stage(self):
        self.terms.append(self.came)
        self.came = []
        self.stage -= 1
        self.left = 1 << max(self.stage, 0)

    def step(self, *after):
        return self.send(0, 1 << self.stage, *after)

    def rest(self):
        return [next(a for a, at in term if at == 0)[0] for term in self.terms]

    def total(self):
        return sum(term.astype(f32) for term in self.rest())


def by_core(core, low, high):
    return jnp.where(core == 0, low, high)


def own_rows(core, total):
    rows = total.shape[0] // 2
    low, high = total[:rows], total[rows:]
    return by_core(core, low, high), swap_core(by_core(core, high, low).astype(bf16))


def all_sum(row):
    if device_count() & (device_count() - 1):
        return lax.psum(row, BOTH)
    bit = 1
    while bit < device_count():
        row = row + lax.ppermute(row, BOTH, [(i, i ^ bit) for i in range(device_count())])
        bit *= 2
    return row


def own_halves(attention, expand, vector):
    turned = vector.T
    rest = jnp.zeros((turned.shape[0], LANES - 6), turned.dtype)
    low = [attention[0], attention[1][:, :HALF], turned[:, :6], rest]
    high = [attention[1][:, HALF:], attention[2], turned[:, 6:], rest]
    low += [expand[:, : FF // 2], attention[3][:, :HALF]]
    high += [expand[:, FF // 2 :], attention[3][:, HALF:]]
    return jnp.concatenate(low, axis=1), jnp.concatenate(high, axis=1)


def gather_weights(table, core, attention, expand, shrink, vector):
    low, high = own_halves(attention, expand, vector)
    cuts = (0, WIDE_A, WIDE_A + WIDE_B)
    outs = []
    if not staged():
        groups = [(jnp.stack([low, high], axis=1)[:, :, a:b], ROWS_A, 0) for a, b in zip(cuts, cuts[1:])]
        for part, rows, base in groups + [(shrink[:, None], ROWS_B, TABLE)]:
            full = lax.all_gather(part, BOTH, axis=0, tiled=True)
            if rows == ROWS_B:
                full = full.reshape(CHIPS, 2, rows, D).swapaxes(1, 2)
            full = full.reshape(2, CHIPS // 2 * rows, 2, full.shape[-1])
            pieces = [full[high, :, half] for half in (0, 1) for high in (0, 1)]
            outs.append(Whole(pieces, rows, base))
        return outs
    mine = by_core(core, low, high)
    came = swap_core(by_core(core, high, low))
    chip_rows = jnp.concatenate([by_core(core, mine, came), by_core(core, came, mine)], axis=0)
    outs = [Gathered(table, chip_rows[:, a:b], ROWS_A, ACROSS_LAST, 0) for a, b in zip(cuts, cuts[1:])]
    return outs + [Gathered(table, shrink, ROWS_B, ALONG_LAST, TABLE)]


class Reduced:
    def __init__(self, table, core, keep, send, orders):
        self.core = core
        self.keep, self.other = keep, send
        self.came = keep
        if staged():
            self.work = Scattered(table, keep, send, orders)
            self.came = self.work.terms[1][0][0]

    def send(self, low, high, *after):
        if not staged():
            return self.keep, self.keep
        came = self.work.send(low, high, *after)
        return self.work.going, came

    def step(self, *after):
        return self.send(0, 1 << self.work.stage if staged() else 0, *after)

    def halves(self):
        if staged():
            return own_rows(self.core, self.work.total())
        both = jnp.stack([self.keep, self.other], axis=2).reshape(D, 2, self.keep.shape[2]).astype(f32)
        total = lax.psum_scatter(both, BOTH, scatter_dimension=0, tiled=True)
        return total[:, 0], total[:, 1]

    def shard(self):
        if staged():
            return self.work.rest()
        both = jnp.stack([self.keep, self.other], axis=1).reshape(FF, D).astype(f32)
        return [lax.psum_scatter(both, BOTH, scatter_dimension=0, tiled=True)]


def per_device(
    tokens,
    score_vec,
    pair_lengths,
    query_ids,
    labels,
    attention_weight,
    expand_weight,
    shrink_weight,
    vector_weight,
    attention_first,
    expand_first,
    shrink_first,
    vector_first,
    attention_second,
    expand_second,
    shrink_second,
    vector_second,
):
    index = lax.axis_index(BOTH)
    core = index % 2
    ends = jnp.cumsum(pair_lengths, axis=-1, dtype=jnp.int32)
    table = jnp.concatenate(
        [layout_table(index, ACROSS_LAST), layout_table(index, ALONG_LAST), ends.reshape(-1)]
    )
    get_a, get_b, get_2 = gather_weights(
        table,
        core,
        attention_weight.astype(bf16),
        expand_weight.astype(bf16),
        shrink_weight.astype(bf16),
        vector_weight.astype(bf16),
    )

    pack_count = pair_lengths.shape[0]
    pairs = pack_count * PAIRS_PACK
    def in_lanes(values, filler):
        row = values.astype(f32).reshape(1, pairs)
        return jnp.pad(row, ((0, 0), (0, LANES - pairs)), constant_values=filler)

    facts = jnp.concatenate(
        [
            jnp.zeros((1, LANES), f32),
            in_lanes(query_ids, -1.0),
            in_lanes(labels, 0.0),
            in_lanes(pair_lengths, 1.0),
            jnp.zeros((4, LANES), f32),
        ],
        axis=0,
    )
    score_row = score_vec.reshape(1, D)

    came_a = get_a.step()
    came_2 = get_2.step()
    came_2 = get_2.step(came_a)
    came_a = get_a.step()
    came_b = get_b.step(came_a)
    came_a_2 = get_a.step(came_2)
    came_a = get_a.step(came_b)
    came_b = get_b.step(came_a_2)
    get_a.swap()
    get_a.swap()
    w_a = get_a.blocks()
    q, k, v, vec = project(table, tokens, w_a, after=[came_b, facts])
    came_2 = get_2.send(0, 1, came_a, came_b)
    came_b = get_b.step(came_a)
    *parts, end = attend(table, 0, q, k, v, after=[q])
    came = [came_2, came_b]
    came = [get_2.send(1, 4, q, *came), get_b.send(0, 4, q, *came)]
    for pack in range(1, pack_count):
        *parts, end_all = attend(table, pack, q, k, v, parts, after=[end])
    ctx, expos, inverse = parts
    came = [get_b.send(4, 8, end, *came), get_2.send(0, 2, end, *came)]
    get_b.swap(q)
    get_b.swap(end)
    get_b.swap(end)
    get_b.swap(end_all)
    w_b = get_b.blocks()
    n1, r1, first_b, active, slope = expand_rows(table, tokens, ctx, w_b, vec)
    get_2.send(2, 8, end_all, *came)
    get_2.swap(end_all)
    get_2.swap(end_all)
    get_2.swap(end_all)
    get_2.swap(first_b)
    w_2 = get_2.blocks()
    n2, r2, stats = shrink_rows(table, active, w_2, n1, vec, score_row, facts)

    n_cand = lax.axis_size("cand")
    blocks = [stats] + [
        lax.ppermute(stats, "cand", [(i, (i + shift) % n_cand) for i in range(n_cand)])
        for shift in range(1, n_cand)
    ]
    outer, dh2, keep_2, send_2, sums_2, grad_block = shrink_back(
        table, blocks, n2, r2, vec, score_row, active
    )
    put_2 = Reduced(table, core, keep_2, send_2, ALONG_LAST)
    inner, dh1, attn, dctx, sums_1, sums_ff = rows_back(table, outer, dh2, slope, n1, r1, w_2, w_b, vec)
    goes, came = put_2.send(6, 8, inner)
    send_b = expand_grads(table, True, first_b, ctx, inner, attn, after=[goes])
    goes, came = put_2.send(4, 6, send_b, came)
    keep_b = expand_grads(table, False, first_b, ctx, inner, attn, after=[send_b, goes])
    put_b = Reduced(table, core, keep_b, send_b, ACROSS_LAST)
    goes, came = zip(put_2.send(0, 4, keep_b, came, put_b.came), put_b.send(2, 8, came))
    *parts, end = attend_back(table, 0, q, k, v, expos, inverse, ctx, dctx, after=[keep_b, *goes])
    goes, came = zip(
        put_2.send(0, 2, end, *came),
        put_2.send(2, 4, end, *came),
        put_b.send(0, 2, end, *came),
        put_b.step(end, *came),
    )
    for pack in range(1, pack_count):
        *parts, end_all = attend_back(
            table, pack, q, k, v, expos, inverse, ctx, dctx, parts, after=[end, *goes]
        )
    grads, sums_attn = parts
    sums = [sums_attn, sums_2, sums_1, sums_ff]
    goes, came = put_2.step(end_all, *came)
    send_a = project_grads(table, True, tokens, grads, sums, after=[goes])
    goes, came = put_2.step(send_a, came)
    keep_a = project_grads(table, False, tokens, grads, sums, after=[send_a, goes])
    put_a = Reduced(table, core, keep_a, send_a, ACROSS_LAST)
    goes, came = zip(put_a.step(came), put_b.step(keep_a, came))
    grad_tokens = token_grads(table, dh1, grads, w_a, after=[keep_a, put_a.came, *goes])
    goes, came_a = put_a.step(grad_tokens)
    put_b.step(grad_tokens, goes)
    put_a.step()
    put_a.step()
    parts_b = put_b.halves()
    expand_moment, expand_square, expand_step, shrink_moment, shrink_square, shrink_step, sums = step_wide(
        table,
        (expand_weight, expand_first, expand_second),
        (shrink_weight, shrink_first, shrink_second),
        parts_b,
        put_2.shard(),
    )
    parts_a = put_a.halves()
    (
        attention_moment,
        attention_square,
        attention_step,
        vector_moment,
        vector_square,
        vector_step,
        sums,
    ) = step_narrow(
        table,
        (attention_weight, attention_first, attention_second),
        (vector_weight, vector_first, vector_second),
        parts_a,
        parts_b,
        sums,
    )
    attention_new, expand_new, shrink_new, vector_new, norms = apply_step(
        table,
        all_sum(sums),
        (attention_weight, expand_weight, shrink_weight, vector_weight),
        (attention_step, expand_step, shrink_step, vector_step),
    )
    return (
        grad_tokens,
        stats[0, :pairs],
        grad_block[0, :pairs],
        norms[0, :7],
        norms[1:3, :7],
        attention_new,
        expand_new,
        shrink_new,
        vector_new,
        attention_moment,
        expand_moment,
        shrink_moment,
        vector_moment,
        attention_square,
        expand_square,
        shrink_square,
        vector_square,
    )


def solution(mesh):
    placed = (
        P(("dp", "cand"), None),
        P(),
        P(("dp", "cand"), None),
        P(("dp", "cand")),
        P(("dp", "cand")),
        P(None, ("dp", "cand"), None),
        P(("dp", "cand"), None),
        P(("dp", "cand"), None),
        P(None, ("dp", "cand")),
        P(None, ("dp", "cand"), None),
        P(("dp", "cand"), None),
        P(("dp", "cand"), None),
        P(None, ("dp", "cand")),
        P(None, ("dp", "cand"), None),
        P(("dp", "cand"), None),
        P(("dp", "cand"), None),
        P(None, ("dp", "cand")),
    )
    return jax.shard_map(
        per_device,
        mesh=mesh,
        in_specs=placed,
        out_specs=(
            P(("dp", "cand"), None),
            P(("dp", "cand")),
            P(("dp", "cand")),
            P(),
            P(),
            P(None, ("dp", "cand"), None),
            P(("dp", "cand"), None),
            P(("dp", "cand"), None),
            P(None, ("dp", "cand")),
            P(None, ("dp", "cand"), None),
            P(("dp", "cand"), None),
            P(("dp", "cand"), None),
            P(None, ("dp", "cand")),
            P(None, ("dp", "cand"), None),
            P(("dp", "cand"), None),
            P(("dp", "cand"), None),
            P(None, ("dp", "cand")),
        ),
        check_vma=False,
    )
```

```python
import functools

import jax
import jax.numpy as jnp
from jax import lax
from jax.experimental import pallas as pl
from jax.experimental.pallas import tpu as pltpu
from jax.sharding import PartitionSpec as P

D = 768
HEADS = 12
HEAD_DIM = 64
FF = 3072
PACK = 512
PAIRS_PACK = 4
STEP = 10
QUERIES_DEV = 2

norm_eps = 1e-05
beta_first = 0.9
beta_second = 0.999
learn_rate = 1.0
weight_decay = 0.01
step_eps = 1e-06
masked_fill = -1e30

BOTH = ("dp", "cand")
LANES = 128
CHIPS = 16
ROWS_A = D // CHIPS
ROWS_B = FF // CHIPS // 2
HALF = D // 2
INNER_A = D + HALF
WIDE_A = INNER_A + LANES
WIDE_B = FF // 2 + HALF
TILE = 256
MIB = 1 << 20
ROOM = {
    "project": 12,
    "attend": 16,
    "expand_rows": 20,
    "shrink_rows": 14,
    "shrink_back": 25,
    "rows_back": 28,
    "expand_grads": 14,
    "attend_back": 20,
    "project_grads": 16,
    "token_grads": 16,
    "own_halves": 12,
    "pick": 12,
    "add_blocks": 12,
    "step_wide": 12,
    "step_narrow": 12,
    "apply_step": 12,
}
bf16 = jnp.bfloat16
f32 = jnp.float32
B_Q, B_V, B_O, G_1, S_1, B_2, G_2, S_2, B_FF = range(9)
VECTORS = 12
OWN, OTHER, CORE, OWN_CHIP, OTHER_CHIP = 0, CHIPS, 2 * CHIPS, 2 * CHIPS + 1, 3 * CHIPS + 1
TABLE = 4 * CHIPS + 1
ENDS = 2 * TABLE


def mm(a, b):
    return lax.dot_general(a, b, (((1,), (0,)), ((), ())), preferred_element_type=f32)


def mm_nt(a, b):
    return lax.dot_general(a, b, (((1,), (1,)), ((), ())), preferred_element_type=f32)


def mm_tn(a, b):
    return lax.dot_general(a, b, (((0,), (0,)), ((), ())), preferred_element_type=f32)


def row_mean(v):
    return jnp.sum(v, axis=1, keepdims=True) * (1.0 / D)


def norm_parts(hidden):
    center = hidden - row_mean(hidden)
    inverse = lax.rsqrt(row_mean(center * center) + norm_eps)
    return center * inverse, inverse


def segments(table, pack, first_row, rows):
    row = lax.broadcasted_iota(jnp.int32, (rows, LANES), 0) + first_row
    return sum(
        jnp.where(row >= table[ENDS + pack * PAIRS_PACK + i], 1, 0) for i in range(PAIRS_PACK)
    )


def whole(array):
    zeros = (0,) * array.ndim
    return array, pl.BlockSpec(array.shape, lambda *_: zeros, pipeline_mode=pl.Buffered(1))


def rows_of(array, tile=TILE):
    return array, pl.BlockSpec((tile, array.shape[1]), lambda i, *_: (i, 0))


def out_rows(tokens, width, dtype, tile=TILE):
    return jax.ShapeDtypeStruct((tokens, width), dtype), pl.BlockSpec((tile, width), lambda i, *_: (i, 0))


def in_hbm(out):
    shape, spec = out
    return pltpu.HBM(shape.shape, shape.dtype), spec


def in_vmem(out):
    shape, spec = out
    return pltpu.VMEM(shape.shape, shape.dtype), spec


def from_hbm(operand):
    array, spec = operand
    return pltpu.with_memory_space_constraint(array, pltpu.HBM), spec


def out_whole(shape, dtype):
    zeros = (0,) * len(shape)
    return jax.ShapeDtypeStruct(shape, dtype), pl.BlockSpec(shape, lambda *_: zeros)


def behind(a, *others):
    return lax.optimization_barrier((a, *others))[0] if others else a


def launch(name, body, grid, table, operands, outs, scratch=(), weights=(), after=(), into=(), mark=False):
    operands = list(operands)
    count = len(operands)
    outs = list(outs)
    idle = pl.BlockSpec(memory_space=pl.ANY)
    arrays = [a for a, _ in operands]
    specs = [spec for _, spec in operands]
    rooms = []
    for weight in weights:
        arrays += [pltpu.with_memory_space_constraint(a, pltpu.HBM) for a in weight.pieces]
        specs += [idle] * len(weight.pieces)
        rooms += [pltpu.VMEM(weight.shape, bf16), pltpu.SemaphoreType.DMA]
    aliases = {1 + len(arrays) + i: i for i in range(len(into))}
    arrays += list(into) + list(after)
    specs += [idle] * (len(into) + len(after))
    if mark:
        outs.append(out_whole((8, LANES), f32))

    def kernel(table_ref, *refs):
        ins = refs[:count]
        rest = refs[len(arrays) :]
        held = rest[len(outs) + len(scratch) :]
        if weights:

            @pl.when(pl.program_id(0) == 0)
            def _():
                copies, at = [], count
                for i, weight in enumerate(weights):
                    pieces = refs[at : at + len(weight.pieces)]
                    at += len(pieces)
                    copies += weight.copies(table_ref, pieces, held[2 * i], held[2 * i + 1])
                for copy in copies:
                    copy.start()
                for i in range(len(weights)):
                    everything, sem = held[2 * i], held[2 * i + 1]
                    pltpu.make_async_copy(everything, everything, sem).wait()

        own = list(rest[: len(outs) + len(scratch)])
        if mark:
            own.pop(len(outs) - 1)[...] = jnp.zeros((8, LANES), f32)
        body(table_ref, *ins, *held[::2], *own)

    results = pl.pallas_call(
        kernel,
        out_shape=[shape for shape, _ in outs],
        grid_spec=pltpu.PrefetchScalarGridSpec(
            num_scalar_prefetch=1,
            grid=grid,
            in_specs=specs,
            out_specs=[spec for _, spec in outs],
            scratch_shapes=list(scratch) + rooms,
        ),
        input_output_aliases=aliases,
        compiler_params=pltpu.CompilerParams(vmem_limit_bytes=ROOM[name] * MIB),
        name=name,
    )(table, *arrays)
    return results


def own_halves(table, attention, expand, vector):
    rows = attention.shape[1]

    def body(table, a_ref, e_ref, v_ref, mine_ref, theirs_ref):
        core = table[CORE]
        vector = jnp.concatenate([v_ref[...], jnp.zeros((VECTORS, LANES - rows), f32)], axis=1)
        vector = jnp.concatenate([vector, jnp.zeros((LANES - VECTORS, LANES), f32)], axis=0)
        turned = jnp.transpose(vector)[:rows]
        lane = lax.broadcasted_iota(jnp.int32, (rows, LANES), 1)
        turned_high = jnp.concatenate([turned[:, 6:], jnp.zeros((rows, 6), f32)], axis=1)
        q, k, v, o = (a_ref[i] for i in range(4))
        expand = e_ref[...]
        low = [q, k[:, :HALF], jnp.where(lane < 6, turned, 0.0), expand[:, : FF // 2], o[:, :HALF]]
        high = [k[:, HALF:], v, jnp.where(lane < 6, turned_high, 0.0), expand[:, FF // 2 :], o[:, HALF:]]
        low, high = (jnp.concatenate(parts, axis=1) for parts in (low, high))
        mine_ref[...] = jnp.where(core == 0, low, high).astype(bf16)
        theirs_ref[...] = jnp.where(core == 0, high, low).astype(bf16)

    return launch(
        "own_halves", body, (1,), table, [whole(a) for a in (attention, expand, vector)],
        [out_whole((rows, WIDE_A + WIDE_B), bf16)] * 2,
    )


def pick(table, parts, rows, low, high, after=()):
    width = parts[0][0].shape[1]
    moves, used, at = [], [], 0
    for array, count in parts:
        start, stop = max(low, at), min(high, at + count)
        if start < stop:
            moves.append(((start - at) * rows, (start - low) * rows, (stop - start) * rows))
            used.append(array)
        at += count

    def body(table, *refs):
        for ref, (source, target, size) in zip(refs[:-1], moves):
            refs[-1][target : target + size, :] = ref[source : source + size, :]

    return launch(
        "pick", body, (1,), table, [whole(a) for a in used],
        [out_whole(((high - low) * rows, width), bf16)], after=after,
    )[0]


def add_blocks(table, terms, low, high, after=()):
    operands, cuts = [], []
    for term in terms:
        used = sorted(
            [(at, a) for a, at in term if at < high and low < at + a.shape[0]], key=lambda part: part[0]
        )
        cuts.append([at - low for at, _ in used[1:]])
        for at, array in used:
            last, rows, width = array.shape
            spec = pl.BlockSpec(
                (1, rows, width),
                lambda i, *_, skip=low - at, last=last - 1: (jnp.clip(i + skip, 0, last), 0, 0),
            )
            operands.append((array, spec))

    def body(table, *refs):
        step = pl.program_id(0)
        total, at = 0.0, 0
        for term_cuts in cuts:
            value = refs[at][...].astype(f32)
            at += 1
            for cut in term_cuts:
                value = jnp.where(step >= cut, refs[at][...].astype(f32), value)
                at += 1
            total = total + value
        refs[-1][...] = total.astype(bf16)

    return launch(
        "add_blocks", body, (high - low,), table, operands,
        [
            (
                jax.ShapeDtypeStruct((high - low, rows, width), bf16),
                pl.BlockSpec((1, rows, width), lambda i, *_: (i, 0, 0)),
            )
        ],
        after=after,
    )[0]


class Blocks:
    def __init__(self, own, others, rows, base):
        self.counts = [count for _, count in own]
        self.pieces = [a for a, _ in own] + list(others)
        self.rows = rows
        self.base = base
        width = self.pieces[0].shape[1]
        self.shape = (2 * CHIPS * rows, width) if rows == ROWS_B else (2, CHIPS * rows, width)

    def copies(self, table, refs, whole_ref, sem):
        core = table[CORE]
        out = []
        places = [(piece, at) for piece, count in enumerate(self.counts) for at in range(count)]
        for position, (piece, at) in enumerate(places):
            for which in range(2):
                chip = table[self.base + (OWN_CHIP, OTHER_CHIP)[which] + position]
                half = core if which == 0 else 1 - core
                if self.rows == ROWS_B:
                    at_row = pl.multiple_of((2 * chip + half) * self.rows, self.rows)
                    there = whole_ref.at[pl.ds(at_row, self.rows)]
                else:
                    at_row = pl.multiple_of(chip * self.rows, self.rows)
                    there = whole_ref.at[half, pl.ds(at_row, self.rows)]
                here = refs[which * len(self.counts) + piece].at[pl.ds(at * self.rows, self.rows)]
                out.append(pltpu.make_async_copy(here, there, sem))
        return out


def project(table, x, w_a, after=()):
    tokens = x.shape[0]

    def body(table, x_ref, w_ref, q_ref, k_ref, v_ref, vec_ref):
        @pl.when(pl.program_id(0) == 0)
        def _():
            for half in range(2):
                turned = jnp.transpose(w_ref[half, :, INNER_A:].astype(f32))
                vec_ref[6 * half : 6 * half + 6, :] = turned[:6]

        x = x_ref[...]
        low = mm(x, w_ref[0, :, :INNER_A])
        q_ref[...] = (low[:, :D] + vec_ref[B_Q : B_Q + 1, :]).astype(bf16)
        k_ref[:, :HALF] = low[:, D:].astype(bf16)
        high = mm(x, w_ref[1, :, :INNER_A])
        k_ref[:, HALF:] = high[:, :HALF].astype(bf16)
        v_ref[...] = (high[:, HALF:] + vec_ref[B_V : B_V + 1, :]).astype(bf16)

    return launch(
        "project", body, (tokens // TILE,), table,
        [rows_of(x)], [out_rows(tokens, D, bf16)] * 3 + [out_whole((16, D), f32)],
        weights=[w_a], after=after, mark=True,
    )


def attend(table, pack, q, k, v, into=(), after=()):
    tokens, width = q.shape
    pair_block = pl.BlockSpec((PACK, LANES), lambda h, *_: (pack, h))

    def body(table, q_ref, k_ref, v_ref, ctx_ref, e_ref, inv_ref):
        lane = lax.broadcasted_iota(jnp.int32, (PACK, LANES), 1)
        segment = segments(table, pack, 0, PACK)
        apart = jnp.where((lane < PAIRS_PACK) & (lane != segment), masked_fill, 0.0).astype(bf16)
        belongs = jnp.where(lane == segment, 1.0, 0.0).astype(bf16)
        keys = jnp.concatenate([k_ref[...], belongs], axis=1)
        values = jnp.concatenate([v_ref[...], jnp.ones((PACK, LANES), bf16)], axis=1)
        queries = q_ref[...].astype(f32) * HEAD_DIM ** (-0.5)
        first = lane < HEAD_DIM
        outs = []
        for head in range(2):
            mine = jnp.where(first if head == 0 else ~first, queries, 0.0).astype(bf16)
            logits = mm_nt(jnp.concatenate([mine, apart], axis=1), keys)
            peak = jnp.max(logits, axis=1, keepdims=True)
            expos = jnp.exp(logits - peak).astype(bf16)
            e_ref[head] = expos
            outs.append(mm(expos, values))
        total = jnp.where(first, outs[0][:, LANES:], outs[1][:, LANES:])
        inverse = 1.0 / total
        inv_ref[...] = inverse
        ctx_ref[...] = (jnp.where(first, outs[0][:, :LANES], outs[1][:, :LANES]) * inverse).astype(bf16)

    heads = width // HEAD_DIM
    return launch(
        "attend", body, (heads // 2,), table,
        [(a, pair_block) for a in (q, k, v)],
        [
            (jax.ShapeDtypeStruct((tokens, width), bf16), pair_block),
            in_hbm(
                (
                    jax.ShapeDtypeStruct((heads, tokens, PACK), bf16),
                    pl.BlockSpec((2, PACK, PACK), lambda h, *_: (h, pack, 0)),
                )
            ),
            (jax.ShapeDtypeStruct((tokens, width), f32), pair_block),
        ],
        into=into, after=after, mark=True,
    )


def gelu_parts(v):
    phi = 0.5 + 0.5 * lax.erf(v * 0.7071067811865476)
    return v * phi, phi + v * (jnp.exp(v * v * -0.5) * 0.3989422804014327)


def expand_rows(table, x, ctx, w_b, vec, after=()):
    tokens = x.shape[0]
    step = HALF

    def body(table, x_ref, ctx_ref, vec_ref, w_ref, n1_ref, r1_ref, fb_ref, act_ref, slope_ref):
        ctx = ctx_ref[...]
        attended = jnp.concatenate([mm(ctx, w_ref[half, :, FF // 2 :]) for half in range(2)], axis=1)
        hidden = x_ref[...].astype(f32) + attended + vec_ref[B_O : B_O + 1, :]
        normed, inverse = norm_parts(hidden)
        n1_ref[...] = normed
        r1_ref[...] = jnp.broadcast_to(inverse, (TILE, LANES))
        first_b = (normed * vec_ref[G_1 : G_1 + 1, :] + vec_ref[S_1 : S_1 + 1, :]).astype(bf16)
        fb_ref[...] = first_b
        for j in range(FF // step):
            half, at = divmod(j * step, FF // 2)
            row, column = divmod(j * step, D)
            bias = vec_ref[B_FF + row : B_FF + row + 1, column : column + step]
            active, slope = gelu_parts(mm(first_b, w_ref[half, :, at : at + step]) + bias)
            act_ref[:, j * step : (j + 1) * step] = active.astype(bf16)
            slope_ref[:, j * step : (j + 1) * step] = slope.astype(bf16)

    return launch(
        "expand_rows", body, (tokens // TILE,), table,
        [rows_of(x), rows_of(ctx), whole(vec)],
        [
            in_hbm(out_rows(tokens, D, f32)),
            in_hbm(out_rows(tokens, LANES, f32)),
            in_hbm(out_rows(tokens, D, bf16)),
            in_vmem(out_rows(tokens, FF, bf16)),
            in_hbm(out_rows(tokens, FF, bf16)),
        ],
        weights=[w_b], after=after, mark=True,
    )


def shrink_rows(table, active, w_2, n1, vec, score_vec, facts, after=()):
    tokens = active.shape[0]

    def body(table, act_ref, n1_ref, vec_ref, sv_ref, facts_ref, w_ref, n2_ref, r2_ref, stats_ref):
        step = pl.program_id(0)
        outer = mm(act_ref[...], w_ref[...])
        first_out = n1_ref[...] * vec_ref[G_1 : G_1 + 1, :] + vec_ref[S_1 : S_1 + 1, :]
        normed, inverse = norm_parts(first_out + outer + vec_ref[B_2 : B_2 + 1, :])
        n2_ref[...] = normed
        r2_ref[...] = jnp.broadcast_to(inverse, (TILE, LANES))
        score_vec = sv_ref[...]
        final = normed * vec_ref[G_2 : G_2 + 1, :] + vec_ref[S_2 : S_2 + 1, :]
        row_score = jnp.sum(final * score_vec, axis=1, keepdims=True)
        lane = lax.broadcasted_iota(jnp.int32, (TILE, LANES), 1)
        pack = step // (PACK // TILE)
        segment = segments(table, pack, step % (PACK // TILE) * TILE, TILE)
        here = lane == segment + pack * PAIRS_PACK
        shares = jnp.sum(jnp.where(here, row_score, 0.0), axis=0, keepdims=True)

        @pl.when(step == 0)
        def _():
            stats_ref[...] = facts_ref[...]

        stats_ref[0:1, :] += shares

        @pl.when(step == pl.num_programs(0) - 1)
        def _():
            stats_ref[0:1, :] = stats_ref[0:1, :] / facts_ref[3:4, :]

    return launch(
        "shrink_rows", body, (tokens // TILE,), table,
        [rows_of(active), from_hbm(rows_of(n1)), whole(vec), whole(score_vec), whole(facts)],
        [out_rows(tokens, D, f32), out_rows(tokens, LANES, f32), out_whole((8, LANES), f32)],
        weights=[w_2], after=after,
    )


def loss_parts(blocks):
    own = blocks[0]
    own_ids = own[1:2]
    grads = -own[2:3]
    for query in range(QUERIES_DEV):
        inside = [b[1:2] == float(query) for b in blocks]
        peak = functools.reduce(
            jnp.maximum,
            [jnp.where(i, b[0:1], masked_fill) for i, b in zip(inside, blocks)],
        )
        peak = jnp.max(peak, axis=1, keepdims=True)
        total = sum(jnp.where(i, jnp.exp(jnp.where(i, b[0:1] - peak, 0.0)), 0.0) for i, b in zip(inside, blocks))
        total = jnp.sum(total, axis=1, keepdims=True)
        labels = sum(jnp.where(i, b[2:3], 0.0) for i, b in zip(inside, blocks))
        labels = jnp.sum(labels, axis=1, keepdims=True)
        share = jnp.exp(jnp.where(inside[0], own[0:1] - peak, 0.0)) / total * labels
        grads = grads + jnp.where(own_ids == float(query), share, 0.0)
    return jnp.where(own_ids >= 0.0, grads, 0.0)


def shrink_back(table, blocks, n2, r2, vec, score_vec, active, after=()):
    tokens = n2.shape[0]
    count = len(blocks)

    def body(table, *refs):
        block_refs = refs[:count]
        n2_ref, r2_ref, vec_ref, sv_ref, act_ref = refs[count : count + 5]
        outer_ref, dh_ref, keep_ref, send_ref, sums_ref, grads_ref = refs[count + 5 :]
        step = pl.program_id(0)
        core = table[CORE]

        @pl.when(step == 0)
        def _():
            parts = [b[...] for b in block_refs]
            grads = loss_parts(parts)
            grads_ref[...] = jnp.broadcast_to(grads, (8, LANES))
            per_row = grads / parts[0][3:4]
            score_vec = sv_ref[...]
            weighted = score_vec * vec_ref[G_2 : G_2 + 1, :]
            middle = jnp.mean(weighted, axis=1, keepdims=True)
            lane = lax.broadcasted_iota(jnp.int32, (TILE, LANES), 1)
            bias = jnp.zeros((1, D), f32)
            gain = jnp.zeros((1, D), f32)
            shift = jnp.zeros((1, 1), f32)
            for i in range(tokens // TILE):
                here = pl.ds(i * TILE, TILE)
                pack, first_row = divmod(i * TILE, PACK)
                pair = segments(table, pack, first_row, TILE) + pack * PAIRS_PACK
                scale = jnp.sum(jnp.where(lane == pair, per_row, 0.0), axis=1, keepdims=True)
                normed = n2_ref[here, :]
                along = row_mean(normed * weighted)
                back = (scale * r2_ref[here, :1]) * (weighted - middle - normed * along)
                dh_ref[here, :] = back
                rounded = back.astype(bf16)
                outer_ref[here, :] = rounded
                bias = bias + jnp.sum(rounded.astype(f32), axis=0, keepdims=True)
                gain = gain + jnp.sum(normed * scale, axis=0, keepdims=True)
                shift = shift + jnp.sum(scale, axis=0, keepdims=True)
            sums_ref[...] = jnp.concatenate(
                [bias, gain * score_vec, shift * score_vec, jnp.zeros((5, D), f32)], axis=0
            )

        grad = mm_tn(act_ref[...], outer_ref[...])
        for pair in range(2):
            chip = 2 * step + pair
            at = pair * 2 * ROWS_B
            low = grad[at : at + ROWS_B].astype(bf16)
            high = grad[at + ROWS_B : at + 2 * ROWS_B].astype(bf16)
            keep_ref[table[TABLE + OWN + chip]] = jnp.where(core == 0, low, high)
            send_ref[table[TABLE + OTHER + chip]] = jnp.where(core == 0, high, low)

    return launch(
        "shrink_back", body, (CHIPS // 2,), table,
        [whole(b) for b in blocks]
        + [whole(a) for a in (n2, r2, vec, score_vec)]
        + [(active, pl.BlockSpec((tokens, 4 * ROWS_B), lambda i, *_: (0, i)))],
        [
            out_whole((tokens, D), bf16),
            in_hbm(out_whole((tokens, D), f32)),
            out_whole((CHIPS, ROWS_B, D), bf16),
            out_whole((CHIPS, ROWS_B, D), bf16),
            out_whole((8, D), f32),
            out_whole((8, LANES), f32),
        ],
        after=after,
    )


def rows_back(table, outer, dh2, slope, n1, r1, w_2, w_b, vec, after=()):
    tokens = outer.shape[0]

    def body(
        table, outer_ref, dh_ref, slope_ref, n1_ref, r1_ref, vec_ref, w2_ref, wb_ref,
        inner_ref, dh1_ref, attn_ref, dctx_ref, sums_ref, ff_ref,
    ):
        @pl.when(pl.program_id(0) == 0)
        def _():
            sums_ref[...] = jnp.zeros_like(sums_ref)
            ff_ref[...] = jnp.zeros_like(ff_ref)

        outer = outer_ref[...]
        first = dh_ref[...]
        step = D
        for j in range(FF // step):
            half, at = divmod(j * step, FF // 2)
            here = slice(j * step, (j + 1) * step)
            active = mm_nt(outer, w2_ref[here, :])
            inner = (active * slope_ref[:, here].astype(f32)).astype(bf16)
            inner_ref[:, here] = inner
            ff_ref[j : j + 1, :] += jnp.sum(inner.astype(f32), axis=0, keepdims=True)
            first = first + mm_nt(inner, wb_ref[half, :, at : at + step])
        normed = n1_ref[...]
        dn = first * vec_ref[G_1 : G_1 + 1, :]
        back = r1_ref[:, :1] * (dn - row_mean(dn) - normed * row_mean(dn * normed))
        dh1_ref[...] = back
        rounded = back.astype(bf16)
        attn_ref[...] = rounded
        sums_ref[0:1, :] += jnp.sum(rounded.astype(f32), axis=0, keepdims=True)
        sums_ref[1:2, :] += jnp.sum(first * normed, axis=0, keepdims=True)
        sums_ref[2:3, :] += jnp.sum(first, axis=0, keepdims=True)
        dctx = mm_nt(rounded[:, :HALF], wb_ref[0, :, FF // 2 :]) + mm_nt(
            rounded[:, HALF:], wb_ref[1, :, FF // 2 :]
        )
        dctx_ref[...] = dctx.astype(bf16)

    return launch(
        "rows_back", body, (tokens // TILE,), table,
        [rows_of(outer), from_hbm(rows_of(dh2)), from_hbm(rows_of(slope)), from_hbm(rows_of(n1)), from_hbm(rows_of(r1)), whole(vec)],
        [
            in_vmem(out_rows(tokens, FF, bf16)),
            in_hbm(out_rows(tokens, D, f32)),
            out_rows(tokens, D, bf16),
            out_rows(tokens, D, bf16),
            out_whole((8, D), f32),
            out_whole((8, D), f32),
        ],
        weights=[w_2, w_b], after=after, mark=True,
    )


def expand_grads(table, send, first_b, ctx, inner, attn, after=()):
    tokens = first_b.shape[0]
    tiles = WIDE_B // HALF

    def half_of(t):
        return 1 - t[CORE] if send else t[CORE]

    def body(table, fb_ref, ctx_ref, inner_ref, attn_ref, out_ref):
        step = pl.program_id(0)
        offset = OTHER if send else OWN

        def put(grad):
            for chip in range(CHIPS):
                out_ref[table[offset + chip]] = grad[chip * ROWS_A : (chip + 1) * ROWS_A].astype(bf16)

        @pl.when(step < tiles - 1)
        def _():
            put(mm_tn(fb_ref[...], inner_ref[...]))

        @pl.when(step == tiles - 1)
        def _():
            put(mm_tn(ctx_ref[...], attn_ref[...]))

    return launch(
        "expand_grads", body, (tiles,), table,
        [whole(first_b), whole(ctx)]
        + [
            (
                inner,
                pl.BlockSpec(
                    (tokens, HALF),
                    lambda i, t: (0, half_of(t) * (tiles - 1) + jnp.minimum(i, tiles - 2)),
                ),
            ),
            (attn, pl.BlockSpec((tokens, HALF), lambda i, t: (0, half_of(t)))),
        ],
        [
            (
                jax.ShapeDtypeStruct((CHIPS, ROWS_A, WIDE_B), bf16),
                pl.BlockSpec((CHIPS, ROWS_A, HALF), lambda i, t: (0, 0, i)),
            )
        ],
        after=after, mark=True,
    )


def attend_back(table, pack, q, k, v, expos, inverse, ctx, dctx, into=(), after=()):
    tokens, width = q.shape
    packs = tokens // PACK
    wide = 2 * LANES
    block = pl.BlockSpec((PACK, wide), lambda h, *_: (pack, h))

    def pair(q, k, v, e_ref, first_head, inverse, ctx, dctx):
        lane = lax.broadcasted_iota(jnp.int32, (PACK, LANES), 1)
        first = lane < HEAD_DIM
        scaled = (dctx.astype(f32) * inverse).astype(bf16)
        scaled_f = scaled.astype(f32)
        product = scaled_f * ctx.astype(f32)
        values = jnp.concatenate([v, jnp.where(lane < 3, 1.0, 0.0).astype(bf16)], axis=1)
        parts = []
        for head in range(2):
            mine = first if head == 0 else ~first
            delta = -jnp.sum(jnp.where(mine, product, 0.0), axis=1, keepdims=True)
            delta_1 = delta.astype(bf16).astype(f32)
            delta_2 = (delta - delta_1).astype(bf16).astype(f32)
            delta_3 = delta - delta_1 - delta_2
            minus = jnp.where(
                lane == 0, delta_1, jnp.where(lane == 1, delta_2, jnp.where(lane == 2, delta_3, 0.0))
            )
            left = jnp.concatenate(
                [jnp.where(mine, scaled_f, 0.0).astype(bf16), minus.astype(bf16)], axis=1
            )
            expos = e_ref[first_head + head]
            grad_logits = (expos.astype(f32) * mm_nt(left, values)).astype(bf16)
            parts.append((mm(grad_logits, k), mm_tn(grad_logits, q), mm_tn(expos, scaled)))
        scale = HEAD_DIM ** (-0.5)
        grad_q, grad_k, grad_v = (jnp.where(first, a, b) for a, b in zip(*parts))
        return (grad_q * scale).astype(bf16), (grad_k * scale).astype(bf16), grad_v.astype(bf16)

    def body(table, q_ref, k_ref, v_ref, e_ref, inv_ref, ctx_ref, dctx_ref, out_ref, sums_ref):
        for i in range(2):
            here = slice(i * LANES, (i + 1) * LANES)
            grad_q, grad_k, grad_v = pair(
                q_ref[:, here], k_ref[:, here], v_ref[:, here], e_ref, 2 * i,
                inv_ref[:, here], ctx_ref[:, here], dctx_ref[:, here],
            )
            out_ref[0, :, here] = grad_q
            out_ref[1, :, here] = grad_k
            out_ref[2, :, here] = grad_v
            sums_ref[:, here] = jnp.concatenate(
                [
                    jnp.sum(grad_q.astype(f32), axis=0, keepdims=True),
                    jnp.sum(grad_v.astype(f32), axis=0, keepdims=True),
                    jnp.zeros((6, LANES), f32),
                ],
                axis=0,
            )

    return launch(
        "attend_back", body, (width // wide,), table,
        [(a, block) for a in (q, k, v)]
        + [from_hbm((expos, pl.BlockSpec((4, PACK, PACK), lambda h, *_: (h, pack, 0))))]
        + [(a, block) for a in (inverse, ctx, dctx)],
        [
            (
                jax.ShapeDtypeStruct((3, tokens, width), bf16),
                pl.BlockSpec((3, PACK, wide), lambda h, *_: (0, pack, h)),
            ),
            (
                jax.ShapeDtypeStruct((8 * packs, width), f32),
                pl.BlockSpec((8, wide), lambda h, *_: (pack, h)),
            ),
        ],
        into=into, after=after, mark=True,
    )


def project_grads(table, send, x, grads, sums, after=()):
    tokens = x.shape[0]
    packs = tokens // PACK
    tiles = INNER_A // HALF
    offset = OTHER if send else OWN

    def half_of(t):
        return 1 - t[CORE] if send else t[CORE]

    def tile_of(i, t):
        tile = half_of(t) * tiles + i
        return (tile // 2, 0, tile % 2)

    def body(table, x_ref, d_ref, sa_ref, s2_ref, s1_ref, ff_ref, out_ref):
        step = pl.program_id(0)
        grad = mm_tn(x_ref[...], d_ref[0])
        here = pl.ds(pl.multiple_of(step * HALF, HALF), HALF)
        for chip in range(CHIPS):
            out_ref[table[offset + chip], :, here] = grad[chip * ROWS_A : (chip + 1) * ROWS_A].astype(bf16)

        @pl.when(step == 0)
        def _():
            attended = sum(sa_ref[8 * p : 8 * (p + 1), :] for p in range(packs))
            low = jnp.concatenate([attended[0:2], s1_ref[0:3, :], s2_ref[0:1, :]], axis=0)
            high = jnp.concatenate([s2_ref[1:3, :], ff_ref[0:4, :]], axis=0)
            rows = jnp.where(half_of(table) == 0, low, high)
            rows = jnp.concatenate([rows, jnp.zeros((LANES - 6, D), f32)], axis=0)
            turned = jnp.transpose(rows).astype(bf16)
            for chip in range(CHIPS):
                out_ref[table[offset + chip], :, INNER_A:] = turned[chip * ROWS_A : (chip + 1) * ROWS_A]

    return launch(
        "project_grads", body, (tiles,), table,
        [whole(x), (grads, pl.BlockSpec((1, tokens, HALF), tile_of))] + [whole(a) for a in sums],
        [out_whole((CHIPS, ROWS_A, WIDE_A), bf16)],
        after=after, mark=True,
    )


def token_grads(table, base, grads, w_a, after=()):
    tokens = base.shape[0]

    def body(table, base_ref, d_ref, w_ref, out_ref):
        grad_k = d_ref[1]
        low = jnp.concatenate([d_ref[0], grad_k[:, :HALF]], axis=1)
        high = jnp.concatenate([grad_k[:, HALF:], d_ref[2]], axis=1)
        out_ref[...] = base_ref[...] + mm_nt(low, w_ref[0, :, :INNER_A]) + mm_nt(high, w_ref[1, :, :INNER_A])

    return launch(
        "token_grads", body, (tokens // TILE,), table,
        [from_hbm(rows_of(base)), (grads, pl.BlockSpec((3, TILE, D), lambda i, *_: (0, i, 0)))],
        [in_hbm(out_rows(tokens, D, f32))],
        weights=[w_a], after=after, mark=True,
    )


def lamb(weight, grad, first, second, decay=weight_decay):
    first_new = beta_first * first + (1.0 - beta_first) * grad
    second_new = beta_second * second + (1.0 - beta_second) * grad * grad
    update = (first_new * (1.0 / (1.0 - beta_first**STEP))) / (
        jnp.sqrt(second_new * (1.0 / (1.0 - beta_second**STEP))) + step_eps
    )
    if decay:
        update = update + decay * weight
    return first_new, second_new, update


def square_rows(entries):
    lane = lax.broadcasted_iota(jnp.int32, (1, LANES), 1)
    rows = [jnp.zeros((1, LANES), f32), jnp.zeros((1, LANES), f32)]
    for group, arrays in entries:
        for i, a in enumerate(arrays):
            total = jnp.sum(jnp.sum(a * a, axis=1, keepdims=True), axis=0, keepdims=True)
            rows[i] = rows[i] + jnp.where(lane == group, total, 0.0)
    return jnp.concatenate(rows + [jnp.zeros((6, LANES), f32)], axis=0)


def like(array):
    return out_whole(array.shape, f32)


def step_wide(table, expand, shrink, parts_b, terms_2):
    rows = expand[0].shape[0]

    def body(table, ew, em, ev, sw, sm, sv, mine_ref, came_ref, *refs):
        term_refs = refs[: len(terms_2)]
        em_out, ev_out, eu_out, sm_out, sv_out, su_out, sums_ref = refs[len(terms_2) :]
        mine, came = mine_ref[...], came_ref[...].astype(f32)
        core = table[CORE]
        grad = jnp.concatenate(
            [
                jnp.where(core == 0, mine, came)[:, : FF // 2],
                jnp.where(core == 0, came, mine)[:, : FF // 2],
            ],
            axis=1,
        )
        em_out[...], ev_out[...], step_e = lamb(ew[...], grad, em[...], ev[...])
        eu_out[...] = step_e
        grad = sum(ref[...].astype(f32) for ref in term_refs)
        sm_out[...], sv_out[...], step_s = lamb(sw[...], grad, sm[...], sv[...])
        su_out[...] = step_s
        sums_ref[...] = square_rows([(4, (ew[...], step_e)), (5, (sw[...], step_s))])

    return launch(
        "step_wide", body, (1,), table,
        [whole(a) for a in (*expand, *shrink, *parts_b, *terms_2)],
        [like(expand[0])] * 3 + [like(shrink[0])] * 3 + [out_whole((8, LANES), f32)],

    )


def step_narrow(table, attention, vector, parts_a, parts_b, sums):
    rows = attention[0].shape[1]
    def body(table, aw, am, av, vw, vm, vv, mine_a, came_a, mine_b, came_b, sums_ref, *outs):
        am_out, av_out, au_out, vm_out, vv_out, vu_out, sums_out = outs
        core = table[CORE]

        def halves(mine_ref, came_ref):
            mine, came = mine_ref[...], came_ref[...].astype(f32)
            return jnp.where(core == 0, mine, came), jnp.where(core == 0, came, mine)

        low_a, high_a = halves(mine_a, came_a)
        low_b, high_b = halves(mine_b, came_b)
        grads = [
            low_a[:, :D],
            jnp.concatenate([low_a[:, D:INNER_A], high_a[:, :HALF]], axis=1),
            high_a[:, HALF:INNER_A],
            jnp.concatenate([low_b[:, FF // 2 :], high_b[:, FF // 2 :]], axis=1),
        ]
        entries = []
        for i, grad in enumerate(grads):
            am_out[i], av_out[i], step = lamb(aw[i], grad, am[i], av[i])
            au_out[i] = step
            entries.append((i, (aw[i], step)))
        rest = jnp.zeros((LANES - rows, LANES), f32)
        grad = jnp.concatenate(
            [
                jnp.transpose(jnp.concatenate([part[:, INNER_A:], rest], axis=0))[:6, :rows]
                for part in (low_a, high_a)
            ],
            axis=0,
        )
        vm_out[...], vv_out[...], step = lamb(vw[...], grad, vm[...], vv[...], 0.0)
        vu_out[...] = step
        entries.append((6, (vw[...], step)))
        sums_out[...] = sums_ref[...] + square_rows(entries)

    return launch(
        "step_narrow", body, (1,), table,
        [whole(a) for a in (*attention, *vector, *parts_a, *parts_b, sums)],
        [like(attention[0])] * 3 + [like(vector[0])] * 3 + [out_whole((8, LANES), f32)],

    )


def apply_step(table, sums, masters, steps):
    def body(table, sums_ref, aw, ew, sw, vw, au, eu, su, vu, a_out, e_out, s_out, v_out, ratio_ref, norms_ref):
        master, step = sums_ref[0:1, :], sums_ref[1:2, :]
        ratio = jnp.sqrt(master) * lax.rsqrt(step + 1e-12)
        ratio_ref[...] = ratio[:, :7]
        norms_ref[...] = jnp.sqrt(sums_ref[0:2, :])[:, :7]
        lane = lax.broadcasted_iota(jnp.int32, (1, LANES), 1)

        def of(group):
            return jnp.sum(jnp.where(lane == group, ratio, 0.0), axis=1, keepdims=True) * learn_rate

        for i in range(4):
            a_out[i] = aw[i] - of(i) * au[i]
        e_out[...] = ew[...] - of(4) * eu[...]
        s_out[...] = sw[...] - of(5) * su[...]
        v_out[...] = vw[...] - of(6) * vu[...]

    return launch(
        "apply_step", body, (1,), table,
        [whole(a) for a in (sums, *masters, *steps)],
        [like(a) for a in masters] + [out_whole((1, 7), f32), out_whole((2, 7), f32)],
    )


ACROSS_LAST = ((8, 4, 1, 2), (4, 8, 2, 1))
ALONG_LAST = ((1, 2, 8, 4), (2, 1, 4, 8))


def device_count():
    return lax.axis_size("dp") * lax.axis_size("cand")


def staged():
    return device_count() == 2 * CHIPS


def exchange(a, orders, stage):
    pairs = [(i, i ^ (2 * orders[i % 2][stage])) for i in range(device_count())]
    return lax.ppermute(a, BOTH, pairs)


def swap_core(a):
    return lax.ppermute(a, BOTH, [(i, i ^ 1) for i in range(device_count())])


def layout_table(index, orders):
    plain = jnp.arange(CHIPS, dtype=jnp.int32)
    if not staged():
        return jnp.concatenate([plain, plain, jnp.zeros((1,), jnp.int32), plain, plain])
    core = index % 2
    chip = index // 2

    def by_order(bits):
        position = jnp.zeros((CHIPS,), jnp.int32)
        holder = jnp.zeros((CHIPS,), jnp.int32)
        for stage, bit in enumerate(bits):
            position = position + jnp.where(((plain ^ chip) & bit) != 0, 1 << stage, 0)
            holder = holder + jnp.where((plain & (1 << stage)) != 0, bit, 0)
        return position, holder ^ chip

    parts = [by_order(bits) for bits in orders]
    own = [jnp.where(core == 0, a, b) for a, b in zip(*parts)]
    other = [jnp.where(core == 0, b, a) for a, b in zip(*parts)]
    return jnp.concatenate([own[0], other[0], core[None], own[1], other[1]]).astype(jnp.int32)


class Gathered:
    def __init__(self, table, block, rows, orders, base):
        self.table = table
        self.rows, self.orders, self.base = rows, orders, base
        self.start = block
        self.parts = [(block, 1)]
        self.sent, self.came = [], []
        self.stage = 0
        self.others = []

    def send(self, low, high, *after):
        if self.stage == 0:
            block = behind(self.parts[0][0], *after)
        else:
            block = pick(self.table, self.parts, self.rows, low, high, after)
        came = exchange(block, self.orders, self.stage)
        self.sent.append((block, high - low))
        self.came.append((came, high - low))
        if high == 1 << self.stage:
            self.parts = (self.parts if self.stage < 3 else self.sent) + self.came
            self.sent, self.came = [], []
            self.stage += 1
        return came

    def step(self, *after):
        return self.send(0, 1 << self.stage, *after)

    def swap(self, *after):
        part = self.parts[len(self.others)]
        block = pick(self.table, [part], self.rows, 0, part[1], after) if after else part[0]
        self.others.append(swap_core(block))
        return self.others[-1]

    def blocks(self):
        return Blocks(self.parts, self.others, self.rows, self.base)


class Whole:
    def __init__(self, pieces, rows, base):
        halves = [(a, CHIPS // 2) for a in pieces[:2]]
        self.own = Blocks(halves, pieces[2:], rows, base)
        self.start = pieces[0]

    def send(self, low, high, *after):
        return self.own.pieces[0]

    step = swap = lambda self, *after: self.own.pieces[0]

    def blocks(self):
        return self.own


class Scattered:
    def __init__(self, table, keep, send, orders, after):
        self.table = table
        self.terms = [[(keep, 0)], [(swap_core(behind(send, *after)), 0)]]
        self.orders = orders
        self.stage = 3
        self.came = []
        self.left = 1 << 3

    def send(self, low, high, *after):
        first = 1 << self.stage
        total = self.going = add_blocks(self.table, self.terms, first + low, first + high, after)
        came = exchange(total, self.orders, self.stage)
        self.came.append((came, low))
        self.left -= high - low
        if self.left == 0:
            self.next_stage()
        return came

    def next_stage(self):
        self.terms.append(self.came)
        self.came = []
        self.stage -= 1
        self.left = 1 << max(self.stage, 0)

    def step(self, *after):
        return self.send(0, 1 << self.stage, *after)

    def rest(self):
        return [next(a for a, at in term if at == 0)[0] for term in self.terms]

    def total(self, *after):
        return sum(term.astype(f32) for term in behind(self.rest(), *after))


def by_core(core, low, high):
    return jnp.where(core == 0, low, high)


def own_rows(core, total):
    rows = total.shape[0] // 2
    low, high = total[:rows], total[rows:]
    return by_core(core, low, high), swap_core(by_core(core, high, low).astype(bf16))


def all_sum(row):
    if not staged():
        return lax.psum(row, BOTH)
    for bits in ((1,), (2, 4, 6), (8, 16, 24)):
        came = [
            lax.ppermute(row, BOTH, [(i, i ^ bit) for i in range(device_count())]) for bit in bits
        ]
        row = sum(came, row)
    return row


def gather_weights(table, core, attention, expand, shrink, vector):
    mine, theirs = own_halves(table, attention, expand, vector)
    shrink = shrink.astype(bf16)
    cuts = (0, WIDE_A, WIDE_A + WIDE_B)
    outs = []
    if not staged():
        groups = [(jnp.stack([mine, theirs], axis=1)[:, :, a:b], ROWS_A, 0) for a, b in zip(cuts, cuts[1:])]
        for part, rows, base in groups + [(shrink[:, None], ROWS_B, TABLE)]:
            full = lax.all_gather(part, BOTH, axis=0, tiled=True)
            if rows == ROWS_B:
                full = full.reshape(CHIPS, 2, rows, D).swapaxes(1, 2)
            full = full.reshape(2, CHIPS // 2 * rows, 2, full.shape[-1])
            pieces = [full[high, :, half] for half in (0, 1) for high in (0, 1)]
            outs.append(Whole(pieces, rows, base))
        return outs
    came = swap_core(theirs)
    chip_rows = jnp.concatenate([by_core(core, mine, came), by_core(core, came, mine)], axis=0)
    outs = [Gathered(table, chip_rows[:, a:b], ROWS_A, ACROSS_LAST, 0) for a, b in zip(cuts, cuts[1:])]
    return outs + [Gathered(table, shrink, ROWS_B, ALONG_LAST, TABLE)]


class Reduced:
    def __init__(self, table, core, keep, send, orders, after=()):
        self.core = core
        self.keep, self.other = keep, send
        self.came = keep
        if staged():
            self.work = Scattered(table, keep, send, orders, after)
            self.came = self.work.terms[1][0][0]

    def send(self, low, high, *after):
        if not staged():
            return self.keep, self.keep
        came = self.work.send(low, high, *after)
        return self.work.going, came

    def step(self, *after):
        return self.send(0, 1 << self.work.stage if staged() else 0, *after)

    def halves(self, *after):
        if staged():
            return own_rows(self.core, self.work.total(*after))
        both = jnp.stack([self.keep, self.other], axis=2).reshape(D, 2, self.keep.shape[2]).astype(f32)
        total = lax.psum_scatter(both, BOTH, scatter_dimension=0, tiled=True)
        return total[:, 0], total[:, 1]

    def shard(self):
        if staged():
            return self.work.rest()
        both = jnp.stack([self.keep, self.other], axis=1).reshape(FF, D).astype(f32)
        return [lax.psum_scatter(both, BOTH, scatter_dimension=0, tiled=True)]


def per_device(
    tokens,
    score_vec,
    pair_lengths,
    query_ids,
    labels,
    attention_weight,
    expand_weight,
    shrink_weight,
    vector_weight,
    attention_first,
    expand_first,
    shrink_first,
    vector_first,
    attention_second,
    expand_second,
    shrink_second,
    vector_second,
):
    index = lax.axis_index(BOTH)
    core = index % 2
    ends = jnp.cumsum(pair_lengths, axis=-1, dtype=jnp.int32)
    table = jnp.concatenate(
        [layout_table(index, ACROSS_LAST), layout_table(index, ALONG_LAST), ends.reshape(-1)]
    )
    get_a, get_b, get_2 = gather_weights(
        table,
        core,
        attention_weight,
        expand_weight,
        shrink_weight,
        vector_weight,
    )

    pack_count = pair_lengths.shape[0]
    pairs = pack_count * PAIRS_PACK
    def in_lanes(values, filler):
        row = values.astype(f32).reshape(1, pairs)
        return jnp.pad(row, ((0, 0), (0, LANES - pairs)), constant_values=filler)

    facts = jnp.concatenate(
        [
            jnp.zeros((1, LANES), f32),
            in_lanes(query_ids, -1.0),
            in_lanes(labels, 0.0),
            in_lanes(pair_lengths, 1.0),
            jnp.zeros((4, LANES), f32),
        ],
        axis=0,
    )
    score_row = score_vec.reshape(1, D)

    came_a = get_a.step()
    came_2 = get_2.step(get_a.start)
    came_2 = get_2.step(came_a)
    came_a = get_a.step()
    came_b = get_b.step(came_a)
    came_a_2 = get_a.step(facts)
    came_a = get_a.step(came_b, came_2)
    came_b = get_b.step(came_a_2)
    get_a.swap()
    get_a.swap()
    w_a = get_a.blocks()
    q, k, v, vec, end_q = project(table, tokens, w_a, after=[came_b])
    came_b = get_b.step(came_a)
    *parts, end = attend(table, 0, q, k, v)
    came = [get_2.step(end_q, came_b), get_b.send(0, 4, end_q, came_b)]
    for pack in range(1, pack_count):
        *parts, end_all = attend(table, pack, q, k, v, parts, after=[end])
    ctx, expos, inverse = parts
    came = [get_b.send(4, 8, end, *came), get_2.send(0, 2, end, *came)]
    came += [get_b.swap(), get_b.swap(), get_b.swap()]
    get_b.swap()
    w_b = get_b.blocks()
    n1, r1, first_b, active, slope, end = expand_rows(table, tokens, ctx, w_b, vec)
    get_2.send(2, 8, end_all, *came)
    get_2.swap()
    get_2.swap()
    get_2.swap()
    get_2.swap(end)
    w_2 = get_2.blocks()
    n2, r2, stats = shrink_rows(table, active, w_2, n1, vec, score_row, facts)

    n_cand = lax.axis_size("cand")
    blocks = [stats] + [
        lax.ppermute(stats, "cand", [(i, (i + shift) % n_cand) for i in range(n_cand)])
        for shift in range(1, n_cand)
    ]
    outer, dh2, keep_2, send_2, sums_2, grad_block = shrink_back(
        table, blocks, n2, r2, vec, score_row, active
    )
    put_2 = Reduced(table, core, keep_2, send_2, ALONG_LAST)
    inner, dh1, attn, dctx, sums_1, sums_ff, end = rows_back(table, outer, dh2, slope, n1, r1, w_2, w_b, vec)
    goes, came = put_2.send(6, 8, end)
    send_b, end = expand_grads(table, True, first_b, ctx, inner, attn, after=[goes])
    goes, came_next = put_2.send(4, 6, end, came)
    keep_b, end = expand_grads(table, False, first_b, ctx, inner, attn, after=[end, goes])
    put_b = Reduced(table, core, keep_b, send_b, ACROSS_LAST, after=[came])
    goes, came = zip(put_2.send(0, 4, end, came_next, put_b.came), put_b.send(2, 8, came_next))
    *parts, end = attend_back(table, 0, q, k, v, expos, inverse, ctx, dctx, after=[end, *goes])
    goes, came = zip(
        put_2.step(end, *came),
        put_b.send(0, 2, end, *came),
        put_b.step(end, *came),
    )
    for pack in range(1, pack_count):
        *parts, end = attend_back(
            table, pack, q, k, v, expos, inverse, ctx, dctx, parts, after=[end, *goes]
        )
    grads, sums_attn = parts
    sums = [sums_attn, sums_2, sums_1, sums_ff]
    send_a, end = project_grads(table, True, tokens, grads, sums, after=came)
    keep_a, end = project_grads(table, False, tokens, grads, sums, after=[end])
    put_a = Reduced(table, core, keep_a, send_a, ACROSS_LAST)
    goes, came = zip(put_a.step(), put_b.step(end))
    grad_tokens, end = token_grads(table, dh1, grads, w_a, after=[end, put_a.came, *goes])
    goes, came_a = put_a.step(end)
    put_b.step(end, goes)
    put_2.step(end, goes)
    goes, came_a = put_a.step()
    put_2.step(goes)
    parts_b = put_b.halves(goes)
    put_a.step()
    expand_moment, expand_square, expand_step, shrink_moment, shrink_square, shrink_step, sums = step_wide(
        table,
        (expand_weight, expand_first, expand_second),
        (shrink_weight, shrink_first, shrink_second),
        parts_b,
        put_2.shard(),
    )
    parts_a = put_a.halves()
    (
        attention_moment,
        attention_square,
        attention_step,
        vector_moment,
        vector_square,
        vector_step,
        sums,
    ) = step_narrow(
        table,
        (attention_weight, attention_first, attention_second),
        (vector_weight, vector_first, vector_second),
        parts_a,
        parts_b,
        sums,
    )
    attention_new, expand_new, shrink_new, vector_new, ratios, norms = apply_step(
        table,
        all_sum(sums),
        (attention_weight, expand_weight, shrink_weight, vector_weight),
        (attention_step, expand_step, shrink_step, vector_step),
    )
    return (
        grad_tokens,
        stats[0, :pairs],
        grad_block[0, :pairs],
        ratios.reshape(7),
        norms,
        attention_new,
        expand_new,
        shrink_new,
        vector_new,
        attention_moment,
        expand_moment,
        shrink_moment,
        vector_moment,
        attention_square,
        expand_square,
        shrink_square,
        vector_square,
    )


def solution(mesh):
    placed = (
        P(("dp", "cand"), None),
        P(),
        P(("dp", "cand"), None),
        P(("dp", "cand")),
        P(("dp", "cand")),
        P(None, ("dp", "cand"), None),
        P(("dp", "cand"), None),
        P(("dp", "cand"), None),
        P(None, ("dp", "cand")),
        P(None, ("dp", "cand"), None),
        P(("dp", "cand"), None),
        P(("dp", "cand"), None),
        P(None, ("dp", "cand")),
        P(None, ("dp", "cand"), None),
        P(("dp", "cand"), None),
        P(("dp", "cand"), None),
        P(None, ("dp", "cand")),
    )
    return jax.shard_map(
        per_device,
        mesh=mesh,
        in_specs=placed,
        out_specs=(
            P(("dp", "cand"), None),
            P(("dp", "cand")),
            P(("dp", "cand")),
            P(),
            P(),
            P(None, ("dp", "cand"), None),
            P(("dp", "cand"), None),
            P(("dp", "cand"), None),
            P(None, ("dp", "cand")),
            P(None, ("dp", "cand"), None),
            P(("dp", "cand"), None),
            P(("dp", "cand"), None),
            P(None, ("dp", "cand")),
            P(None, ("dp", "cand"), None),
            P(("dp", "cand"), None),
            P(("dp", "cand"), None),
            P(None, ("dp", "cand")),
        ),
        check_vma=False,
    )
```

```python
import functools

import jax
import jax.numpy as jnp
from jax import lax
from jax.experimental import pallas as pl
from jax.experimental.pallas import tpu as pltpu
from jax.sharding import PartitionSpec as P

D = 768
HEADS = 12
HEAD_DIM = 64
FF = 3072
PACK = 512
PAIRS_PACK = 4
STEP = 10
QUERIES_DEV = 2

norm_eps = 1e-05
beta_first = 0.9
beta_second = 0.999
learn_rate = 1.0
weight_decay = 0.01
step_eps = 1e-06
masked_fill = -1e30

BOTH = ("dp", "cand")
LANES = 128
CHIPS = 16
ROWS_A = D // CHIPS
ROWS_B = FF // CHIPS // 2
HALF = D // 2
INNER_A = D + HALF
WIDE_A = INNER_A + LANES
WIDE_B = FF // 2 + HALF
TILE = 256
MIB = 1 << 20
ROOM = {
    "project": 12,
    "attend": 16,
    "expand_rows": 20,
    "shrink_rows": 14,
    "shrink_back": 25,
    "rows_back": 28,
    "expand_grads": 14,
    "attend_back": 20,
    "project_grads": 16,
    "token_grads": 16,
    "own_halves": 12,
    "pick": 12,
    "add_blocks": 12,
    "step_wide": 12,
    "step_narrow": 12,
    "apply_step": 12,
}
bf16 = jnp.bfloat16
f32 = jnp.float32
B_Q, B_V, B_O, G_1, S_1, B_2, G_2, S_2, B_FF = range(9)
VECTORS = 12
OWN, OTHER, CORE, OWN_CHIP, OTHER_CHIP = 0, CHIPS, 2 * CHIPS, 2 * CHIPS + 1, 3 * CHIPS + 1
TABLE = 4 * CHIPS + 1
ENDS = 2 * TABLE


def mm(a, b):
    return lax.dot_general(a, b, (((1,), (0,)), ((), ())), preferred_element_type=f32)


def mm_nt(a, b):
    return lax.dot_general(a, b, (((1,), (1,)), ((), ())), preferred_element_type=f32)


def mm_tn(a, b):
    return lax.dot_general(a, b, (((0,), (0,)), ((), ())), preferred_element_type=f32)


def row_mean(v):
    return jnp.sum(v, axis=1, keepdims=True) * (1.0 / D)


def norm_parts(hidden):
    center = hidden - row_mean(hidden)
    inverse = lax.rsqrt(row_mean(center * center) + norm_eps)
    return center * inverse, inverse


def segments(table, pack, first_row, rows):
    row = lax.broadcasted_iota(jnp.int32, (rows, LANES), 0) + first_row
    return sum(
        jnp.where(row >= table[ENDS + pack * PAIRS_PACK + i], 1, 0) for i in range(PAIRS_PACK)
    )


def whole(array):
    zeros = (0,) * array.ndim
    return array, pl.BlockSpec(array.shape, lambda *_: zeros, pipeline_mode=pl.Buffered(1))


def rows_of(array, tile=TILE):
    return array, pl.BlockSpec((tile, array.shape[1]), lambda i, *_: (i, 0))


def out_rows(tokens, width, dtype, tile=TILE):
    return jax.ShapeDtypeStruct((tokens, width), dtype), pl.BlockSpec((tile, width), lambda i, *_: (i, 0))


def in_hbm(out):
    shape, spec = out
    return pltpu.HBM(shape.shape, shape.dtype), spec


def in_vmem(out):
    shape, spec = out
    return pltpu.VMEM(shape.shape, shape.dtype), spec


def from_hbm(operand):
    array, spec = operand
    return pltpu.with_memory_space_constraint(array, pltpu.HBM), spec


def out_whole(shape, dtype):
    zeros = (0,) * len(shape)
    return jax.ShapeDtypeStruct(shape, dtype), pl.BlockSpec(shape, lambda *_: zeros)


def behind(a, *others):
    return lax.optimization_barrier((a, *others))[0] if others else a


def launch(name, body, grid, table, operands, outs, scratch=(), weights=(), after=(), into=(), mark=False):
    operands = list(operands)
    count = len(operands)
    outs = list(outs)
    idle = pl.BlockSpec(memory_space=pl.ANY)
    arrays = [a for a, _ in operands]
    specs = [spec for _, spec in operands]
    rooms = []
    for weight in weights:
        arrays += [pltpu.with_memory_space_constraint(a, pltpu.HBM) for a in weight.pieces]
        specs += [idle] * len(weight.pieces)
        rooms += [pltpu.VMEM(weight.shape, bf16), pltpu.SemaphoreType.DMA]
    aliases = {1 + len(arrays) + i: i for i in range(len(into))}
    arrays += list(into) + list(after)
    specs += [idle] * (len(into) + len(after))
    if mark:
        outs.append(out_whole((8, LANES), f32))

    def kernel(table_ref, *refs):
        ins = refs[:count]
        rest = refs[len(arrays) :]
        held = rest[len(outs) + len(scratch) :]
        if weights:

            @pl.when(pl.program_id(0) == 0)
            def _():
                copies, at = [], count
                for i, weight in enumerate(weights):
                    pieces = refs[at : at + len(weight.pieces)]
                    at += len(pieces)
                    copies += weight.copies(table_ref, pieces, held[2 * i], held[2 * i + 1])
                for copy in copies:
                    copy.start()
                for i in range(len(weights)):
                    everything, sem = held[2 * i], held[2 * i + 1]
                    pltpu.make_async_copy(everything, everything, sem).wait()

        own = list(rest[: len(outs) + len(scratch)])
        if mark:
            own.pop(len(outs) - 1)[...] = jnp.zeros((8, LANES), f32)
        body(table_ref, *ins, *held[::2], *own)

    results = pl.pallas_call(
        kernel,
        out_shape=[shape for shape, _ in outs],
        grid_spec=pltpu.PrefetchScalarGridSpec(
            num_scalar_prefetch=1,
            grid=grid,
            in_specs=specs,
            out_specs=[spec for _, spec in outs],
            scratch_shapes=list(scratch) + rooms,
        ),
        input_output_aliases=aliases,
        compiler_params=pltpu.CompilerParams(vmem_limit_bytes=ROOM[name] * MIB),
        name=name,
    )(table, *arrays)
    return results


def own_halves(table, attention, expand, vector):
    rows = attention.shape[1]

    def body(table, a_ref, e_ref, v_ref, mine_ref, theirs_ref):
        core = table[CORE]
        vector = jnp.concatenate([v_ref[...], jnp.zeros((VECTORS, LANES - rows), f32)], axis=1)
        vector = jnp.concatenate([vector, jnp.zeros((LANES - VECTORS, LANES), f32)], axis=0)
        turned = jnp.transpose(vector)[:rows]
        lane = lax.broadcasted_iota(jnp.int32, (rows, LANES), 1)
        turned_high = jnp.concatenate([turned[:, 6:], jnp.zeros((rows, 6), f32)], axis=1)
        q, k, v, o = (a_ref[i] for i in range(4))
        expand = e_ref[...]
        low = [q, k[:, :HALF], jnp.where(lane < 6, turned, 0.0), expand[:, : FF // 2], o[:, :HALF]]
        high = [k[:, HALF:], v, jnp.where(lane < 6, turned_high, 0.0), expand[:, FF // 2 :], o[:, HALF:]]
        low, high = (jnp.concatenate(parts, axis=1) for parts in (low, high))
        mine_ref[...] = jnp.where(core == 0, low, high).astype(bf16)
        theirs_ref[...] = jnp.where(core == 0, high, low).astype(bf16)

    return launch(
        "own_halves", body, (1,), table, [from_hbm(whole(a)) for a in (attention, expand, vector)],
        [out_whole((rows, WIDE_A + WIDE_B), bf16)] * 2,
    )


def pick(table, parts, rows, low, high, after=()):
    width = parts[0][0].shape[1]
    moves, used, at = [], [], 0
    for array, count in parts:
        start, stop = max(low, at), min(high, at + count)
        if start < stop:
            moves.append(((start - at) * rows, (start - low) * rows, (stop - start) * rows))
            used.append(array)
        at += count

    def body(table, *refs):
        for ref, (source, target, size) in zip(refs[:-1], moves):
            refs[-1][target : target + size, :] = ref[source : source + size, :]

    return launch(
        "pick", body, (1,), table, [whole(a) for a in used],
        [out_whole(((high - low) * rows, width), bf16)], after=after,
    )[0]


def add_blocks(table, terms, low, high, after=()):
    operands, cuts = [], []
    for term in terms:
        used = sorted(
            [(at, a) for a, at in term if at < high and low < at + a.shape[0]], key=lambda part: part[0]
        )
        cuts.append([at - low for at, _ in used[1:]])
        for at, array in used:
            last, rows, width = array.shape
            spec = pl.BlockSpec(
                (1, rows, width),
                lambda i, *_, skip=low - at, last=last - 1: (jnp.clip(i + skip, 0, last), 0, 0),
            )
            operands.append((array, spec))

    def body(table, *refs):
        step = pl.program_id(0)
        total, at = 0.0, 0
        for term_cuts in cuts:
            value = refs[at][...].astype(f32)
            at += 1
            for cut in term_cuts:
                value = jnp.where(step >= cut, refs[at][...].astype(f32), value)
                at += 1
            total = total + value
        refs[-1][...] = total.astype(bf16)

    return launch(
        "add_blocks", body, (high - low,), table, operands,
        [
            (
                jax.ShapeDtypeStruct((high - low, rows, width), bf16),
                pl.BlockSpec((1, rows, width), lambda i, *_: (i, 0, 0)),
            )
        ],
        after=after,
    )[0]


class Blocks:
    def __init__(self, own, others, rows, base):
        self.counts = [count for _, count in own]
        self.pieces = [a for a, _ in own] + list(others)
        self.rows = rows
        self.base = base
        width = self.pieces[0].shape[1]
        self.shape = (2 * CHIPS * rows, width) if rows == ROWS_B else (2, CHIPS * rows, width)

    def copies(self, table, refs, whole_ref, sem):
        core = table[CORE]
        out = []
        places = [(piece, at) for piece, count in enumerate(self.counts) for at in range(count)]
        for position, (piece, at) in enumerate(places):
            for which in range(2):
                chip = table[self.base + (OWN_CHIP, OTHER_CHIP)[which] + position]
                half = core if which == 0 else 1 - core
                if self.rows == ROWS_B:
                    at_row = pl.multiple_of((2 * chip + half) * self.rows, self.rows)
                    there = whole_ref.at[pl.ds(at_row, self.rows)]
                else:
                    at_row = pl.multiple_of(chip * self.rows, self.rows)
                    there = whole_ref.at[half, pl.ds(at_row, self.rows)]
                here = refs[which * len(self.counts) + piece].at[pl.ds(at * self.rows, self.rows)]
                out.append(pltpu.make_async_copy(here, there, sem))
        return out


def project(table, x, w_a, after=()):
    tokens = x.shape[0]

    def body(table, x_ref, w_ref, q_ref, k_ref, v_ref, vec_ref):
        @pl.when(pl.program_id(0) == 0)
        def _():
            for half in range(2):
                turned = jnp.transpose(w_ref[half, :, INNER_A:].astype(f32))
                vec_ref[6 * half : 6 * half + 6, :] = turned[:6]

        x = x_ref[...]
        low = mm(x, w_ref[0, :, :INNER_A])
        q_ref[...] = (low[:, :D] + vec_ref[B_Q : B_Q + 1, :]).astype(bf16)
        k_ref[:, :HALF] = low[:, D:].astype(bf16)
        high = mm(x, w_ref[1, :, :INNER_A])
        k_ref[:, HALF:] = high[:, :HALF].astype(bf16)
        v_ref[...] = (high[:, HALF:] + vec_ref[B_V : B_V + 1, :]).astype(bf16)

    return launch(
        "project", body, (tokens // TILE,), table,
        [rows_of(x)], [out_rows(tokens, D, bf16)] * 3 + [out_whole((16, D), f32)],
        weights=[w_a], after=after, mark=True,
    )


def attend(table, pack, q, k, v, into=(), after=()):
    tokens, width = q.shape
    pair_block = pl.BlockSpec((PACK, LANES), lambda h, *_: (pack, h))

    def body(table, q_ref, k_ref, v_ref, ctx_ref, e_ref, inv_ref):
        lane = lax.broadcasted_iota(jnp.int32, (PACK, LANES), 1)
        segment = segments(table, pack, 0, PACK)
        apart = jnp.where((lane < PAIRS_PACK) & (lane != segment), masked_fill, 0.0).astype(bf16)
        belongs = jnp.where(lane == segment, 1.0, 0.0).astype(bf16)
        keys = jnp.concatenate([k_ref[...], belongs], axis=1)
        values = jnp.concatenate([v_ref[...], jnp.ones((PACK, LANES), bf16)], axis=1)
        queries = q_ref[...].astype(f32) * HEAD_DIM ** (-0.5)
        first = lane < HEAD_DIM
        outs = []
        for head in range(2):
            mine = jnp.where(first if head == 0 else ~first, queries, 0.0).astype(bf16)
            logits = mm_nt(jnp.concatenate([mine, apart], axis=1), keys)
            peak = jnp.max(logits, axis=1, keepdims=True)
            expos = jnp.exp(logits - peak).astype(bf16)
            e_ref[head] = expos
            outs.append(mm(expos, values))
        total = jnp.where(first, outs[0][:, LANES:], outs[1][:, LANES:])
        inverse = 1.0 / total
        inv_ref[...] = inverse
        ctx_ref[...] = (jnp.where(first, outs[0][:, :LANES], outs[1][:, :LANES]) * inverse).astype(bf16)

    heads = width // HEAD_DIM
    return launch(
        "attend", body, (heads // 2,), table,
        [(a, pair_block) for a in (q, k, v)],
        [
            (jax.ShapeDtypeStruct((tokens, width), bf16), pair_block),
            in_hbm(
                (
                    jax.ShapeDtypeStruct((heads, tokens, PACK), bf16),
                    pl.BlockSpec((2, PACK, PACK), lambda h, *_: (h, pack, 0)),
                )
            ),
            (jax.ShapeDtypeStruct((tokens, width), f32), pair_block),
        ],
        into=into, after=after, mark=True,
    )


def gelu_parts(v):
    phi = 0.5 + 0.5 * lax.erf(v * 0.7071067811865476)
    return v * phi, phi + v * (jnp.exp(v * v * -0.5) * 0.3989422804014327)


def expand_rows(table, x, ctx, w_b, vec, after=()):
    tokens = x.shape[0]
    step = HALF

    def body(table, x_ref, ctx_ref, vec_ref, w_ref, n1_ref, r1_ref, fb_ref, act_ref, slope_ref):
        ctx = ctx_ref[...]
        attended = jnp.concatenate([mm(ctx, w_ref[half, :, FF // 2 :]) for half in range(2)], axis=1)
        hidden = x_ref[...].astype(f32) + attended + vec_ref[B_O : B_O + 1, :]
        normed, inverse = norm_parts(hidden)
        n1_ref[...] = normed
        r1_ref[...] = jnp.broadcast_to(inverse, (TILE, LANES))
        first_b = (normed * vec_ref[G_1 : G_1 + 1, :] + vec_ref[S_1 : S_1 + 1, :]).astype(bf16)
        fb_ref[...] = first_b
        for j in range(FF // step):
            half, at = divmod(j * step, FF // 2)
            row, column = divmod(j * step, D)
            bias = vec_ref[B_FF + row : B_FF + row + 1, column : column + step]
            active, slope = gelu_parts(mm(first_b, w_ref[half, :, at : at + step]) + bias)
            act_ref[:, j * step : (j + 1) * step] = active.astype(bf16)
            slope_ref[:, j * step : (j + 1) * step] = slope.astype(bf16)

    return launch(
        "expand_rows", body, (tokens // TILE,), table,
        [rows_of(x), rows_of(ctx), whole(vec)],
        [
            in_hbm(out_rows(tokens, D, f32)),
            in_hbm(out_rows(tokens, LANES, f32)),
            in_hbm(out_rows(tokens, D, bf16)),
            in_vmem(out_rows(tokens, FF, bf16)),
            in_hbm(out_rows(tokens, FF, bf16)),
        ],
        weights=[w_b], after=after, mark=True,
    )


def shrink_rows(table, active, w_2, n1, vec, score_vec, facts, after=()):
    tokens = active.shape[0]

    def body(table, act_ref, n1_ref, vec_ref, sv_ref, facts_ref, w_ref, n2_ref, r2_ref, stats_ref):
        step = pl.program_id(0)
        outer = mm(act_ref[...], w_ref[...])
        first_out = n1_ref[...] * vec_ref[G_1 : G_1 + 1, :] + vec_ref[S_1 : S_1 + 1, :]
        normed, inverse = norm_parts(first_out + outer + vec_ref[B_2 : B_2 + 1, :])
        n2_ref[...] = normed
        r2_ref[...] = jnp.broadcast_to(inverse, (TILE, LANES))
        score_vec = sv_ref[...]
        final = normed * vec_ref[G_2 : G_2 + 1, :] + vec_ref[S_2 : S_2 + 1, :]
        row_score = jnp.sum(final * score_vec, axis=1, keepdims=True)
        lane = lax.broadcasted_iota(jnp.int32, (TILE, LANES), 1)
        pack = step // (PACK // TILE)
        segment = segments(table, pack, step % (PACK // TILE) * TILE, TILE)
        here = lane == segment + pack * PAIRS_PACK
        shares = jnp.sum(jnp.where(here, row_score, 0.0), axis=0, keepdims=True)

        @pl.when(step == 0)
        def _():
            stats_ref[...] = facts_ref[...]

        stats_ref[0:1, :] += shares

        @pl.when(step == pl.num_programs(0) - 1)
        def _():
            stats_ref[0:1, :] = stats_ref[0:1, :] / facts_ref[3:4, :]

    return launch(
        "shrink_rows", body, (tokens // TILE,), table,
        [rows_of(active), from_hbm(rows_of(n1)), whole(vec), whole(score_vec), whole(facts)],
        [out_rows(tokens, D, f32), out_rows(tokens, LANES, f32), out_whole((8, LANES), f32)],
        weights=[w_2], after=after,
    )


def loss_parts(blocks):
    own = blocks[0]
    own_ids = own[1:2]
    grads = -own[2:3]
    for query in range(QUERIES_DEV):
        inside = [b[1:2] == float(query) for b in blocks]
        peak = functools.reduce(
            jnp.maximum,
            [jnp.where(i, b[0:1], masked_fill) for i, b in zip(inside, blocks)],
        )
        peak = jnp.max(peak, axis=1, keepdims=True)
        total = sum(jnp.where(i, jnp.exp(jnp.where(i, b[0:1] - peak, 0.0)), 0.0) for i, b in zip(inside, blocks))
        total = jnp.sum(total, axis=1, keepdims=True)
        labels = sum(jnp.where(i, b[2:3], 0.0) for i, b in zip(inside, blocks))
        labels = jnp.sum(labels, axis=1, keepdims=True)
        share = jnp.exp(jnp.where(inside[0], own[0:1] - peak, 0.0)) / total * labels
        grads = grads + jnp.where(own_ids == float(query), share, 0.0)
    return jnp.where(own_ids >= 0.0, grads, 0.0)


def shrink_back(table, blocks, n2, r2, vec, score_vec, active, after=()):
    tokens = n2.shape[0]
    count = len(blocks)

    def body(table, *refs):
        block_refs = refs[:count]
        n2_ref, r2_ref, vec_ref, sv_ref, act_ref = refs[count : count + 5]
        outer_ref, dh_ref, keep_ref, send_ref, sums_ref, grads_ref = refs[count + 5 :]
        step = pl.program_id(0)
        core = table[CORE]

        @pl.when(step == 0)
        def _():
            parts = [b[...] for b in block_refs]
            grads = loss_parts(parts)
            grads_ref[...] = jnp.broadcast_to(grads, (8, LANES))
            per_row = grads / parts[0][3:4]
            score_vec = sv_ref[...]
            weighted = score_vec * vec_ref[G_2 : G_2 + 1, :]
            middle = jnp.mean(weighted, axis=1, keepdims=True)
            lane = lax.broadcasted_iota(jnp.int32, (TILE, LANES), 1)
            bias = jnp.zeros((1, D), f32)
            gain = jnp.zeros((1, D), f32)
            shift = jnp.zeros((1, 1), f32)
            for i in range(tokens // TILE):
                here = pl.ds(i * TILE, TILE)
                pack, first_row = divmod(i * TILE, PACK)
                pair = segments(table, pack, first_row, TILE) + pack * PAIRS_PACK
                scale = jnp.sum(jnp.where(lane == pair, per_row, 0.0), axis=1, keepdims=True)
                normed = n2_ref[here, :]
                along = row_mean(normed * weighted)
                back = (scale * r2_ref[here, :1]) * (weighted - middle - normed * along)
                dh_ref[here, :] = back
                rounded = back.astype(bf16)
                outer_ref[here, :] = rounded
                bias = bias + jnp.sum(rounded.astype(f32), axis=0, keepdims=True)
                gain = gain + jnp.sum(normed * scale, axis=0, keepdims=True)
                shift = shift + jnp.sum(scale, axis=0, keepdims=True)
            sums_ref[...] = jnp.concatenate(
                [bias, gain * score_vec, shift * score_vec, jnp.zeros((5, D), f32)], axis=0
            )

        grad = mm_tn(act_ref[...], outer_ref[...])
        for pair in range(2):
            chip = 2 * step + pair
            at = pair * 2 * ROWS_B
            low = grad[at : at + ROWS_B].astype(bf16)
            high = grad[at + ROWS_B : at + 2 * ROWS_B].astype(bf16)
            keep_ref[table[TABLE + OWN + chip]] = jnp.where(core == 0, low, high)
            send_ref[table[TABLE + OTHER + chip]] = jnp.where(core == 0, high, low)

    return launch(
        "shrink_back", body, (CHIPS // 2,), table,
        [whole(b) for b in blocks]
        + [whole(a) for a in (n2, r2, vec, score_vec)]
        + [(active, pl.BlockSpec((tokens, 4 * ROWS_B), lambda i, *_: (0, i)))],
        [
            out_whole((tokens, D), bf16),
            in_hbm(out_whole((tokens, D), f32)),
            out_whole((CHIPS, ROWS_B, D), bf16),
            out_whole((CHIPS, ROWS_B, D), bf16),
            out_whole((8, D), f32),
            out_whole((8, LANES), f32),
        ],
        after=after,
    )


def rows_back(table, outer, dh2, slope, n1, r1, w_2, w_b, vec, after=()):
    tokens = outer.shape[0]

    def body(
        table, outer_ref, dh_ref, slope_ref, n1_ref, r1_ref, vec_ref, w2_ref, wb_ref,
        inner_ref, dh1_ref, attn_ref, dctx_ref, sums_ref, ff_ref,
    ):
        @pl.when(pl.program_id(0) == 0)
        def _():
            sums_ref[...] = jnp.zeros_like(sums_ref)
            ff_ref[...] = jnp.zeros_like(ff_ref)

        outer = outer_ref[...]
        first = dh_ref[...]
        step = D
        for j in range(FF // step):
            half, at = divmod(j * step, FF // 2)
            here = slice(j * step, (j + 1) * step)
            active = mm_nt(outer, w2_ref[here, :])
            inner = (active * slope_ref[:, here].astype(f32)).astype(bf16)
            inner_ref[:, here] = inner
            ff_ref[j : j + 1, :] += jnp.sum(inner.astype(f32), axis=0, keepdims=True)
            first = first + mm_nt(inner, wb_ref[half, :, at : at + step])
        normed = n1_ref[...]
        dn = first * vec_ref[G_1 : G_1 + 1, :]
        back = r1_ref[:, :1] * (dn - row_mean(dn) - normed * row_mean(dn * normed))
        dh1_ref[...] = back
        rounded = back.astype(bf16)
        attn_ref[...] = rounded
        sums_ref[0:1, :] += jnp.sum(rounded.astype(f32), axis=0, keepdims=True)
        sums_ref[1:2, :] += jnp.sum(first * normed, axis=0, keepdims=True)
        sums_ref[2:3, :] += jnp.sum(first, axis=0, keepdims=True)
        dctx = mm_nt(rounded[:, :HALF], wb_ref[0, :, FF // 2 :]) + mm_nt(
            rounded[:, HALF:], wb_ref[1, :, FF // 2 :]
        )
        dctx_ref[...] = dctx.astype(bf16)

    return launch(
        "rows_back", body, (tokens // TILE,), table,
        [rows_of(outer), from_hbm(rows_of(dh2)), from_hbm(rows_of(slope)), from_hbm(rows_of(n1)), from_hbm(rows_of(r1)), whole(vec)],
        [
            in_vmem(out_rows(tokens, FF, bf16)),
            in_hbm(out_rows(tokens, D, f32)),
            out_rows(tokens, D, bf16),
            out_rows(tokens, D, bf16),
            out_whole((8, D), f32),
            out_whole((8, D), f32),
        ],
        weights=[w_2, w_b], after=after, mark=True,
    )


def expand_grads(table, send, first_b, ctx, inner, attn, after=()):
    tokens = first_b.shape[0]
    tiles = WIDE_B // HALF

    def half_of(t):
        return 1 - t[CORE] if send else t[CORE]

    def body(table, fb_ref, ctx_ref, inner_ref, attn_ref, out_ref):
        step = pl.program_id(0)
        offset = OTHER if send else OWN

        def put(grad):
            for chip in range(CHIPS):
                out_ref[table[offset + chip]] = grad[chip * ROWS_A : (chip + 1) * ROWS_A].astype(bf16)

        @pl.when(step < tiles - 1)
        def _():
            put(mm_tn(fb_ref[...], inner_ref[...]))

        @pl.when(step == tiles - 1)
        def _():
            put(mm_tn(ctx_ref[...], attn_ref[...]))

    return launch(
        "expand_grads", body, (tiles,), table,
        [whole(first_b), whole(ctx)]
        + [
            (
                inner,
                pl.BlockSpec(
                    (tokens, HALF),
                    lambda i, t: (0, half_of(t) * (tiles - 1) + jnp.minimum(i, tiles - 2)),
                ),
            ),
            (attn, pl.BlockSpec((tokens, HALF), lambda i, t: (0, half_of(t)))),
        ],
        [
            (
                jax.ShapeDtypeStruct((CHIPS, ROWS_A, WIDE_B), bf16),
                pl.BlockSpec((CHIPS, ROWS_A, HALF), lambda i, t: (0, 0, i)),
            )
        ],
        after=after, mark=True,
    )


def attend_back(table, pack, q, k, v, expos, inverse, ctx, dctx, into=(), after=()):
    tokens, width = q.shape
    packs = tokens // PACK
    wide = 2 * LANES
    block = pl.BlockSpec((PACK, wide), lambda h, *_: (pack, h))

    def pair(q, k, v, e_ref, first_head, inverse, ctx, dctx):
        lane = lax.broadcasted_iota(jnp.int32, (PACK, LANES), 1)
        first = lane < HEAD_DIM
        scaled = (dctx.astype(f32) * inverse).astype(bf16)
        scaled_f = scaled.astype(f32)
        product = scaled_f * ctx.astype(f32)
        values = jnp.concatenate([v, jnp.where(lane < 3, 1.0, 0.0).astype(bf16)], axis=1)
        parts = []
        for head in range(2):
            mine = first if head == 0 else ~first
            delta = -jnp.sum(jnp.where(mine, product, 0.0), axis=1, keepdims=True)
            delta_1 = delta.astype(bf16).astype(f32)
            delta_2 = (delta - delta_1).astype(bf16).astype(f32)
            delta_3 = delta - delta_1 - delta_2
            minus = jnp.where(
                lane == 0, delta_1, jnp.where(lane == 1, delta_2, jnp.where(lane == 2, delta_3, 0.0))
            )
            left = jnp.concatenate(
                [jnp.where(mine, scaled_f, 0.0).astype(bf16), minus.astype(bf16)], axis=1
            )
            expos = e_ref[first_head + head]
            grad_logits = (expos.astype(f32) * mm_nt(left, values)).astype(bf16)
            parts.append((mm(grad_logits, k), mm_tn(grad_logits, q), mm_tn(expos, scaled)))
        scale = HEAD_DIM ** (-0.5)
        grad_q, grad_k, grad_v = (jnp.where(first, a, b) for a, b in zip(*parts))
        return (grad_q * scale).astype(bf16), (grad_k * scale).astype(bf16), grad_v.astype(bf16)

    def body(table, q_ref, k_ref, v_ref, e_ref, inv_ref, ctx_ref, dctx_ref, out_ref, sums_ref):
        for i in range(2):
            here = slice(i * LANES, (i + 1) * LANES)
            grad_q, grad_k, grad_v = pair(
                q_ref[:, here], k_ref[:, here], v_ref[:, here], e_ref, 2 * i,
                inv_ref[:, here], ctx_ref[:, here], dctx_ref[:, here],
            )
            out_ref[0, :, here] = grad_q
            out_ref[1, :, here] = grad_k
            out_ref[2, :, here] = grad_v
            sums_ref[:, here] = jnp.concatenate(
                [
                    jnp.sum(grad_q.astype(f32), axis=0, keepdims=True),
                    jnp.sum(grad_v.astype(f32), axis=0, keepdims=True),
                    jnp.zeros((6, LANES), f32),
                ],
                axis=0,
            )

    return launch(
        "attend_back", body, (width // wide,), table,
        [(a, block) for a in (q, k, v)]
        + [from_hbm((expos, pl.BlockSpec((4, PACK, PACK), lambda h, *_: (h, pack, 0))))]
        + [(a, block) for a in (inverse, ctx, dctx)],
        [
            (
                jax.ShapeDtypeStruct((3, tokens, width), bf16),
                pl.BlockSpec((3, PACK, wide), lambda h, *_: (0, pack, h)),
            ),
            (
                jax.ShapeDtypeStruct((8 * packs, width), f32),
                pl.BlockSpec((8, wide), lambda h, *_: (pack, h)),
            ),
        ],
        into=into, after=after, mark=True,
    )


def project_grads(table, send, x, grads, sums, after=()):
    tokens = x.shape[0]
    packs = tokens // PACK
    tiles = INNER_A // HALF
    offset = OTHER if send else OWN

    def half_of(t):
        return 1 - t[CORE] if send else t[CORE]

    def tile_of(i, t):
        tile = half_of(t) * tiles + i
        return (tile // 2, 0, tile % 2)

    def body(table, x_ref, d_ref, sa_ref, s2_ref, s1_ref, ff_ref, out_ref):
        step = pl.program_id(0)
        grad = mm_tn(x_ref[...], d_ref[0])
        here = pl.ds(pl.multiple_of(step * HALF, HALF), HALF)
        for chip in range(CHIPS):
            out_ref[table[offset + chip], :, here] = grad[chip * ROWS_A : (chip + 1) * ROWS_A].astype(bf16)

        @pl.when(step == 0)
        def _():
            attended = sum(sa_ref[8 * p : 8 * (p + 1), :] for p in range(packs))
            low = jnp.concatenate([attended[0:2], s1_ref[0:3, :], s2_ref[0:1, :]], axis=0)
            high = jnp.concatenate([s2_ref[1:3, :], ff_ref[0:4, :]], axis=0)
            rows = jnp.where(half_of(table) == 0, low, high)
            rows = jnp.concatenate([rows, jnp.zeros((LANES - 6, D), f32)], axis=0)
            turned = jnp.transpose(rows).astype(bf16)
            for chip in range(CHIPS):
                out_ref[table[offset + chip], :, INNER_A:] = turned[chip * ROWS_A : (chip + 1) * ROWS_A]

    return launch(
        "project_grads", body, (tiles,), table,
        [whole(x), (grads, pl.BlockSpec((1, tokens, HALF), tile_of))] + [whole(a) for a in sums],
        [out_whole((CHIPS, ROWS_A, WIDE_A), bf16)],
        after=after, mark=True,
    )


def token_grads(table, base, grads, w_a, after=()):
    tokens = base.shape[0]

    def body(table, base_ref, d_ref, w_ref, out_ref):
        grad_k = d_ref[1]
        low = jnp.concatenate([d_ref[0], grad_k[:, :HALF]], axis=1)
        high = jnp.concatenate([grad_k[:, HALF:], d_ref[2]], axis=1)
        out_ref[...] = base_ref[...] + mm_nt(low, w_ref[0, :, :INNER_A]) + mm_nt(high, w_ref[1, :, :INNER_A])

    return launch(
        "token_grads", body, (tokens // TILE,), table,
        [from_hbm(rows_of(base)), (grads, pl.BlockSpec((3, TILE, D), lambda i, *_: (0, i, 0)))],
        [in_hbm(out_rows(tokens, D, f32))],
        weights=[w_a], after=after, mark=True,
    )


def lamb(weight, grad, first, second, decay=weight_decay):
    first_new = beta_first * first + (1.0 - beta_first) * grad
    second_new = beta_second * second + (1.0 - beta_second) * grad * grad
    update = (first_new * (1.0 / (1.0 - beta_first**STEP))) / (
        jnp.sqrt(second_new * (1.0 / (1.0 - beta_second**STEP))) + step_eps
    )
    if decay:
        update = update + decay * weight
    return first_new, second_new, update


def square_rows(entries):
    lane = lax.broadcasted_iota(jnp.int32, (1, LANES), 1)
    rows = [jnp.zeros((1, LANES), f32), jnp.zeros((1, LANES), f32)]
    for group, arrays in entries:
        for i, a in enumerate(arrays):
            total = jnp.sum(jnp.sum(a * a, axis=1, keepdims=True), axis=0, keepdims=True)
            rows[i] = rows[i] + jnp.where(lane == group, total, 0.0)
    return jnp.concatenate(rows + [jnp.zeros((6, LANES), f32)], axis=0)


def like(array):
    return out_whole(array.shape, f32)


def step_wide(table, expand, shrink, parts_b, terms_2):
    rows = expand[0].shape[0]

    def body(table, ew, em, ev, sw, sm, sv, mine_ref, came_ref, *refs):
        term_refs = refs[: len(terms_2)]
        em_out, ev_out, eu_out, sm_out, sv_out, su_out, sums_ref = refs[len(terms_2) :]
        mine, came = mine_ref[...], came_ref[...].astype(f32)
        core = table[CORE]
        grad = jnp.concatenate(
            [
                jnp.where(core == 0, mine, came)[:, : FF // 2],
                jnp.where(core == 0, came, mine)[:, : FF // 2],
            ],
            axis=1,
        )
        em_out[...], ev_out[...], step_e = lamb(ew[...], grad, em[...], ev[...])
        eu_out[...] = step_e
        grad = sum(ref[...].astype(f32) for ref in term_refs)
        sm_out[...], sv_out[...], step_s = lamb(sw[...], grad, sm[...], sv[...])
        su_out[...] = step_s
        sums_ref[...] = square_rows([(4, (ew[...], step_e)), (5, (sw[...], step_s))])

    return launch(
        "step_wide", body, (1,), table,
        [whole(a) for a in (*expand, *shrink, *parts_b, *terms_2)],
        [like(expand[0])] * 3 + [like(shrink[0])] * 3 + [out_whole((8, LANES), f32)],

    )


def step_narrow(table, attention, vector, parts_a, parts_b, sums):
    rows = attention[0].shape[1]
    def body(table, aw, am, av, vw, vm, vv, mine_a, came_a, mine_b, came_b, sums_ref, *outs):
        am_out, av_out, au_out, vm_out, vv_out, vu_out, sums_out = outs
        core = table[CORE]

        def halves(mine_ref, came_ref):
            mine, came = mine_ref[...], came_ref[...].astype(f32)
            return jnp.where(core == 0, mine, came), jnp.where(core == 0, came, mine)

        low_a, high_a = halves(mine_a, came_a)
        low_b, high_b = halves(mine_b, came_b)
        grads = [
            low_a[:, :D],
            jnp.concatenate([low_a[:, D:INNER_A], high_a[:, :HALF]], axis=1),
            high_a[:, HALF:INNER_A],
            jnp.concatenate([low_b[:, FF // 2 :], high_b[:, FF // 2 :]], axis=1),
        ]
        entries = []
        for i, grad in enumerate(grads):
            am_out[i], av_out[i], step = lamb(aw[i], grad, am[i], av[i])
            au_out[i] = step
            entries.append((i, (aw[i], step)))
        rest = jnp.zeros((LANES - rows, LANES), f32)
        grad = jnp.concatenate(
            [
                jnp.transpose(jnp.concatenate([part[:, INNER_A:], rest], axis=0))[:6, :rows]
                for part in (low_a, high_a)
            ],
            axis=0,
        )
        vm_out[...], vv_out[...], step = lamb(vw[...], grad, vm[...], vv[...], 0.0)
        vu_out[...] = step
        entries.append((6, (vw[...], step)))
        sums_out[...] = sums_ref[...] + square_rows(entries)

    return launch(
        "step_narrow", body, (1,), table,
        [whole(a) for a in (*attention, *vector, *parts_a, *parts_b, sums)],
        [like(attention[0])] * 3 + [like(vector[0])] * 3 + [out_whole((8, LANES), f32)],

    )


def apply_step(table, sums, masters, steps):
    def body(table, sums_ref, aw, ew, sw, vw, au, eu, su, vu, a_out, e_out, s_out, v_out, ratio_ref, norms_ref):
        master, step = sums_ref[0:1, :], sums_ref[1:2, :]
        ratio = jnp.sqrt(master) * lax.rsqrt(step + 1e-12)
        ratio_ref[...] = ratio[:, :7]
        norms_ref[...] = jnp.sqrt(sums_ref[0:2, :])[:, :7]
        lane = lax.broadcasted_iota(jnp.int32, (1, LANES), 1)

        def of(group):
            return jnp.sum(jnp.where(lane == group, ratio, 0.0), axis=1, keepdims=True) * learn_rate

        for i in range(4):
            a_out[i] = aw[i] - of(i) * au[i]
        e_out[...] = ew[...] - of(4) * eu[...]
        s_out[...] = sw[...] - of(5) * su[...]
        v_out[...] = vw[...] - of(6) * vu[...]

    return launch(
        "apply_step", body, (1,), table,
        [whole(a) for a in (sums, *masters, *steps)],
        [like(a) for a in masters] + [out_whole((1, 7), f32), out_whole((2, 7), f32)],
    )


ACROSS_LAST = ((8, 4, 1, 2), (4, 8, 2, 1))
ALONG_LAST = ((1, 2, 8, 4), (2, 1, 4, 8))


def device_count():
    return lax.axis_size("dp") * lax.axis_size("cand")


def staged():
    return device_count() == 2 * CHIPS


def exchange(a, orders, stage):
    pairs = [(i, i ^ (2 * orders[i % 2][stage])) for i in range(device_count())]
    return lax.ppermute(a, BOTH, pairs)


def swap_core(a):
    return lax.ppermute(a, BOTH, [(i, i ^ 1) for i in range(device_count())])


def layout_table(index, orders):
    plain = jnp.arange(CHIPS, dtype=jnp.int32)
    if not staged():
        return jnp.concatenate([plain, plain, jnp.zeros((1,), jnp.int32), plain, plain])
    core = index % 2
    chip = index // 2

    def by_order(bits):
        position = jnp.zeros((CHIPS,), jnp.int32)
        holder = jnp.zeros((CHIPS,), jnp.int32)
        for stage, bit in enumerate(bits):
            position = position + jnp.where(((plain ^ chip) & bit) != 0, 1 << stage, 0)
            holder = holder + jnp.where((plain & (1 << stage)) != 0, bit, 0)
        return position, holder ^ chip

    parts = [by_order(bits) for bits in orders]
    own = [jnp.where(core == 0, a, b) for a, b in zip(*parts)]
    other = [jnp.where(core == 0, b, a) for a, b in zip(*parts)]
    return jnp.concatenate([own[0], other[0], core[None], own[1], other[1]]).astype(jnp.int32)


class Gathered:
    def __init__(self, table, block, rows, orders, base):
        self.table = table
        self.rows, self.orders, self.base = rows, orders, base
        self.start = block
        self.parts = [(block, 1)]
        self.sent, self.came = [], []
        self.stage = 0
        self.others = []

    def send(self, low, high, *after):
        if self.stage == 0:
            block = behind(self.parts[0][0], *after)
        else:
            block = pick(self.table, self.parts, self.rows, low, high, after)
        came = exchange(block, self.orders, self.stage)
        self.sent.append((block, high - low))
        self.came.append((came, high - low))
        if high == 1 << self.stage:
            self.parts = (self.parts if self.stage < 3 else self.sent) + self.came
            self.sent, self.came = [], []
            self.stage += 1
        return came

    def step(self, *after):
        return self.send(0, 1 << self.stage, *after)

    def swap(self, *after):
        part = self.parts[len(self.others)]
        block = pick(self.table, [part], self.rows, 0, part[1], after) if after else part[0]
        self.others.append(swap_core(block))
        return self.others[-1]

    def blocks(self):
        return Blocks(self.parts, self.others, self.rows, self.base)


class Whole:
    def __init__(self, pieces, rows, base):
        halves = [(a, CHIPS // 2) for a in pieces[:2]]
        self.own = Blocks(halves, pieces[2:], rows, base)
        self.start = pieces[0]

    def send(self, low, high, *after):
        return self.own.pieces[0]

    step = swap = lambda self, *after: self.own.pieces[0]

    def blocks(self):
        return self.own


class Scattered:
    def __init__(self, table, keep, send, orders, after):
        self.table = table
        self.terms = [[(keep, 0)], [(swap_core(behind(send, *after)), 0)]]
        self.orders = orders
        self.stage = 3
        self.came = []
        self.left = 1 << 3

    def send(self, low, high, *after):
        first = 1 << self.stage
        total = self.going = add_blocks(self.table, self.terms, first + low, first + high, after)
        came = exchange(total, self.orders, self.stage)
        self.came.append((came, low))
        self.left -= high - low
        if self.left == 0:
            self.next_stage()
        return came

    def next_stage(self):
        self.terms.append(self.came)
        self.came = []
        self.stage -= 1
        self.left = 1 << max(self.stage, 0)

    def step(self, *after):
        return self.send(0, 1 << self.stage, *after)

    def rest(self):
        return [next(a for a, at in term if at == 0)[0] for term in self.terms]

    def total(self, *after):
        return sum(term.astype(f32) for term in behind(self.rest(), *after))


def by_core(core, low, high):
    return jnp.where(core == 0, low, high)


def own_rows(core, total):
    rows = total.shape[0] // 2
    low, high = total[:rows], total[rows:]
    return by_core(core, low, high), swap_core(by_core(core, high, low).astype(bf16))


def all_sum(row):
    if not staged():
        return lax.psum(row, BOTH)
    for bits in ((1,), (2, 4, 6), (8, 16, 24)):
        came = [
            lax.ppermute(row, BOTH, [(i, i ^ bit) for i in range(device_count())]) for bit in bits
        ]
        row = sum(came, row)
    return row


def gather_weights(places, table, core, attention, expand, shrink, vector):
    mine, theirs = own_halves(places, attention, expand, vector)
    shrink = shrink.astype(bf16)
    cuts = (0, WIDE_A, WIDE_A + WIDE_B)
    outs = []
    if not staged():
        groups = [(jnp.stack([mine, theirs], axis=1)[:, :, a:b], ROWS_A, 0) for a, b in zip(cuts, cuts[1:])]
        for part, rows, base in groups + [(shrink[:, None], ROWS_B, TABLE)]:
            full = lax.all_gather(part, BOTH, axis=0, tiled=True)
            if rows == ROWS_B:
                full = full.reshape(CHIPS, 2, rows, D).swapaxes(1, 2)
            full = full.reshape(2, CHIPS // 2 * rows, 2, full.shape[-1])
            pieces = [full[high, :, half] for half in (0, 1) for high in (0, 1)]
            outs.append(Whole(pieces, rows, base))
        return outs
    came = swap_core(theirs)
    chip_rows = jnp.concatenate([by_core(core, mine, came), by_core(core, came, mine)], axis=0)
    outs = [Gathered(table, chip_rows[:, a:b], ROWS_A, ACROSS_LAST, 0) for a, b in zip(cuts, cuts[1:])]
    return outs + [Gathered(table, shrink, ROWS_B, ALONG_LAST, TABLE)]


class Reduced:
    def __init__(self, table, core, keep, send, orders, after=()):
        self.core = core
        self.keep, self.other = keep, send
        self.came = keep
        if staged():
            self.work = Scattered(table, keep, send, orders, after)
            self.came = self.work.terms[1][0][0]

    def send(self, low, high, *after):
        if not staged():
            return self.keep, self.keep
        came = self.work.send(low, high, *after)
        return self.work.going, came

    def step(self, *after):
        return self.send(0, 1 << self.work.stage if staged() else 0, *after)

    def halves(self, *after):
        if staged():
            return own_rows(self.core, self.work.total(*after))
        both = jnp.stack([self.keep, self.other], axis=2).reshape(D, 2, self.keep.shape[2]).astype(f32)
        total = lax.psum_scatter(both, BOTH, scatter_dimension=0, tiled=True)
        return total[:, 0], total[:, 1]

    def shard(self):
        if staged():
            return self.work.rest()
        both = jnp.stack([self.keep, self.other], axis=1).reshape(FF, D).astype(f32)
        return [lax.psum_scatter(both, BOTH, scatter_dimension=0, tiled=True)]


def per_device(
    tokens,
    score_vec,
    pair_lengths,
    query_ids,
    labels,
    attention_weight,
    expand_weight,
    shrink_weight,
    vector_weight,
    attention_first,
    expand_first,
    shrink_first,
    vector_first,
    attention_second,
    expand_second,
    shrink_second,
    vector_second,
):
    index = lax.axis_index(BOTH)
    core = index % 2
    ends = jnp.cumsum(pair_lengths, axis=-1, dtype=jnp.int32)
    places = jnp.concatenate([layout_table(index, ACROSS_LAST), layout_table(index, ALONG_LAST)])
    table = jnp.concatenate([places, ends.reshape(-1)])
    get_a, get_b, get_2 = gather_weights(
        places,
        table,
        core,
        attention_weight,
        expand_weight,
        shrink_weight,
        vector_weight,
    )

    pack_count = pair_lengths.shape[0]
    pairs = pack_count * PAIRS_PACK
    def in_lanes(values, filler):
        row = values.astype(f32).reshape(1, pairs)
        return jnp.pad(row, ((0, 0), (0, LANES - pairs)), constant_values=filler)

    facts = jnp.concatenate(
        [
            jnp.zeros((1, LANES), f32),
            in_lanes(query_ids, -1.0),
            in_lanes(labels, 0.0),
            in_lanes(pair_lengths, 1.0),
            jnp.zeros((4, LANES), f32),
        ],
        axis=0,
    )
    score_row = score_vec.reshape(1, D)

    came_a = get_a.step()
    came_2 = get_2.step(get_a.start)
    came_2 = get_2.step(came_a)
    came_a = get_a.step()
    came_b = get_b.step(came_a)
    came_a_2 = get_a.step(facts)
    came_a = get_a.step(came_b, came_2)
    came_b = get_b.step(came_a_2)
    get_a.swap()
    get_a.swap()
    w_a = get_a.blocks()
    q, k, v, vec, end_q = project(table, tokens, w_a, after=[came_b])
    came_b = get_b.step(came_a)
    *parts, end = attend(table, 0, q, k, v)
    came = [get_2.step(end_q, came_b), get_b.send(0, 4, end_q, came_b)]
    for pack in range(1, pack_count):
        *parts, end_all = attend(table, pack, q, k, v, parts, after=[end])
    ctx, expos, inverse = parts
    came = [get_b.send(4, 8, end, *came), get_2.send(0, 2, end, *came)]
    came += [get_b.swap(), get_b.swap(), get_b.swap()]
    get_b.swap()
    w_b = get_b.blocks()
    n1, r1, first_b, active, slope, end = expand_rows(table, tokens, ctx, w_b, vec)
    get_2.send(2, 8, end_all, *came)
    get_2.swap()
    get_2.swap()
    get_2.swap()
    get_2.swap(end)
    w_2 = get_2.blocks()
    n2, r2, stats = shrink_rows(table, active, w_2, n1, vec, score_row, facts)

    n_cand = lax.axis_size("cand")
    blocks = [stats] + [
        lax.ppermute(stats, "cand", [(i, (i + shift) % n_cand) for i in range(n_cand)])
        for shift in range(1, n_cand)
    ]
    outer, dh2, keep_2, send_2, sums_2, grad_block = shrink_back(
        table, blocks, n2, r2, vec, score_row, active
    )
    put_2 = Reduced(table, core, keep_2, send_2, ALONG_LAST)
    inner, dh1, attn, dctx, sums_1, sums_ff, end = rows_back(table, outer, dh2, slope, n1, r1, w_2, w_b, vec)
    goes, came = put_2.send(6, 8, end)
    send_b, end = expand_grads(table, True, first_b, ctx, inner, attn, after=[goes])
    goes, came_next = put_2.send(4, 6, end, came)
    keep_b, end = expand_grads(table, False, first_b, ctx, inner, attn, after=[end, goes])
    put_b = Reduced(table, core, keep_b, send_b, ACROSS_LAST, after=[came])
    goes, came = zip(put_2.send(0, 4, end, came_next, put_b.came), put_b.send(2, 8, came_next))
    *parts, end = attend_back(table, 0, q, k, v, expos, inverse, ctx, dctx, after=[end, *goes])
    goes, came = zip(
        put_2.step(end, *came),
        put_b.send(0, 2, end, *came),
        put_b.step(end, *came),
    )
    for pack in range(1, pack_count):
        *parts, end = attend_back(
            table, pack, q, k, v, expos, inverse, ctx, dctx, parts, after=[end, *goes]
        )
    grads, sums_attn = parts
    sums = [sums_attn, sums_2, sums_1, sums_ff]
    send_a, end = project_grads(table, True, tokens, grads, sums, after=came)
    keep_a, end = project_grads(table, False, tokens, grads, sums, after=[end])
    put_a = Reduced(table, core, keep_a, send_a, ACROSS_LAST)
    goes, came = zip(put_a.step(), put_b.step(end))
    grad_tokens, end = token_grads(table, dh1, grads, w_a, after=[end, put_a.came, *goes])
    goes, came_a = put_a.step(end)
    put_b.step(end, goes)
    put_2.step(end, goes)
    goes, came_a = put_a.step()
    put_2.step(goes)
    parts_b = put_b.halves(goes)
    put_a.step()
    expand_moment, expand_square, expand_step, shrink_moment, shrink_square, shrink_step, sums = step_wide(
        table,
        (expand_weight, expand_first, expand_second),
        (shrink_weight, shrink_first, shrink_second),
        parts_b,
        put_2.shard(),
    )
    parts_a = put_a.halves()
    (
        attention_moment,
        attention_square,
        attention_step,
        vector_moment,
        vector_square,
        vector_step,
        sums,
    ) = step_narrow(
        table,
        (attention_weight, attention_first, attention_second),
        (vector_weight, vector_first, vector_second),
        parts_a,
        parts_b,
        sums,
    )
    attention_new, expand_new, shrink_new, vector_new, ratios, norms = apply_step(
        table,
        all_sum(sums),
        (attention_weight, expand_weight, shrink_weight, vector_weight),
        (attention_step, expand_step, shrink_step, vector_step),
    )
    return (
        grad_tokens,
        stats[0, :pairs],
        grad_block[0, :pairs],
        ratios.reshape(7),
        norms,
        attention_new,
        expand_new,
        shrink_new,
        vector_new,
        attention_moment,
        expand_moment,
        shrink_moment,
        vector_moment,
        attention_square,
        expand_square,
        shrink_square,
        vector_square,
    )


def solution(mesh):
    placed = (
        P(("dp", "cand"), None),
        P(),
        P(("dp", "cand"), None),
        P(("dp", "cand")),
        P(("dp", "cand")),
        P(None, ("dp", "cand"), None),
        P(("dp", "cand"), None),
        P(("dp", "cand"), None),
        P(None, ("dp", "cand")),
        P(None, ("dp", "cand"), None),
        P(("dp", "cand"), None),
        P(("dp", "cand"), None),
        P(None, ("dp", "cand")),
        P(None, ("dp", "cand"), None),
        P(("dp", "cand"), None),
        P(("dp", "cand"), None),
        P(None, ("dp", "cand")),
    )
    return jax.shard_map(
        per_device,
        mesh=mesh,
        in_specs=placed,
        out_specs=(
            P(("dp", "cand"), None),
            P(("dp", "cand")),
            P(("dp", "cand")),
            P(),
            P(),
            P(None, ("dp", "cand"), None),
            P(("dp", "cand"), None),
            P(("dp", "cand"), None),
            P(None, ("dp", "cand")),
            P(None, ("dp", "cand"), None),
            P(("dp", "cand"), None),
            P(("dp", "cand"), None),
            P(None, ("dp", "cand")),
            P(None, ("dp", "cand"), None),
            P(("dp", "cand"), None),
            P(("dp", "cand"), None),
            P(None, ("dp", "cand")),
        ),
        check_vma=False,
    )
```

```python
import functools

import jax
import jax.numpy as jnp
from jax import lax
from jax.experimental import pallas as pl
from jax.experimental.pallas import tpu as pltpu
from jax.sharding import PartitionSpec as P

D = 768
HEADS = 12
HEAD_DIM = 64
FF = 3072
PACK = 512
PAIRS_PACK = 4
STEP = 10
QUERIES_DEV = 2

norm_eps = 1e-05
beta_first = 0.9
beta_second = 0.999
learn_rate = 1.0
weight_decay = 0.01
step_eps = 1e-06
masked_fill = -1e30

BOTH = ("dp", "cand")
LANES = 128
CHIPS = 16
ROWS_A = D // CHIPS
ROWS_B = FF // CHIPS // 2
HALF = D // 2
INNER_A = D + HALF
WIDE_A = INNER_A + LANES
WIDE_B = FF // 2 + HALF
TILE = 256
MIB = 1 << 20
ROOM = {
    "project": 12,
    "attend": 16,
    "expand_rows": 20,
    "shrink_rows": 14,
    "shrink_back": 25,
    "rows_back": 28,
    "expand_grads": 14,
    "attend_back": 20,
    "project_grads": 16,
    "token_grads": 16,
    "own_halves": 12,
    "pick": 12,
    "add_blocks": 12,
    "step_wide": 12,
    "step_narrow": 12,
    "apply_step": 12,
}
bf16 = jnp.bfloat16
f32 = jnp.float32
B_Q, B_V, B_O, G_1, S_1, B_2, G_2, S_2, B_FF = range(9)
VECTORS = 12
OWN, OTHER, CORE, OWN_CHIP, OTHER_CHIP = 0, CHIPS, 2 * CHIPS, 2 * CHIPS + 1, 3 * CHIPS + 1
TABLE = 4 * CHIPS + 1
ENDS = 2 * TABLE


def mm(a, b):
    return lax.dot_general(a, b, (((1,), (0,)), ((), ())), preferred_element_type=f32)


def mm_nt(a, b):
    return lax.dot_general(a, b, (((1,), (1,)), ((), ())), preferred_element_type=f32)


def mm_tn(a, b):
    return lax.dot_general(a, b, (((0,), (0,)), ((), ())), preferred_element_type=f32)


def row_mean(v):
    return jnp.sum(v, axis=1, keepdims=True) * (1.0 / D)


def norm_parts(hidden):
    center = hidden - row_mean(hidden)
    inverse = lax.rsqrt(row_mean(center * center) + norm_eps)
    return center * inverse, inverse


def segments(table, pack, first_row, rows):
    row = lax.broadcasted_iota(jnp.int32, (rows, LANES), 0) + first_row
    return sum(
        jnp.where(row >= table[ENDS + pack * PAIRS_PACK + i], 1, 0) for i in range(PAIRS_PACK)
    )


def whole(array):
    zeros = (0,) * array.ndim
    return array, pl.BlockSpec(array.shape, lambda *_: zeros, pipeline_mode=pl.Buffered(1))


def rows_of(array, tile=TILE):
    return array, pl.BlockSpec((tile, array.shape[1]), lambda i, *_: (i, 0))


def out_rows(tokens, width, dtype, tile=TILE):
    return jax.ShapeDtypeStruct((tokens, width), dtype), pl.BlockSpec((tile, width), lambda i, *_: (i, 0))


def in_hbm(out):
    shape, spec = out
    return pltpu.HBM(shape.shape, shape.dtype), spec


def in_vmem(out):
    shape, spec = out
    return pltpu.VMEM(shape.shape, shape.dtype), spec


def from_hbm(operand):
    array, spec = operand
    return pltpu.with_memory_space_constraint(array, pltpu.HBM), spec


def out_whole(shape, dtype):
    zeros = (0,) * len(shape)
    return jax.ShapeDtypeStruct(shape, dtype), pl.BlockSpec(shape, lambda *_: zeros)


def behind(a, *others):
    return lax.optimization_barrier((a, *others))[0] if others else a


def launch(name, body, grid, table, operands, outs, scratch=(), weights=(), after=(), into=(), mark=False):
    operands = list(operands)
    count = len(operands)
    outs = list(outs)
    idle = pl.BlockSpec(memory_space=pl.ANY)
    arrays = [a for a, _ in operands]
    specs = [spec for _, spec in operands]
    rooms = []
    for weight in weights:
        arrays += [pltpu.with_memory_space_constraint(a, pltpu.HBM) for a in weight.pieces]
        specs += [idle] * len(weight.pieces)
        rooms += [pltpu.VMEM(weight.shape, bf16), pltpu.SemaphoreType.DMA]
    aliases = {1 + len(arrays) + i: i for i in range(len(into))}
    arrays += list(into) + list(after)
    specs += [idle] * (len(into) + len(after))
    if mark:
        outs.append(out_whole((8, LANES), f32))

    def kernel(table_ref, *refs):
        ins = refs[:count]
        rest = refs[len(arrays) :]
        held = rest[len(outs) + len(scratch) :]
        if weights:

            @pl.when(pl.program_id(0) == 0)
            def _():
                copies, at = [], count
                for i, weight in enumerate(weights):
                    pieces = refs[at : at + len(weight.pieces)]
                    at += len(pieces)
                    copies += weight.copies(table_ref, pieces, held[2 * i], held[2 * i + 1])
                for copy in copies:
                    copy.start()
                for i in range(len(weights)):
                    everything, sem = held[2 * i], held[2 * i + 1]
                    pltpu.make_async_copy(everything, everything, sem).wait()

        own = list(rest[: len(outs) + len(scratch)])
        if mark:
            own.pop(len(outs) - 1)[...] = jnp.zeros((8, LANES), f32)
        body(table_ref, *ins, *held[::2], *own)

    results = pl.pallas_call(
        kernel,
        out_shape=[shape for shape, _ in outs],
        grid_spec=pltpu.PrefetchScalarGridSpec(
            num_scalar_prefetch=1,
            grid=grid,
            in_specs=specs,
            out_specs=[spec for _, spec in outs],
            scratch_shapes=list(scratch) + rooms,
        ),
        input_output_aliases=aliases,
        compiler_params=pltpu.CompilerParams(vmem_limit_bytes=ROOM[name] * MIB),
        name=name,
    )(table, *arrays)
    return results


def own_halves(table, attention, expand, vector):
    rows = attention.shape[1]

    def body(table, a_ref, e_ref, v_ref, mine_ref, theirs_ref):
        core = table[CORE]
        vector = jnp.concatenate([v_ref[...], jnp.zeros((VECTORS, LANES - rows), f32)], axis=1)
        vector = jnp.concatenate([vector, jnp.zeros((LANES - VECTORS, LANES), f32)], axis=0)
        turned = jnp.transpose(vector)[:rows]
        lane = lax.broadcasted_iota(jnp.int32, (rows, LANES), 1)
        turned_high = jnp.concatenate([turned[:, 6:], jnp.zeros((rows, 6), f32)], axis=1)
        q, k, v, o = (a_ref[i] for i in range(4))
        expand = e_ref[...]
        low = [q, k[:, :HALF], jnp.where(lane < 6, turned, 0.0), expand[:, : FF // 2], o[:, :HALF]]
        high = [k[:, HALF:], v, jnp.where(lane < 6, turned_high, 0.0), expand[:, FF // 2 :], o[:, HALF:]]
        low, high = (jnp.concatenate(parts, axis=1) for parts in (low, high))
        mine_ref[...] = jnp.where(core == 0, low, high).astype(bf16)
        theirs_ref[...] = jnp.where(core == 0, high, low).astype(bf16)

    return launch(
        "own_halves", body, (1,), table, [from_hbm(whole(a)) for a in (attention, expand, vector)],
        [out_whole((rows, WIDE_A + WIDE_B), bf16)] * 2,
    )


def pick(table, parts, rows, low, high, after=()):
    width = parts[0][0].shape[1]
    moves, used, at = [], [], 0
    for array, count in parts:
        start, stop = max(low, at), min(high, at + count)
        if start < stop:
            moves.append(((start - at) * rows, (start - low) * rows, (stop - start) * rows))
            used.append(array)
        at += count

    def body(table, *refs):
        for ref, (source, target, size) in zip(refs[:-1], moves):
            refs[-1][target : target + size, :] = ref[source : source + size, :]

    return launch(
        "pick", body, (1,), table, [whole(a) for a in used],
        [out_whole(((high - low) * rows, width), bf16)], after=after,
    )[0]


def add_blocks(table, terms, low, high, after=()):
    operands, cuts = [], []
    for term in terms:
        used = sorted(
            [(at, a) for a, at in term if at < high and low < at + a.shape[0]], key=lambda part: part[0]
        )
        cuts.append([at - low for at, _ in used[1:]])
        for at, array in used:
            last, rows, width = array.shape
            spec = pl.BlockSpec(
                (1, rows, width),
                lambda i, *_, skip=low - at, last=last - 1: (jnp.clip(i + skip, 0, last), 0, 0),
            )
            operands.append((array, spec))

    def body(table, *refs):
        step = pl.program_id(0)
        total, at = 0.0, 0
        for term_cuts in cuts:
            value = refs[at][...].astype(f32)
            at += 1
            for cut in term_cuts:
                value = jnp.where(step >= cut, refs[at][...].astype(f32), value)
                at += 1
            total = total + value
        refs[-1][...] = total.astype(bf16)

    return launch(
        "add_blocks", body, (high - low,), table, operands,
        [
            (
                jax.ShapeDtypeStruct((high - low, rows, width), bf16),
                pl.BlockSpec((1, rows, width), lambda i, *_: (i, 0, 0)),
            )
        ],
        after=after,
    )[0]


class Blocks:
    def __init__(self, own, others, rows, base):
        self.counts = [count for _, count in own]
        self.pieces = [a for a, _ in own] + list(others)
        self.rows = rows
        self.base = base
        width = self.pieces[0].shape[1]
        self.shape = (2 * CHIPS * rows, width) if rows == ROWS_B else (2, CHIPS * rows, width)

    def copies(self, table, refs, whole_ref, sem):
        core = table[CORE]
        out = []
        places = [(piece, at) for piece, count in enumerate(self.counts) for at in range(count)]
        for position, (piece, at) in enumerate(places):
            for which in range(2):
                chip = table[self.base + (OWN_CHIP, OTHER_CHIP)[which] + position]
                half = core if which == 0 else 1 - core
                if self.rows == ROWS_B:
                    at_row = pl.multiple_of((2 * chip + half) * self.rows, self.rows)
                    there = whole_ref.at[pl.ds(at_row, self.rows)]
                else:
                    at_row = pl.multiple_of(chip * self.rows, self.rows)
                    there = whole_ref.at[half, pl.ds(at_row, self.rows)]
                here = refs[which * len(self.counts) + piece].at[pl.ds(at * self.rows, self.rows)]
                out.append(pltpu.make_async_copy(here, there, sem))
        return out


def project(table, x, w_a, after=()):
    tokens = x.shape[0]

    def body(table, x_ref, w_ref, q_ref, k_ref, v_ref, vec_ref):
        @pl.when(pl.program_id(0) == 0)
        def _():
            for half in range(2):
                turned = jnp.transpose(w_ref[half, :, INNER_A:].astype(f32))
                vec_ref[6 * half : 6 * half + 6, :] = turned[:6]

        x = x_ref[...]
        low = mm(x, w_ref[0, :, :INNER_A])
        q_ref[...] = (low[:, :D] + vec_ref[B_Q : B_Q + 1, :]).astype(bf16)
        k_ref[:, :HALF] = low[:, D:].astype(bf16)
        high = mm(x, w_ref[1, :, :INNER_A])
        k_ref[:, HALF:] = high[:, :HALF].astype(bf16)
        v_ref[...] = (high[:, HALF:] + vec_ref[B_V : B_V + 1, :]).astype(bf16)

    return launch(
        "project", body, (tokens // TILE,), table,
        [rows_of(x)], [out_rows(tokens, D, bf16)] * 3 + [out_whole((16, D), f32)],
        weights=[w_a], after=after, mark=True,
    )


def attend(table, pack, q, k, v, into=(), after=()):
    tokens, width = q.shape
    pair_block = pl.BlockSpec((PACK, LANES), lambda h, *_: (pack, h))

    def body(table, q_ref, k_ref, v_ref, ctx_ref, e_ref, inv_ref):
        lane = lax.broadcasted_iota(jnp.int32, (PACK, LANES), 1)
        segment = segments(table, pack, 0, PACK)
        apart = jnp.where((lane < PAIRS_PACK) & (lane != segment), masked_fill, 0.0).astype(bf16)
        belongs = jnp.where(lane == segment, 1.0, 0.0).astype(bf16)
        keys = jnp.concatenate([k_ref[...], belongs], axis=1)
        values = jnp.concatenate([v_ref[...], jnp.ones((PACK, LANES), bf16)], axis=1)
        queries = q_ref[...].astype(f32) * HEAD_DIM ** (-0.5)
        first = lane < HEAD_DIM
        outs = []
        for head in range(2):
            mine = jnp.where(first if head == 0 else ~first, queries, 0.0).astype(bf16)
            logits = mm_nt(jnp.concatenate([mine, apart], axis=1), keys)
            peak = jnp.max(logits, axis=1, keepdims=True)
            expos = jnp.exp(logits - peak).astype(bf16)
            e_ref[head] = expos
            outs.append(mm(expos, values))
        total = jnp.where(first, outs[0][:, LANES:], outs[1][:, LANES:])
        inverse = 1.0 / total
        inv_ref[...] = inverse
        ctx_ref[...] = (jnp.where(first, outs[0][:, :LANES], outs[1][:, :LANES]) * inverse).astype(bf16)

    heads = width // HEAD_DIM
    return launch(
        "attend", body, (heads // 2,), table,
        [(a, pair_block) for a in (q, k, v)],
        [
            (jax.ShapeDtypeStruct((tokens, width), bf16), pair_block),
            in_hbm(
                (
                    jax.ShapeDtypeStruct((heads, tokens, PACK), bf16),
                    pl.BlockSpec((2, PACK, PACK), lambda h, *_: (h, pack, 0)),
                )
            ),
            (jax.ShapeDtypeStruct((tokens, width), f32), pair_block),
        ],
        into=into, after=after, mark=True,
    )


def gelu_parts(v):
    phi = 0.5 + 0.5 * lax.erf(v * 0.7071067811865476)
    return v * phi, phi + v * (jnp.exp(v * v * -0.5) * 0.3989422804014327)


def expand_rows(table, x, ctx, w_b, vec, after=()):
    tokens = x.shape[0]
    step = HALF

    def body(table, x_ref, ctx_ref, vec_ref, w_ref, n1_ref, r1_ref, fb_ref, act_ref, slope_ref):
        ctx = ctx_ref[...]
        attended = jnp.concatenate([mm(ctx, w_ref[half, :, FF // 2 :]) for half in range(2)], axis=1)
        hidden = x_ref[...].astype(f32) + attended + vec_ref[B_O : B_O + 1, :]
        normed, inverse = norm_parts(hidden)
        n1_ref[...] = normed
        r1_ref[...] = jnp.broadcast_to(inverse, (TILE, LANES))
        first_b = (normed * vec_ref[G_1 : G_1 + 1, :] + vec_ref[S_1 : S_1 + 1, :]).astype(bf16)
        fb_ref[...] = first_b
        for j in range(FF // step):
            half, at = divmod(j * step, FF // 2)
            row, column = divmod(j * step, D)
            bias = vec_ref[B_FF + row : B_FF + row + 1, column : column + step]
            active, slope = gelu_parts(mm(first_b, w_ref[half, :, at : at + step]) + bias)
            act_ref[:, j * step : (j + 1) * step] = active.astype(bf16)
            slope_ref[:, j * step : (j + 1) * step] = slope.astype(bf16)

    return launch(
        "expand_rows", body, (tokens // TILE,), table,
        [rows_of(x), rows_of(ctx), whole(vec)],
        [
            in_hbm(out_rows(tokens, D, f32)),
            in_hbm(out_rows(tokens, LANES, f32)),
            in_hbm(out_rows(tokens, D, bf16)),
            in_vmem(out_rows(tokens, FF, bf16)),
            in_hbm(out_rows(tokens, FF, bf16)),
        ],
        weights=[w_b], after=after, mark=True,
    )


def shrink_rows(table, active, w_2, n1, vec, score_vec, facts, after=()):
    tokens = active.shape[0]

    def body(table, act_ref, n1_ref, vec_ref, sv_ref, facts_ref, w_ref, n2_ref, r2_ref, stats_ref):
        step = pl.program_id(0)
        outer = mm(act_ref[...], w_ref[...])
        first_out = n1_ref[...] * vec_ref[G_1 : G_1 + 1, :] + vec_ref[S_1 : S_1 + 1, :]
        normed, inverse = norm_parts(first_out + outer + vec_ref[B_2 : B_2 + 1, :])
        n2_ref[...] = normed
        r2_ref[...] = jnp.broadcast_to(inverse, (TILE, LANES))
        score_vec = sv_ref[...]
        final = normed * vec_ref[G_2 : G_2 + 1, :] + vec_ref[S_2 : S_2 + 1, :]
        row_score = jnp.sum(final * score_vec, axis=1, keepdims=True)
        lane = lax.broadcasted_iota(jnp.int32, (TILE, LANES), 1)
        pack = step // (PACK // TILE)
        segment = segments(table, pack, step % (PACK // TILE) * TILE, TILE)
        here = lane == segment + pack * PAIRS_PACK
        shares = jnp.sum(jnp.where(here, row_score, 0.0), axis=0, keepdims=True)

        @pl.when(step == 0)
        def _():
            stats_ref[...] = facts_ref[...]

        stats_ref[0:1, :] += shares

        @pl.when(step == pl.num_programs(0) - 1)
        def _():
            stats_ref[0:1, :] = stats_ref[0:1, :] / facts_ref[3:4, :]

    return launch(
        "shrink_rows", body, (tokens // TILE,), table,
        [rows_of(active), from_hbm(rows_of(n1)), whole(vec), whole(score_vec), whole(facts)],
        [out_rows(tokens, D, f32), out_rows(tokens, LANES, f32), out_whole((8, LANES), f32)],
        weights=[w_2], after=after,
    )


def loss_parts(blocks):
    own = blocks[0]
    own_ids = own[1:2]
    grads = -own[2:3]
    for query in range(QUERIES_DEV):
        inside = [b[1:2] == float(query) for b in blocks]
        peak = functools.reduce(
            jnp.maximum,
            [jnp.where(i, b[0:1], masked_fill) for i, b in zip(inside, blocks)],
        )
        peak = jnp.max(peak, axis=1, keepdims=True)
        total = sum(jnp.where(i, jnp.exp(jnp.where(i, b[0:1] - peak, 0.0)), 0.0) for i, b in zip(inside, blocks))
        total = jnp.sum(total, axis=1, keepdims=True)
        labels = sum(jnp.where(i, b[2:3], 0.0) for i, b in zip(inside, blocks))
        labels = jnp.sum(labels, axis=1, keepdims=True)
        share = jnp.exp(jnp.where(inside[0], own[0:1] - peak, 0.0)) / total * labels
        grads = grads + jnp.where(own_ids == float(query), share, 0.0)
    return jnp.where(own_ids >= 0.0, grads, 0.0)


def shrink_back(table, blocks, n2, r2, vec, score_vec, active, after=()):
    tokens = n2.shape[0]
    count = len(blocks)

    def body(table, *refs):
        block_refs = refs[:count]
        n2_ref, r2_ref, vec_ref, sv_ref, act_ref = refs[count : count + 5]
        outer_ref, dh_ref, keep_ref, send_ref, sums_ref, grads_ref = refs[count + 5 :]
        step = pl.program_id(0)
        core = table[CORE]

        @pl.when(step == 0)
        def _():
            parts = [b[...] for b in block_refs]
            grads = loss_parts(parts)
            grads_ref[...] = jnp.broadcast_to(grads, (8, LANES))
            per_row = grads / parts[0][3:4]
            score_vec = sv_ref[...]
            weighted = score_vec * vec_ref[G_2 : G_2 + 1, :]
            middle = jnp.mean(weighted, axis=1, keepdims=True)
            lane = lax.broadcasted_iota(jnp.int32, (TILE, LANES), 1)
            bias = jnp.zeros((1, D), f32)
            gain = jnp.zeros((1, D), f32)
            shift = jnp.zeros((1, 1), f32)
            for i in range(tokens // TILE):
                here = pl.ds(i * TILE, TILE)
                pack, first_row = divmod(i * TILE, PACK)
                pair = segments(table, pack, first_row, TILE) + pack * PAIRS_PACK
                scale = jnp.sum(jnp.where(lane == pair, per_row, 0.0), axis=1, keepdims=True)
                normed = n2_ref[here, :]
                along = row_mean(normed * weighted)
                back = (scale * r2_ref[here, :1]) * (weighted - middle - normed * along)
                dh_ref[here, :] = back
                rounded = back.astype(bf16)
                outer_ref[here, :] = rounded
                bias = bias + jnp.sum(rounded.astype(f32), axis=0, keepdims=True)
                gain = gain + jnp.sum(normed * scale, axis=0, keepdims=True)
                shift = shift + jnp.sum(scale, axis=0, keepdims=True)
            sums_ref[...] = jnp.concatenate(
                [bias, gain * score_vec, shift * score_vec, jnp.zeros((5, D), f32)], axis=0
            )

        grad = mm_tn(act_ref[...], outer_ref[...])
        for pair in range(2):
            chip = 2 * step + pair
            at = pair * 2 * ROWS_B
            low = grad[at : at + ROWS_B].astype(bf16)
            high = grad[at + ROWS_B : at + 2 * ROWS_B].astype(bf16)
            keep_ref[table[TABLE + OWN + chip]] = jnp.where(core == 0, low, high)
            send_ref[table[TABLE + OTHER + chip]] = jnp.where(core == 0, high, low)

    return launch(
        "shrink_back", body, (CHIPS // 2,), table,
        [whole(b) for b in blocks]
        + [whole(a) for a in (n2, r2, vec, score_vec)]
        + [(active, pl.BlockSpec((tokens, 4 * ROWS_B), lambda i, *_: (0, i)))],
        [
            out_whole((tokens, D), bf16),
            in_hbm(out_whole((tokens, D), f32)),
            out_whole((CHIPS, ROWS_B, D), bf16),
            out_whole((CHIPS, ROWS_B, D), bf16),
            out_whole((8, D), f32),
            out_whole((8, LANES), f32),
        ],
        after=after,
    )


def rows_back(table, outer, dh2, slope, n1, r1, w_2, w_b, vec, after=()):
    tokens = outer.shape[0]

    def body(
        table, outer_ref, dh_ref, slope_ref, n1_ref, r1_ref, vec_ref, w2_ref, wb_ref,
        inner_ref, dh1_ref, attn_ref, dctx_ref, sums_ref, ff_ref,
    ):
        @pl.when(pl.program_id(0) == 0)
        def _():
            sums_ref[...] = jnp.zeros_like(sums_ref)
            ff_ref[...] = jnp.zeros_like(ff_ref)

        outer = outer_ref[...]
        first = dh_ref[...]
        step = D
        for j in range(FF // step):
            half, at = divmod(j * step, FF // 2)
            here = slice(j * step, (j + 1) * step)
            active = mm_nt(outer, w2_ref[here, :])
            inner = (active * slope_ref[:, here].astype(f32)).astype(bf16)
            inner_ref[:, here] = inner
            ff_ref[j : j + 1, :] += jnp.sum(inner.astype(f32), axis=0, keepdims=True)
            first = first + mm_nt(inner, wb_ref[half, :, at : at + step])
        normed = n1_ref[...]
        dn = first * vec_ref[G_1 : G_1 + 1, :]
        back = r1_ref[:, :1] * (dn - row_mean(dn) - normed * row_mean(dn * normed))
        dh1_ref[...] = back
        rounded = back.astype(bf16)
        attn_ref[...] = rounded
        sums_ref[0:1, :] += jnp.sum(rounded.astype(f32), axis=0, keepdims=True)
        sums_ref[1:2, :] += jnp.sum(first * normed, axis=0, keepdims=True)
        sums_ref[2:3, :] += jnp.sum(first, axis=0, keepdims=True)
        dctx = mm_nt(rounded[:, :HALF], wb_ref[0, :, FF // 2 :]) + mm_nt(
            rounded[:, HALF:], wb_ref[1, :, FF // 2 :]
        )
        dctx_ref[...] = dctx.astype(bf16)

    return launch(
        "rows_back", body, (tokens // TILE,), table,
        [rows_of(outer), from_hbm(rows_of(dh2)), from_hbm(rows_of(slope)), from_hbm(rows_of(n1)), from_hbm(rows_of(r1)), whole(vec)],
        [
            in_vmem(out_rows(tokens, FF, bf16)),
            in_hbm(out_rows(tokens, D, f32)),
            out_rows(tokens, D, bf16),
            out_rows(tokens, D, bf16),
            out_whole((8, D), f32),
            out_whole((8, D), f32),
        ],
        weights=[w_2, w_b], after=after, mark=True,
    )


def expand_grads(table, send, first_b, ctx, inner, attn, after=()):
    tokens = first_b.shape[0]
    tiles = WIDE_B // HALF

    def half_of(t):
        return 1 - t[CORE] if send else t[CORE]

    def body(table, fb_ref, ctx_ref, inner_ref, attn_ref, out_ref):
        step = pl.program_id(0)
        offset = OTHER if send else OWN

        def put(grad):
            for chip in range(CHIPS):
                out_ref[table[offset + chip]] = grad[chip * ROWS_A : (chip + 1) * ROWS_A].astype(bf16)

        @pl.when(step < tiles - 1)
        def _():
            put(mm_tn(fb_ref[...], inner_ref[...]))

        @pl.when(step == tiles - 1)
        def _():
            put(mm_tn(ctx_ref[...], attn_ref[...]))

    return launch(
        "expand_grads", body, (tiles,), table,
        [whole(first_b), whole(ctx)]
        + [
            (
                inner,
                pl.BlockSpec(
                    (tokens, HALF),
                    lambda i, t: (0, half_of(t) * (tiles - 1) + jnp.minimum(i, tiles - 2)),
                ),
            ),
            (attn, pl.BlockSpec((tokens, HALF), lambda i, t: (0, half_of(t)))),
        ],
        [
            (
                jax.ShapeDtypeStruct((CHIPS, ROWS_A, WIDE_B), bf16),
                pl.BlockSpec((CHIPS, ROWS_A, HALF), lambda i, t: (0, 0, i)),
            )
        ],
        after=after, mark=True,
    )


def attend_back(table, pack, q, k, v, expos, inverse, ctx, dctx, into=(), after=()):
    tokens, width = q.shape
    packs = tokens // PACK
    wide = 2 * LANES
    block = pl.BlockSpec((PACK, wide), lambda h, *_: (pack, h))

    def pair(q, k, v, e_ref, first_head, inverse, ctx, dctx):
        lane = lax.broadcasted_iota(jnp.int32, (PACK, LANES), 1)
        first = lane < HEAD_DIM
        scaled = (dctx.astype(f32) * inverse).astype(bf16)
        scaled_f = scaled.astype(f32)
        product = scaled_f * ctx.astype(f32)
        values = jnp.concatenate([v, jnp.where(lane < 3, 1.0, 0.0).astype(bf16)], axis=1)
        parts = []
        for head in range(2):
            mine = first if head == 0 else ~first
            delta = -jnp.sum(jnp.where(mine, product, 0.0), axis=1, keepdims=True)
            delta_1 = delta.astype(bf16).astype(f32)
            delta_2 = (delta - delta_1).astype(bf16).astype(f32)
            delta_3 = delta - delta_1 - delta_2
            minus = jnp.where(
                lane == 0, delta_1, jnp.where(lane == 1, delta_2, jnp.where(lane == 2, delta_3, 0.0))
            )
            left = jnp.concatenate(
                [jnp.where(mine, scaled_f, 0.0).astype(bf16), minus.astype(bf16)], axis=1
            )
            expos = e_ref[first_head + head]
            grad_logits = (expos.astype(f32) * mm_nt(left, values)).astype(bf16)
            parts.append((mm(grad_logits, k), mm_tn(grad_logits, q), mm_tn(expos, scaled)))
        scale = HEAD_DIM ** (-0.5)
        grad_q, grad_k, grad_v = (jnp.where(first, a, b) for a, b in zip(*parts))
        return (grad_q * scale).astype(bf16), (grad_k * scale).astype(bf16), grad_v.astype(bf16)

    def body(table, q_ref, k_ref, v_ref, e_ref, inv_ref, ctx_ref, dctx_ref, out_ref, sums_ref):
        for i in range(2):
            here = slice(i * LANES, (i + 1) * LANES)
            grad_q, grad_k, grad_v = pair(
                q_ref[:, here], k_ref[:, here], v_ref[:, here], e_ref, 2 * i,
                inv_ref[:, here], ctx_ref[:, here], dctx_ref[:, here],
            )
            out_ref[0, :, here] = grad_q
            out_ref[1, :, here] = grad_k
            out_ref[2, :, here] = grad_v
            sums_ref[:, here] = jnp.concatenate(
                [
                    jnp.sum(grad_q.astype(f32), axis=0, keepdims=True),
                    jnp.sum(grad_v.astype(f32), axis=0, keepdims=True),
                    jnp.zeros((6, LANES), f32),
                ],
                axis=0,
            )

    return launch(
        "attend_back", body, (width // wide,), table,
        [(a, block) for a in (q, k, v)]
        + [from_hbm((expos, pl.BlockSpec((4, PACK, PACK), lambda h, *_: (h, pack, 0))))]
        + [(a, block) for a in (inverse, ctx, dctx)],
        [
            (
                jax.ShapeDtypeStruct((3, tokens, width), bf16),
                pl.BlockSpec((3, PACK, wide), lambda h, *_: (0, pack, h)),
            ),
            (
                jax.ShapeDtypeStruct((8 * packs, width), f32),
                pl.BlockSpec((8, wide), lambda h, *_: (pack, h)),
            ),
        ],
        into=into, after=after, mark=True,
    )


def project_grads(table, send, x, grads, sums, after=()):
    tokens = x.shape[0]
    packs = tokens // PACK
    tiles = INNER_A // HALF
    offset = OTHER if send else OWN

    def half_of(t):
        return 1 - t[CORE] if send else t[CORE]

    def tile_of(i, t):
        tile = half_of(t) * tiles + i
        return (tile // 2, 0, tile % 2)

    def body(table, x_ref, d_ref, sa_ref, s2_ref, s1_ref, ff_ref, out_ref):
        step = pl.program_id(0)
        grad = mm_tn(x_ref[...], d_ref[0])
        here = pl.ds(pl.multiple_of(step * HALF, HALF), HALF)
        for chip in range(CHIPS):
            out_ref[table[offset + chip], :, here] = grad[chip * ROWS_A : (chip + 1) * ROWS_A].astype(bf16)

        @pl.when(step == 0)
        def _():
            attended = sum(sa_ref[8 * p : 8 * (p + 1), :] for p in range(packs))
            low = jnp.concatenate([attended[0:2], s1_ref[0:3, :], s2_ref[0:1, :]], axis=0)
            high = jnp.concatenate([s2_ref[1:3, :], ff_ref[0:4, :]], axis=0)
            rows = jnp.where(half_of(table) == 0, low, high)
            rows = jnp.concatenate([rows, jnp.zeros((LANES - 6, D), f32)], axis=0)
            turned = jnp.transpose(rows).astype(bf16)
            for chip in range(CHIPS):
                out_ref[table[offset + chip], :, INNER_A:] = turned[chip * ROWS_A : (chip + 1) * ROWS_A]

    return launch(
        "project_grads", body, (tiles,), table,
        [whole(x), (grads, pl.BlockSpec((1, tokens, HALF), tile_of))] + [whole(a) for a in sums],
        [out_whole((CHIPS, ROWS_A, WIDE_A), bf16)],
        after=after, mark=True,
    )


def token_grads(table, base, grads, w_a, after=()):
    tokens = base.shape[0]

    def body(table, base_ref, d_ref, w_ref, out_ref):
        grad_k = d_ref[1]
        low = jnp.concatenate([d_ref[0], grad_k[:, :HALF]], axis=1)
        high = jnp.concatenate([grad_k[:, HALF:], d_ref[2]], axis=1)
        out_ref[...] = base_ref[...] + mm_nt(low, w_ref[0, :, :INNER_A]) + mm_nt(high, w_ref[1, :, :INNER_A])

    return launch(
        "token_grads", body, (tokens // TILE,), table,
        [from_hbm(rows_of(base)), (grads, pl.BlockSpec((3, TILE, D), lambda i, *_: (0, i, 0)))],
        [in_hbm(out_rows(tokens, D, f32))],
        weights=[w_a], after=after, mark=True,
    )


def lamb(weight, grad, first, second, decay=weight_decay):
    first_new = beta_first * first + (1.0 - beta_first) * grad
    second_new = beta_second * second + (1.0 - beta_second) * grad * grad
    update = (first_new * (1.0 / (1.0 - beta_first**STEP))) / (
        jnp.sqrt(second_new * (1.0 / (1.0 - beta_second**STEP))) + step_eps
    )
    if decay:
        update = update + decay * weight
    return first_new, second_new, update


def square_rows(entries):
    lane = lax.broadcasted_iota(jnp.int32, (1, LANES), 1)
    rows = [jnp.zeros((1, LANES), f32), jnp.zeros((1, LANES), f32)]
    for group, arrays in entries:
        for i, a in enumerate(arrays):
            total = jnp.sum(jnp.sum(a * a, axis=1, keepdims=True), axis=0, keepdims=True)
            rows[i] = rows[i] + jnp.where(lane == group, total, 0.0)
    return jnp.concatenate(rows + [jnp.zeros((6, LANES), f32)], axis=0)


def like(array):
    return out_whole(array.shape, f32)


def step_wide(table, expand, shrink, parts_b, terms_2):
    rows = expand[0].shape[0]

    def body(table, ew, em, ev, sw, sm, sv, mine_ref, came_ref, *refs):
        term_refs = refs[: len(terms_2)]
        em_out, ev_out, eu_out, sm_out, sv_out, su_out, sums_ref = refs[len(terms_2) :]
        mine, came = mine_ref[...], came_ref[...].astype(f32)
        core = table[CORE]
        grad = jnp.concatenate(
            [
                jnp.where(core == 0, mine, came)[:, : FF // 2],
                jnp.where(core == 0, came, mine)[:, : FF // 2],
            ],
            axis=1,
        )
        em_out[...], ev_out[...], step_e = lamb(ew[...], grad, em[...], ev[...])
        eu_out[...] = step_e
        grad = sum(ref[...].astype(f32) for ref in term_refs)
        sm_out[...], sv_out[...], step_s = lamb(sw[...], grad, sm[...], sv[...])
        su_out[...] = step_s
        sums_ref[...] = square_rows([(4, (ew[...], step_e)), (5, (sw[...], step_s))])

    return launch(
        "step_wide", body, (1,), table,
        [whole(a) for a in (*expand, *shrink, *parts_b, *terms_2)],
        [like(expand[0])] * 3 + [like(shrink[0])] * 3 + [out_whole((8, LANES), f32)],

    )


def step_narrow(table, attention, vector, parts_a, parts_b, sums):
    rows = attention[0].shape[1]
    def body(table, aw, am, av, vw, vm, vv, mine_a, came_a, mine_b, came_b, sums_ref, *outs):
        am_out, av_out, au_out, vm_out, vv_out, vu_out, sums_out = outs
        core = table[CORE]

        def halves(mine_ref, came_ref):
            mine, came = mine_ref[...], came_ref[...].astype(f32)
            return jnp.where(core == 0, mine, came), jnp.where(core == 0, came, mine)

        low_a, high_a = halves(mine_a, came_a)
        low_b, high_b = halves(mine_b, came_b)
        grads = [
            low_a[:, :D],
            jnp.concatenate([low_a[:, D:INNER_A], high_a[:, :HALF]], axis=1),
            high_a[:, HALF:INNER_A],
            jnp.concatenate([low_b[:, FF // 2 :], high_b[:, FF // 2 :]], axis=1),
        ]
        entries = []
        for i, grad in enumerate(grads):
            am_out[i], av_out[i], step = lamb(aw[i], grad, am[i], av[i])
            au_out[i] = step
            entries.append((i, (aw[i], step)))
        rest = jnp.zeros((LANES - rows, LANES), f32)
        grad = jnp.concatenate(
            [
                jnp.transpose(jnp.concatenate([part[:, INNER_A:], rest], axis=0))[:6, :rows]
                for part in (low_a, high_a)
            ],
            axis=0,
        )
        vm_out[...], vv_out[...], step = lamb(vw[...], grad, vm[...], vv[...], 0.0)
        vu_out[...] = step
        entries.append((6, (vw[...], step)))
        sums_out[...] = sums_ref[...] + square_rows(entries)

    return launch(
        "step_narrow", body, (1,), table,
        [whole(a) for a in (*attention, *vector, *parts_a, *parts_b, sums)],
        [like(attention[0])] * 3 + [like(vector[0])] * 3 + [out_whole((8, LANES), f32)],

    )


def apply_step(table, sums, masters, steps):
    def body(table, sums_ref, aw, ew, sw, vw, au, eu, su, vu, a_out, e_out, s_out, v_out, ratio_ref, norms_ref):
        master, step = sums_ref[0:1, :], sums_ref[1:2, :]
        ratio = jnp.sqrt(master) * lax.rsqrt(step + 1e-12)
        ratio_ref[...] = ratio[:, :7]
        norms_ref[...] = jnp.sqrt(sums_ref[0:2, :])[:, :7]
        lane = lax.broadcasted_iota(jnp.int32, (1, LANES), 1)

        def of(group):
            return jnp.sum(jnp.where(lane == group, ratio, 0.0), axis=1, keepdims=True) * learn_rate

        for i in range(4):
            a_out[i] = aw[i] - of(i) * au[i]
        e_out[...] = ew[...] - of(4) * eu[...]
        s_out[...] = sw[...] - of(5) * su[...]
        v_out[...] = vw[...] - of(6) * vu[...]

    return launch(
        "apply_step", body, (1,), table,
        [whole(a) for a in (sums, *masters, *steps)],
        [like(a) for a in masters] + [out_whole((1, 7), f32), out_whole((2, 7), f32)],
    )


ACROSS_LAST = ((8, 4, 1, 2), (4, 8, 2, 1))
ALONG_LAST = ((1, 2, 8, 4), (2, 1, 4, 8))


def device_count():
    return lax.axis_size("dp") * lax.axis_size("cand")


def staged():
    return device_count() == 2 * CHIPS


def exchange(a, orders, stage):
    pairs = [(i, i ^ (2 * orders[i % 2][stage])) for i in range(device_count())]
    return lax.ppermute(a, BOTH, pairs)


def swap_core(a):
    return lax.ppermute(a, BOTH, [(i, i ^ 1) for i in range(device_count())])


def layout_table(index, orders):
    plain = jnp.arange(CHIPS, dtype=jnp.int32)
    if not staged():
        return jnp.concatenate([plain, plain, jnp.zeros((1,), jnp.int32), plain, plain])
    core = index % 2
    chip = index // 2

    def by_order(bits):
        position = jnp.zeros((CHIPS,), jnp.int32)
        holder = jnp.zeros((CHIPS,), jnp.int32)
        for stage, bit in enumerate(bits):
            position = position + jnp.where(((plain ^ chip) & bit) != 0, 1 << stage, 0)
            holder = holder + jnp.where((plain & (1 << stage)) != 0, bit, 0)
        return position, holder ^ chip

    parts = [by_order(bits) for bits in orders]
    own = [jnp.where(core == 0, a, b) for a, b in zip(*parts)]
    other = [jnp.where(core == 0, b, a) for a, b in zip(*parts)]
    return jnp.concatenate([own[0], other[0], core[None], own[1], other[1]]).astype(jnp.int32)


class Gathered:
    def __init__(self, table, block, rows, orders, base):
        self.table = table
        self.rows, self.orders, self.base = rows, orders, base
        self.start = block
        self.parts = [(block, 1)]
        self.sent, self.came = [], []
        self.stage = 0
        self.others = []

    def send(self, low, high, *after):
        if self.stage == 0:
            block = behind(self.parts[0][0], *after)
        else:
            block = pick(self.table, self.parts, self.rows, low, high, after)
        came = exchange(block, self.orders, self.stage)
        self.sent.append((block, high - low))
        self.came.append((came, high - low))
        if high == 1 << self.stage:
            self.parts = (self.parts if self.stage < 3 else self.sent) + self.came
            self.sent, self.came = [], []
            self.stage += 1
        return came

    def step(self, *after):
        return self.send(0, 1 << self.stage, *after)

    def swap(self, *after):
        part = self.parts[len(self.others)]
        block = pick(self.table, [part], self.rows, 0, part[1], after) if after else part[0]
        self.others.append(swap_core(block))
        return self.others[-1]

    def blocks(self):
        return Blocks(self.parts, self.others, self.rows, self.base)


class Whole:
    def __init__(self, pieces, rows, base):
        halves = [(a, CHIPS // 2) for a in pieces[:2]]
        self.own = Blocks(halves, pieces[2:], rows, base)
        self.start = pieces[0]

    def send(self, low, high, *after):
        return self.own.pieces[0]

    step = swap = lambda self, *after: self.own.pieces[0]

    def blocks(self):
        return self.own


class Scattered:
    def __init__(self, table, keep, send, orders, after):
        self.table = table
        self.terms = [[(keep, 0)], [(swap_core(behind(send, *after)), 0)]]
        self.orders = orders
        self.stage = 3
        self.came = []
        self.left = 1 << 3

    def send(self, low, high, *after):
        first = 1 << self.stage
        total = self.going = add_blocks(self.table, self.terms, first + low, first + high, after)
        came = exchange(total, self.orders, self.stage)
        self.came.append((came, low))
        self.left -= high - low
        if self.left == 0:
            self.next_stage()
        return came

    def next_stage(self):
        self.terms.append(self.came)
        self.came = []
        self.stage -= 1
        self.left = 1 << max(self.stage, 0)

    def step(self, *after):
        return self.send(0, 1 << self.stage, *after)

    def rest(self):
        return [next(a for a, at in term if at == 0)[0] for term in self.terms]

    def total(self, *after):
        return sum(term.astype(f32) for term in behind(self.rest(), *after))


def by_core(core, low, high):
    return jnp.where(core == 0, low, high)


def own_rows(core, total):
    rows = total.shape[0] // 2
    low, high = total[:rows], total[rows:]
    return by_core(core, low, high), swap_core(by_core(core, high, low).astype(bf16))


def all_sum(row):
    if not staged():
        return lax.psum(row, BOTH)
    for bits in ((1,), (2, 4, 6), (8, 16, 24)):
        came = [
            lax.ppermute(row, BOTH, [(i, i ^ bit) for i in range(device_count())]) for bit in bits
        ]
        row = sum(came, row)
    return row


def gather_weights(places, table, core, attention, expand, shrink, vector):
    mine, theirs = own_halves(places, attention, expand, vector)
    shrink = shrink.astype(bf16)
    cuts = (0, WIDE_A, WIDE_A + WIDE_B)
    outs = []
    if not staged():
        groups = [(jnp.stack([mine, theirs], axis=1)[:, :, a:b], ROWS_A, 0) for a, b in zip(cuts, cuts[1:])]
        for part, rows, base in groups + [(shrink[:, None], ROWS_B, TABLE)]:
            full = lax.all_gather(part, BOTH, axis=0, tiled=True)
            if rows == ROWS_B:
                full = full.reshape(CHIPS, 2, rows, D).swapaxes(1, 2)
            full = full.reshape(2, CHIPS // 2 * rows, 2, full.shape[-1])
            pieces = [full[high, :, half] for half in (0, 1) for high in (0, 1)]
            outs.append(Whole(pieces, rows, base))
        return outs
    came = swap_core(theirs)
    chip_rows = jnp.concatenate([by_core(core, mine, came), by_core(core, came, mine)], axis=0)
    outs = [Gathered(table, chip_rows[:, a:b], ROWS_A, ACROSS_LAST, 0) for a, b in zip(cuts, cuts[1:])]
    return outs + [Gathered(table, shrink, ROWS_B, ALONG_LAST, TABLE)]


class Reduced:
    def __init__(self, table, core, keep, send, orders, after=()):
        self.core = core
        self.keep, self.other = keep, send
        self.came = keep
        if staged():
            self.work = Scattered(table, keep, send, orders, after)
            self.came = self.work.terms[1][0][0]

    def send(self, low, high, *after):
        if not staged():
            return self.keep, self.keep
        came = self.work.send(low, high, *after)
        return self.work.going, came

    def step(self, *after):
        return self.send(0, 1 << self.work.stage if staged() else 0, *after)

    def halves(self, *after):
        if staged():
            return own_rows(self.core, self.work.total(*after))
        both = jnp.stack([self.keep, self.other], axis=2).reshape(D, 2, self.keep.shape[2]).astype(f32)
        total = lax.psum_scatter(both, BOTH, scatter_dimension=0, tiled=True)
        return total[:, 0], total[:, 1]

    def shard(self):
        if staged():
            return self.work.rest()
        both = jnp.stack([self.keep, self.other], axis=1).reshape(FF, D).astype(f32)
        return [lax.psum_scatter(both, BOTH, scatter_dimension=0, tiled=True)]


def per_device(
    tokens,
    score_vec,
    pair_lengths,
    query_ids,
    labels,
    attention_weight,
    expand_weight,
    shrink_weight,
    vector_weight,
    attention_first,
    expand_first,
    shrink_first,
    vector_first,
    attention_second,
    expand_second,
    shrink_second,
    vector_second,
):
    index = lax.axis_index(BOTH)
    core = index % 2
    ends = jnp.cumsum(pair_lengths, axis=-1, dtype=jnp.int32)
    places = jnp.concatenate([layout_table(index, ACROSS_LAST), layout_table(index, ALONG_LAST)])
    table = jnp.concatenate([places, ends.reshape(-1)])
    get_a, get_b, get_2 = gather_weights(
        places,
        table,
        core,
        attention_weight,
        expand_weight,
        shrink_weight,
        vector_weight,
    )

    pack_count = pair_lengths.shape[0]
    pairs = pack_count * PAIRS_PACK
    def in_lanes(values, filler):
        row = values.astype(f32).reshape(1, pairs)
        return jnp.pad(row, ((0, 0), (0, LANES - pairs)), constant_values=filler)

    facts = jnp.concatenate(
        [
            jnp.zeros((1, LANES), f32),
            in_lanes(query_ids, -1.0),
            in_lanes(labels, 0.0),
            in_lanes(pair_lengths, 1.0),
            jnp.zeros((4, LANES), f32),
        ],
        axis=0,
    )
    score_row = score_vec.reshape(1, D)

    came_a = get_a.step()
    came_2 = get_2.step(get_a.start)
    came_2 = get_2.step(came_a)
    came_a = get_a.step()
    came_b = get_b.step(came_a)
    came_a_2 = get_a.step(facts)
    came_a = get_a.step(came_b, came_2)
    came_b = get_b.step(came_a_2)
    get_a.swap()
    get_a.swap()
    w_a = get_a.blocks()
    q, k, v, vec, end_q = project(table, tokens, w_a, after=[came_b])
    came_b = get_b.step(came_a)
    *parts, end = attend(table, 0, q, k, v)
    came = [get_2.step(end_q, came_b), get_b.send(0, 4, end_q, came_b)]
    for pack in range(1, pack_count):
        *parts, end_all = attend(table, pack, q, k, v, parts, after=[end])
    ctx, expos, inverse = parts
    came = [get_b.send(4, 8, end, *came), get_2.send(0, 2, end, *came)]
    came += [get_b.swap(), get_b.swap(), get_b.swap()]
    get_b.swap()
    w_b = get_b.blocks()
    n1, r1, first_b, active, slope, end = expand_rows(table, tokens, ctx, w_b, vec)
    get_2.send(2, 8, end_all, *came)
    get_2.swap()
    get_2.swap()
    get_2.swap()
    get_2.swap(end)
    w_2 = get_2.blocks()
    n2, r2, stats = shrink_rows(table, active, w_2, n1, vec, score_row, facts)

    n_cand = lax.axis_size("cand")
    blocks = [stats] + [
        lax.ppermute(stats, "cand", [(i, (i + shift) % n_cand) for i in range(n_cand)])
        for shift in range(1, n_cand)
    ]
    outer, dh2, keep_2, send_2, sums_2, grad_block = shrink_back(
        table, blocks, n2, r2, vec, score_row, active
    )
    put_2 = Reduced(table, core, keep_2, send_2, ALONG_LAST)
    inner, dh1, attn, dctx, sums_1, sums_ff, end = rows_back(table, outer, dh2, slope, n1, r1, w_2, w_b, vec)
    goes, came = put_2.send(6, 8, end)
    send_b, end = expand_grads(table, True, first_b, ctx, inner, attn, after=[goes])
    goes, came_next = put_2.send(4, 6, end, came)
    keep_b, end = expand_grads(table, False, first_b, ctx, inner, attn, after=[end, goes])
    put_b = Reduced(table, core, keep_b, send_b, ACROSS_LAST, after=[came])
    goes, came = zip(put_2.send(0, 4, end, came_next, put_b.came), put_b.send(2, 8, came_next))
    *parts, end = attend_back(table, 0, q, k, v, expos, inverse, ctx, dctx, after=[end, *goes])
    goes, came = zip(
        put_2.step(end, *came),
        put_b.send(0, 2, end, *came),
        put_b.step(end, *came),
    )
    for pack in range(1, pack_count):
        *parts, end = attend_back(
            table, pack, q, k, v, expos, inverse, ctx, dctx, parts, after=[end, *goes]
        )
    grads, sums_attn = parts
    sums = [sums_attn, sums_2, sums_1, sums_ff]
    send_a, end = project_grads(table, True, tokens, grads, sums, after=came)
    keep_a, end = project_grads(table, False, tokens, grads, sums, after=[end])
    put_a = Reduced(table, core, keep_a, send_a, ACROSS_LAST)
    goes, came = zip(put_a.step(), put_b.step(end))
    grad_tokens, end = token_grads(table, dh1, grads, w_a, after=[end, put_a.came, *goes])
    goes, came_a = put_a.step(end)
    put_b.step(end, goes)
    goes, came_a = put_a.step()
    put_2.step(end, goes)
    parts_b = put_b.halves(goes)
    goes, came_a = put_a.step()
    put_2.step(goes)
    expand_moment, expand_square, expand_step, shrink_moment, shrink_square, shrink_step, sums = step_wide(
        table,
        (expand_weight, expand_first, expand_second),
        (shrink_weight, shrink_first, shrink_second),
        parts_b,
        put_2.shard(),
    )
    parts_a = put_a.halves()
    (
        attention_moment,
        attention_square,
        attention_step,
        vector_moment,
        vector_square,
        vector_step,
        sums,
    ) = step_narrow(
        table,
        (attention_weight, attention_first, attention_second),
        (vector_weight, vector_first, vector_second),
        parts_a,
        parts_b,
        sums,
    )
    attention_new, expand_new, shrink_new, vector_new, ratios, norms = apply_step(
        table,
        all_sum(sums),
        (attention_weight, expand_weight, shrink_weight, vector_weight),
        (attention_step, expand_step, shrink_step, vector_step),
    )
    return (
        grad_tokens,
        stats[0, :pairs],
        grad_block[0, :pairs],
        ratios.reshape(7),
        norms,
        attention_new,
        expand_new,
        shrink_new,
        vector_new,
        attention_moment,
        expand_moment,
        shrink_moment,
        vector_moment,
        attention_square,
        expand_square,
        shrink_square,
        vector_square,
    )


def solution(mesh):
    placed = (
        P(("dp", "cand"), None),
        P(),
        P(("dp", "cand"), None),
        P(("dp", "cand")),
        P(("dp", "cand")),
        P(None, ("dp", "cand"), None),
        P(("dp", "cand"), None),
        P(("dp", "cand"), None),
        P(None, ("dp", "cand")),
        P(None, ("dp", "cand"), None),
        P(("dp", "cand"), None),
        P(("dp", "cand"), None),
        P(None, ("dp", "cand")),
        P(None, ("dp", "cand"), None),
        P(("dp", "cand"), None),
        P(("dp", "cand"), None),
        P(None, ("dp", "cand")),
    )
    return jax.shard_map(
        per_device,
        mesh=mesh,
        in_specs=placed,
        out_specs=(
            P(("dp", "cand"), None),
            P(("dp", "cand")),
            P(("dp", "cand")),
            P(),
            P(),
            P(None, ("dp", "cand"), None),
            P(("dp", "cand"), None),
            P(("dp", "cand"), None),
            P(None, ("dp", "cand")),
            P(None, ("dp", "cand"), None),
            P(("dp", "cand"), None),
            P(("dp", "cand"), None),
            P(None, ("dp", "cand")),
            P(None, ("dp", "cand"), None),
            P(("dp", "cand"), None),
            P(("dp", "cand"), None),
            P(None, ("dp", "cand")),
        ),
        check_vma=False,
    )
```
